128 devices in a mesh: heads: 4 (over x_hi, core), seq: 32 (over z, y, x_lo).
Axes of the slice: x: 4 (x_hi: 2, x_lo: 2; x = x_hi * 2 + x_lo), y: 4, z: 4, core: 2. Of those that a mesh axis runs over, the one named last changes fastest.
Arguments:
- decoder_states: bfloat16 [8192, 4096], P('seq', 'heads'), may hold values from -6 to 6
- query_weight: bfloat16 [4096, 4096], P(None, 'heads'), may hold values from -1 to 1
- output_weight: bfloat16 [4096, 4096], P('heads'), may hold values from -0.09375 to 0.09375
- context_keys: bfloat16 [1024, 4096], P(('heads', 'seq')), may hold values from -512 to 512
- context_values: bfloat16 [1024, 4096], P(('heads', 'seq')), may hold values from -6 to 6
- lengths: int32 [4], replicated, may hold values from 1 to 256, 704 in all
- slot_passage: int32 [4], replicated, may hold values from 0 to 3, each once
- output_cotangent: bfloat16 [8192, 4096], P('seq', 'heads'), may hold values from -6 to 6
Outputs:
- attended: bfloat16 [8192, 4096], P('seq', 'heads')
- query_weight_grad: float32 [4096, 4096], P('seq', 'heads')
- output_weight_grad: float32 [4096, 4096], P('heads', 'seq')
- context_keys_grad: float32 [1024, 4096], P(('heads', 'seq'))
- context_values_grad: float32 [1024, 4096], P(('heads', 'seq'))
The draws below stay inside these ranges and needn't reach their ends.
Inputs may be any that keep to these rules, and one draw needn't show every extreme that they name: `lengths`: the valid tokens of all passages add up to 704. `slot_passage`: each passage stands in exactly one slot.
All inputs are finite; a program needn't handle non-finite values.
Results may differ from the reference program's by a relative error of at most 0.035.
Values may be sent and summed in bfloat16 or wider, within the bound.
No kernel may reach another device: no remote copies, remote signals or barrier semaphores. Data moves between devices by JAX's collectives and lax.ppermute only.
A program may use at most 128 MiB of HBM per device.

```python
import math
import jax
import jax.numpy as jnp
import numpy as np
from jax import lax

D = 4096
HEAD = 128
HEADS = 32
TOK_DEV = 256
TOKENS = 8192
CONTEXT = 1024
PAS_LEN = 256
PASSAGES = 4
N_SEQ = 32


def shared_decoder(key):
    states = jnp.clip(jax.random.normal(jax.random.fold_in(key, 101), (TOKENS, D), jnp.float32), -6.0, 6.0)
    bound_value = 6.0 / math.sqrt(D)
    weights = jax.random.normal(jax.random.fold_in(key, 102), (D, D), jnp.float32) / math.sqrt(D)
    weights = jnp.clip(weights, -bound_value, bound_value)
    return (states, weights)


def draw_decoder_states(key, part):
    states, weights = shared_decoder(key)
    return states.astype(jnp.bfloat16)


def draw_query_weight(key, part):
    states, weights = shared_decoder(key)
    return weights.astype(jnp.bfloat16)


def draw_context_keys(key, part):
    key = jax.random.fold_in(key, 7)
    context = 2.0 * jnp.clip(jax.random.normal(key, (CONTEXT, D), jnp.float32), -6.0, 6.0)
    return context.astype(jnp.bfloat16)


def raised(values, own_key, source, target, parts, factor):
    owner, partner = [(jnp.arange(values.shape[axis_at]) // (values.shape[axis_at] // parts)).reshape([-1 if axis == axis_at else 1 for axis in range(values.ndim)]) for axis_at in (source, target)]
    chosen = jax.random.permutation(own_key, parts)[partner]
    strong = (owner == chosen) | (owner == (partner + parts // 2) % parts)
    return jnp.where(strong, factor * values, values)


def shard_levels(stream_key, shape, shards, low, largest):
    def one(dim, parts):
        draws = jax.random.uniform(jax.random.fold_in(jax.random.fold_in(stream_key, 6), dim), (parts,), jnp.float32, low / len(shards), largest / len(shards))
        return jnp.repeat(jnp.exp(draws), shape[dim] // parts).reshape((-1,) + (1,) * (len(shape) - dim - 1))

    loudness = one(*shards[0])
    for cut in shards[1:]:
        loudness = loudness * one(*cut)
    return loudness


def split_up(amount, total, limit, slope):
    portions = [(1 << 20) // math.isqrt(standing ** slope) + 1 for standing in range(2, amount + 1)]
    spare, given = total - limit - (amount - 1), [1] * (amount - 1)
    while spare > 0:
        free = [i for i in range(amount - 1) if given[i] < limit]
        whole, left = sum([portions[i] for i in free]), spare
        for i in free:
            extra = min(limit - given[i], max(1, left * portions[i] // whole), spare)
            given[i] = given[i] + extra
            spare = spare - extra
    return np.array([limit] + given)


def ragged_sizes(rng, number_of, total, reach, lean):
    if number_of == 2:
        one = jax.random.randint(rng, (), max(1, total - reach), min(reach, total - 1) + 1)
        return jnp.stack([one, total - one])
    sizes = jnp.asarray(split_up(number_of, total, reach, lean), jnp.int32)
    couples = (number_of - 1) // 2
    donor, taker = sizes[1:1 + 2 * couples:2], sizes[2:2 + 2 * couples:2]
    slack = jnp.minimum(donor - 1, reach - taker)
    moved = jax.random.randint(jax.random.fold_in(rng, 1), (couples,), 0, 1 << 20) % (slack + 1)
    sizes = sizes.at[1:1 + 2 * couples:2].set(donor - moved).at[2:2 + 2 * couples:2].set(taker + moved)
    return sizes[jax.random.permutation(jax.random.fold_in(rng, 2), number_of)]


def scatter_about(rng, extent, scale, most, shards=(), held_as=jnp.bfloat16):
    array = scale * jax.random.normal(rng, extent, jnp.float32)
    if shards:
        array = array * shard_levels(rng, extent, shards, -0.22, 0.18)
    return jnp.clip(array, -most, most).astype(held_as)


def bell_draw_with(stream_key, dims, deviation, bound, cuts, heavy, kind=jnp.bfloat16):
    values = deviation * jax.random.normal(stream_key, dims, jnp.float32)
    if cuts:
        values = values * shard_levels(stream_key, dims, cuts, -0.22, 0.18)
    return jnp.clip(raised(values, jax.random.fold_in(stream_key, 3), *heavy), -bound, bound).astype(kind)


def setup_inputs(seed: int = 0) -> dict:
    key_list = jax.random.split(jax.random.key(seed), 9)
    decoder_states = draw_decoder_states(jax.random.fold_in(key_list[8], 71), 0)
    query_weight = draw_query_weight(jax.random.fold_in(key_list[8], 71), 0)
    output_weight = scatter_about(key_list[2], (D, D), D ** -0.5, 0.09375, ((0, 4),))
    context_keys = draw_context_keys(jax.random.fold_in(key_list[8], 71), 0)
    context_values = scatter_about(key_list[4], (CONTEXT, D), 1.0, 6.0, ((0, 128),))
    lengths = ragged_sizes(key_list[5], PASSAGES, PASSAGES * PAS_LEN * 11 // 16, PAS_LEN, 1).astype(jnp.int32)
    slot_passage = jax.random.permutation(key_list[6], PASSAGES).astype(jnp.int32)
    output_cotangent = bell_draw_with(key_list[7], (TOKENS, D), 1.0, 6.0, ((0, 32), (1, 4)), (0, 1, 32, 2.75))
    return dict(decoder_states=decoder_states, query_weight=query_weight, output_weight=output_weight, context_keys=context_keys, context_values=context_values, lengths=lengths, slot_passage=slot_passage, output_cotangent=output_cotangent)


def key_validity(lengths, slot_passage):
    slot_lengths = lengths[slot_passage]
    position = jnp.arange(CONTEXT, dtype=jnp.int32)
    return position % PAS_LEN < slot_lengths[position // PAS_LEN]

def rounded(value):
    return lax.optimization_barrier(value.astype(jnp.bfloat16)).astype(jnp.float32)

def group_products(left, right):
    left_groups = left.reshape(N_SEQ, TOK_DEV, left.shape[1])
    right_groups = right.reshape(N_SEQ, TOK_DEV, right.shape[1])

    def accumulate(running, operands):
        product = jnp.dot(operands[0].T, operands[1], preferred_element_type=jnp.float32)
        return (running + rounded(product), None)
    start_total = jnp.zeros((left.shape[1], right.shape[1]), jnp.float32)
    summed, unused = lax.scan(accumulate, start_total, (left_groups, right_groups))
    return summed

def split_heads(matrix, row_count):
    return matrix.reshape(row_count, HEADS, HEAD).transpose(1, 0, 2)

def join_heads(stacked, row_count):
    return stacked.transpose(1, 0, 2).reshape(row_count, D)

def reference(decoder_states, query_weight, output_weight, context_keys, context_values, lengths, slot_passage, output_cotangent):
    score_scale = 1.0 / math.sqrt(HEAD)
    key_valid = key_validity(lengths, slot_passage)
    queries = jnp.dot(decoder_states, query_weight, preferred_element_type=jnp.float32).astype(jnp.bfloat16)
    heads_grad = lax.dot_general(output_cotangent, output_weight, (((1,), (1,)), ((), ())), preferred_element_type=jnp.float32).astype(jnp.bfloat16)

    def one_head(operands):
        query_head, key_head, value_head, grad_head = operands
        scores = jnp.dot(query_head, key_head.T, preferred_element_type=jnp.float32) * score_scale
        masked = jnp.where(key_valid[None, :], scores, -jnp.inf)
        row_max = lax.optimization_barrier(jnp.max(masked, axis=1, keepdims=True))
        weights = jnp.exp(masked - row_max)
        probabilities = weights / lax.optimization_barrier(jnp.sum(weights, axis=1, keepdims=True))
        probs_low = probabilities.astype(jnp.bfloat16)
        heads_out = jnp.dot(probs_low, value_head, preferred_element_type=jnp.float32).astype(jnp.bfloat16)
        value_dots = jnp.dot(grad_head, value_head.T, preferred_element_type=jnp.float32)
        row_delta = lax.optimization_barrier(jnp.sum(grad_head.astype(jnp.float32) * heads_out.astype(jnp.float32), axis=1, keepdims=True))
        score_grad = (probabilities * (value_dots - row_delta) * score_scale).astype(jnp.bfloat16)
        query_grad = jnp.dot(score_grad, key_head, preferred_element_type=jnp.float32).astype(jnp.bfloat16)
        score_groups = score_grad.astype(jnp.float32).reshape(N_SEQ, TOK_DEV, CONTEXT)
        query_groups = query_head.astype(jnp.float32).reshape(N_SEQ, TOK_DEV, HEAD)
        key_terms = jnp.einsum('gtk,gtd->gkd', score_groups, query_groups)
        key_grad = lax.optimization_barrier(jnp.sum(rounded(key_terms), axis=0))
        prob_groups = probs_low.astype(jnp.float32).reshape(N_SEQ, TOK_DEV, CONTEXT)
        grad_groups = grad_head.astype(jnp.float32).reshape(N_SEQ, TOK_DEV, HEAD)
        value_terms = jnp.einsum('gtk,gtd->gkd', prob_groups, grad_groups)
        value_grad = lax.optimization_barrier(jnp.sum(rounded(value_terms), axis=0))
        return (heads_out, query_grad, key_grad, value_grad)
    stacked = lax.map(one_head, (split_heads(queries, TOKENS), split_heads(context_keys, CONTEXT), split_heads(context_values, CONTEXT), split_heads(heads_grad, TOKENS)))
    heads_out = join_heads(stacked[0], TOKENS)
    query_grad = join_heads(stacked[1], TOKENS)
    attended = jnp.dot(heads_out, output_weight, preferred_element_type=jnp.float32).astype(jnp.bfloat16)
    output_weight_grad = group_products(heads_out, output_cotangent)
    query_weight_grad = group_products(decoder_states, query_grad)
    context_keys_grad = join_heads(stacked[2], CONTEXT)
    context_values_grad = join_heads(stacked[3], CONTEXT)
    return (attended, query_weight_grad, output_weight_grad, context_keys_grad, context_values_grad)
```

```python
import math

import jax
import jax.numpy as jnp
from jax import lax
from jax.experimental import pallas as pl
from jax.experimental.pallas import tpu as pltpu
from jax.sharding import Mesh
from jax.sharding import PartitionSpec as P

HEAD = 128
SCALE = 1.0 / math.sqrt(HEAD)
F32 = jnp.float32
BF16 = jnp.bfloat16
AXES = (("xh", 2), ("core", 2), ("z", 4), ("y", 4), ("xl", 2))
HEADS = ("xh", "core")
SEQ = ("z", "y", "xl")
SWAP = [(0, 1), (1, 0)]
VMEM = 56 * 1024 * 1024


def context_bias(lengths, slot_passage, slot_tokens):
    slot_lengths = jnp.sum(
        jnp.where(slot_passage[:, None] == jnp.arange(4)[None, :], lengths[None, :], 0), axis=1
    )
    token = jnp.arange(4 * slot_tokens, dtype=jnp.int32)
    plane, slot, layer, row = token // 128, (token // 32) % 4, (token // 8) % 4, token % 8
    position = (layer * 8 + plane) * 8 + row
    limit = jnp.sum(jnp.where(slot[:, None] == jnp.arange(4)[None, :], slot_lengths[None, :], 0), axis=1)
    return jnp.where(position < limit, 0.0, -jnp.inf).astype(F32)[None, :]


def dot(a, b, contract):
    return lax.dot_general(a, b, (contract, ((), ())), preferred_element_type=F32)


def attention_kernel(bias, q_ref, g_ref, k_ref, v_ref, ho_ref, dq_ref, dk_ref, dv_ref, dk_sum, dv_sum):
    step = pl.program_id(1)

    @pl.when(step == 0)
    def _():
        dk_sum[...] = jnp.zeros_like(dk_sum)
        dv_sum[...] = jnp.zeros_like(dv_sum)

    q, g, k, v = q_ref[...], g_ref[...], k_ref[...], v_ref[...]
    scores = dot(q, k, ((1,), (1,))) + bias[...]
    top = jnp.max(scores, axis=1, keepdims=True)
    weights = jnp.exp((scores - top) * SCALE)
    probs = weights * (1.0 / jnp.sum(weights, axis=1, keepdims=True))
    probs_low = probs.astype(BF16)
    heads_out = dot(probs_low, v, ((1,), (0,))).astype(BF16)
    ho_ref[...] = heads_out
    value_dots = dot(g, v, ((1,), (1,)))
    delta = jnp.sum(g.astype(F32) * heads_out.astype(F32), axis=1, keepdims=True)
    score_grad = (probs * (value_dots - delta) * SCALE).astype(BF16)
    dq_ref[...] = dot(score_grad, k, ((1,), (0,))).astype(BF16)
    dk_sum[...] += dot(q, score_grad, ((0,), (0,)))
    dv_sum[...] += dot(g, probs_low, ((0,), (0,)))

    @pl.when(step == pl.num_programs(1) - 1)
    def _():
        dk_ref[...] = dk_sum[...].T.astype(BF16)
        dv_ref[...] = dv_sum[...].T.astype(BF16)


def attention(bias, q, g, k, v, rows=256):
    tokens, cols = q.shape
    context = k.shape[0]
    token_block = pl.BlockSpec((rows, HEAD), lambda h, t: (t, h))
    context_block = pl.BlockSpec((context, HEAD), lambda h, t: (0, h))
    return pl.pallas_call(
        attention_kernel,
        grid=(cols // HEAD, tokens // rows),
        in_specs=[
            pl.BlockSpec((1, context), lambda h, t: (0, 0)),
            token_block,
            token_block,
            context_block,
            context_block,
        ],
        out_specs=[token_block, token_block, context_block, context_block],
        out_shape=[
            jax.ShapeDtypeStruct((tokens, cols), BF16),
            jax.ShapeDtypeStruct((tokens, cols), BF16),
            jax.ShapeDtypeStruct((context, cols), BF16),
            jax.ShapeDtypeStruct((context, cols), BF16),
        ],
        scratch_shapes=[pltpu.VMEM((HEAD, context), F32), pltpu.VMEM((HEAD, context), F32)],
        compiler_params=pltpu.CompilerParams(vmem_limit_bytes=VMEM),
        cost_estimate=pl.CostEstimate(
            flops=12 * tokens * cols * context,
            bytes_accessed=2 * (4 * tokens * cols + 4 * context * cols),
            transcendentals=tokens * context * cols // HEAD,
        ),
        name="attention",
    )(bias, q, g, k, v)


def output_grad_kernel(ho_ref, g_ref, out_ref):
    product = dot(ho_ref[0], g_ref[...], ((0,), (0,))).astype(BF16)
    for part in range(out_ref.shape[0]):
        out_ref[part] = product[:, part * 128 : (part + 1) * 128]


def output_weight_terms(heads_out, cotangent):
    layers, tokens, cols = heads_out.shape
    wide = cotangent.shape[1]
    return pl.pallas_call(
        output_grad_kernel,
        grid=(layers,),
        in_specs=[
            pl.BlockSpec((1, tokens, cols), lambda i: (i, 0, 0)),
            pl.BlockSpec((tokens, wide), lambda i: (0, 0)),
        ],
        out_specs=pl.BlockSpec((wide // 128, cols, 128), lambda i: (0, i, 0)),
        out_shape=jax.ShapeDtypeStruct((wide // 128, layers * cols, 128), BF16),
        compiler_params=pltpu.CompilerParams(vmem_limit_bytes=VMEM),
        cost_estimate=pl.CostEstimate(
            flops=2 * tokens * layers * cols * wide,
            bytes_accessed=2 * (tokens * layers * cols + tokens * wide + layers * cols * wide),
            transcendentals=0,
        ),
        name="output_weight_terms",
    )(heads_out, cotangent)


def query_grad_kernel(x_ref, dq_ref, out_ref):
    left = x_ref[...].T
    cols = dq_ref.shape[2]
    for layer in range(dq_ref.shape[0]):
        out_ref[:, layer * cols : (layer + 1) * cols] = dot(left, dq_ref[layer], ((1,), (0,))).astype(BF16)


def query_weight_terms(states, query_grad):
    layers, tokens, cols = query_grad.shape
    wide = states.shape[1]
    rows = 256
    return pl.pallas_call(
        query_grad_kernel,
        grid=(wide // rows,),
        in_specs=[
            pl.BlockSpec((tokens, rows), lambda i: (0, i)),
            pl.BlockSpec((layers, tokens, cols), lambda i: (0, 0, 0)),
        ],
        out_specs=pl.BlockSpec((rows, layers * cols), lambda i: (i, 0)),
        out_shape=jax.ShapeDtypeStruct((wide, layers * cols), BF16),
        compiler_params=pltpu.CompilerParams(vmem_limit_bytes=VMEM),
        cost_estimate=pl.CostEstimate(
            flops=2 * tokens * layers * cols * wide,
            bytes_accessed=2 * (tokens * layers * cols + tokens * wide + layers * cols * wide),
            transcendentals=0,
        ),
        name="query_weight_terms",
    )(states, query_grad)


def ordered(mine, other, index, axis):
    return jnp.where(
        index == 0, jnp.concatenate([mine, other], axis), jnp.concatenate([other, mine], axis)
    )


def on_device(
    decoder_states,
    query_weight,
    output_weight,
    context_keys,
    context_values,
    lengths,
    slot_passage,
    output_cotangent,
):
    xh, core, z = lax.axis_index("xh"), lax.axis_index("core"), lax.axis_index("z")
    tokens, cols = decoder_states.shape
    layers = lax.axis_size("z")
    piece = cols // layers

    def all_features(local):
        over_x = ordered(local[:, None], lax.ppermute(local, "xh", SWAP)[:, None], xh, 1)
        other = lax.ppermute(over_x, "core", SWAP)
        full = ordered(over_x[:, :, None], other[:, :, None], core, 2)
        return full.reshape(tokens, 4 * cols)

    own = jnp.stack([context_keys, context_values]).reshape(2, 8, 16, piece).transpose(2, 0, 1, 3)
    parts = lax.all_to_all(own, HEADS + ("z",), 0, 0, tiled=True)
    parts = parts.transpose(1, 0, 2, 3).reshape(1, 2, 128, piece)
    context = lax.all_to_all(
        jnp.broadcast_to(parts, (8, 2, 128, piece)), ("y", "xl"), 0, 0, tiled=True
    )
    keys = context[:, 0].reshape(1024, piece)
    values = context[:, 1].reshape(1024, piece)
    bias = context_bias(lengths, slot_passage, 256)

    wide_states = all_features(decoder_states)
    wide_grad = all_features(output_cotangent)
    queries = jnp.dot(wide_states, query_weight, preferred_element_type=F32).astype(BF16)
    heads_grad = dot(wide_grad, output_weight, ((1,), (1,))).astype(BF16)

    def by_heads(rows):
        split = rows.reshape(tokens, layers, piece).transpose(1, 0, 2)
        return lax.all_to_all(split, "z", 0, 0, tiled=True).reshape(layers * tokens, piece)

    group_queries = by_heads(queries)
    group_grad = by_heads(heads_grad)

    def column_block(full):
        half = lax.dynamic_index_in_dim(full.reshape(tokens, layers, 2, cols // 2), core, 2, False)
        mine = lax.all_to_all(half.transpose(1, 0, 2), "z", 0, 0, tiled=True)
        mine = mine.reshape(layers * tokens, cols // 2)
        return ordered(mine, lax.ppermute(mine, "core", SWAP), core, 1)

    group_cotangent = column_block(wide_grad)
    group_states = column_block(wide_states)

    heads_out, query_grad, key_terms, value_terms = attention(
        bias, group_queries, group_grad, keys, values
    )

    def along_z(local):
        copies = jnp.broadcast_to(local[None], (layers,) + local.shape)
        return lax.all_to_all(copies, "z", 0, 0, tiled=True)

    every_out = along_z(heads_out)

    def plane_sum(terms):
        moved = lax.all_to_all(terms, ("y", "xl"), 0, 0, tiled=True)
        return jnp.sum(moved.astype(F32), axis=0)

    output_weight_grad = plane_sum(output_weight_terms(every_out, group_cotangent))

    own_out = lax.dynamic_slice_in_dim(every_out, z * tokens, tokens, 1)
    own_out = own_out.transpose(1, 0, 2).reshape(tokens, cols)
    partial = jnp.dot(own_out, output_weight, preferred_element_type=F32)
    partial = partial.reshape(tokens, 2, 2, cols)
    kept = lax.dynamic_index_in_dim(partial, core, 2, False)
    given = lax.dynamic_index_in_dim(partial, 1 - core, 2, False).astype(BF16)
    pair = kept + lax.ppermute(given, "core", SWAP).astype(F32)
    kept = lax.dynamic_index_in_dim(pair, xh, 1, False)
    given = lax.dynamic_index_in_dim(pair, 1 - xh, 1, False).astype(BF16)
    attended = (kept + lax.ppermute(given, "xh", SWAP).astype(F32)).astype(BF16)

    every_query_grad = along_z(query_grad)
    query_weight_grad = plane_sum(
        query_weight_terms(group_states, every_query_grad).reshape(8, 128, cols)
    )

    terms = jnp.stack([key_terms.reshape(8, 128, piece), value_terms.reshape(8, 128, piece)], 1)
    sums = plane_sum(terms).astype(BF16)
    owned = lax.all_to_all(
        sums.reshape(2, 16, 8, piece).transpose(1, 0, 2, 3), HEADS + ("z",), 0, 0, tiled=True
    )
    owned = owned.transpose(1, 2, 0, 3).reshape(2, 8, 16 * piece).astype(F32)
    return attended, query_weight_grad, output_weight_grad, owned[0], owned[1]


def solution(mesh):
    devices = mesh.devices.reshape([size for _, size in AXES])
    split = Mesh(devices, [name for name, _ in AXES])
    return jax.shard_map(
        on_device,
        mesh=split,
        in_specs=(
            P(SEQ, HEADS),
            P(None, HEADS),
            P(HEADS, None),
            P(HEADS + SEQ, None),
            P(HEADS + SEQ, None),
            P(),
            P(),
            P(SEQ, HEADS),
        ),
        out_specs=(
            P(SEQ, HEADS),
            P(SEQ, HEADS),
            P(HEADS, SEQ),
            P(HEADS + SEQ, None),
            P(HEADS + SEQ, None),
        ),
        check_vma=False,
    )
```

```python
import math

import jax
import jax.numpy as jnp
from jax import lax
from jax.experimental import pallas as pl
from jax.experimental.pallas import tpu as pltpu
from jax.sharding import Mesh
from jax.sharding import PartitionSpec as P

HEAD = 128
SCALE = 1.0 / math.sqrt(HEAD)
F32 = jnp.float32
BF16 = jnp.bfloat16
AXES = (("xh", 2), ("core", 2), ("z", 4), ("y", 4), ("xl", 2))
HEADS = ("xh", "core")
SEQ = ("z", "y", "xl")
XH, CORE, Z, Y, XL = range(5)
SWAP = [(0, 1), (1, 0)]
VMEM = 56 * 1024 * 1024
TOK = 256
PIECE = 256
GROUP = 4 * TOK
BLOCK = 1024
PLANES = 8


def dot(a, b, contract=((1,), (0,))):
    return lax.dot_general(a, b, (contract, ((), ())), preferred_element_type=F32)


def shifted(index, by, size=4):
    return lax.rem(index + by + size, size)


def head_block(step, pos):
    return lax.rem(pos[XH] + step // 2, 2) * 2 + lax.rem(pos[CORE] + step % 2, 2)


def plane_at(r, pos):
    return shifted(pos[Y], r // 2) * 2 + lax.rem(pos[XL] + r % 2, 2)


def struct(shape, dtype=BF16):
    return jax.ShapeDtypeStruct(shape, dtype)


def whole(shape):
    return pl.BlockSpec(shape, lambda *_: (0,) * len(shape))


def call(kernel, name, grid, in_specs, out_specs, out_shape, scratch, flops, moved, pos, *args):
    return pl.pallas_call(
        kernel,
        grid_spec=pltpu.PrefetchScalarGridSpec(
            num_scalar_prefetch=1,
            grid=grid,
            in_specs=in_specs,
            out_specs=out_specs,
            scratch_shapes=scratch,
        ),
        out_shape=out_shape,
        compiler_params=pltpu.CompilerParams(vmem_limit_bytes=VMEM),
        cost_estimate=pl.CostEstimate(flops=flops, bytes_accessed=moved, transcendentals=0),
        name=name,
    )(pos, *args)


def project_kernel(transposed, pos, x0, x1, x2, x3, w_ref, *rest):
    rows, parts, (total, held) = rest[:4], rest[4:8], rest[8:]
    step = pl.program_id(0)
    contract = ((1,), (1,)) if transposed else ((1,), (0,))
    for i, x in enumerate((x0, x1, x2, x3)):

        @pl.when(step == i)
        def _(i=i, x=x):
            product = dot(x[...], w_ref[...], contract)
            total[...] = product if i == 0 else total[...] + product
            held[head_block(i, pos)] = x[...]

    @pl.when(step == 3)
    def _():
        half = pl.multiple_of(pos[CORE] * (BLOCK // 2), BLOCK // 2)
        for d in range(4):
            layer = shifted(pos[Z], d)
            start = pl.multiple_of(layer * PIECE, PIECE)
            rows[d][...] = total[:, pl.ds(start, PIECE)].astype(BF16)
            parts[d][...] = held[layer, :, pl.ds(half, BLOCK // 2)]


def project(name, pos, blocks, weight, transposed):
    where = (lambda i, pos: (0, head_block(i, pos))) if transposed else (lambda i, pos: (head_block(i, pos), 0))
    outs = call(
        lambda *refs: project_kernel(transposed, *refs),
        name,
        (4,),
        [whole((TOK, BLOCK))] * 4 + [pl.BlockSpec((BLOCK, BLOCK), where)],
        [whole((TOK, PIECE))] * 4 + [whole((TOK, BLOCK // 2))] * 4,
        [struct((TOK, PIECE))] * 4 + [struct((TOK, BLOCK // 2))] * 4,
        [pltpu.VMEM((TOK, BLOCK), F32), pltpu.VMEM((4, TOK, BLOCK), BF16)],
        2 * TOK * 4 * BLOCK * BLOCK,
        2 * 4 * BLOCK * BLOCK,
        pos,
        *blocks,
        weight,
    )
    return outs[:4], outs[4:]


def assemble_kernel(transposed, pos, *refs):
    out = refs[8]
    for d in range(4):
        token = pl.multiple_of(shifted(pos[Z], -d) * TOK, TOK)
        for side in range(2):
            half = pl.multiple_of(lax.rem(pos[CORE] + side, 2) * (BLOCK // 2), BLOCK // 2)
            part = refs[4 * side + d][...]
            if transposed:
                out[pl.ds(half, BLOCK // 2), pl.ds(token, TOK)] = part.T
            else:
                out[pl.ds(token, TOK), pl.ds(half, BLOCK // 2)] = part


def assemble(name, pos, mine, other, transposed):
    return call(
        lambda *refs: assemble_kernel(transposed, *refs),
        name,
        (1,),
        [whole((TOK, BLOCK // 2))] * 8,
        whole((BLOCK, GROUP)),
        struct((BLOCK, GROUP)),
        [],
        0,
        4 * BLOCK * GROUP,
        pos,
        *mine,
        *other,
    )


def attention_kernel(pos, bias, *refs):
    q_refs, g_refs, kv_refs = refs[:4], refs[4:8], refs[8:16]
    out_ref, dq_ref, grad_refs = refs[16], refs[17], refs[18:26]
    dk_sum, dv_sum = refs[26:]
    k = jnp.concatenate([ref[0] for ref in kv_refs], axis=0)
    v = jnp.concatenate([ref[1] for ref in kv_refs], axis=0)
    for d in range(4):
        q, g = q_refs[d][...], g_refs[d][...]
        scores = dot(q, k, ((1,), (1,))) + bias[...]
        top = jnp.max(scores, axis=1, keepdims=True)
        weights = jnp.exp((scores - top) * SCALE)
        probs = weights * (1.0 / jnp.sum(weights, axis=1, keepdims=True))
        probs_low = probs.astype(BF16)
        heads_out = dot(probs_low, v).astype(BF16)
        value_dots = dot(g, v, ((1,), (1,)))
        delta = jnp.sum(g.astype(F32) * heads_out.astype(F32), axis=1, keepdims=True)
        score_grad = (probs * (value_dots - delta) * SCALE).astype(BF16)
        token = pl.multiple_of(shifted(pos[Z], -d) * TOK, TOK)
        out_ref[:, pl.ds(token, TOK)] = heads_out.T
        dq_ref[pl.ds(token, TOK), :] = dot(score_grad, k).astype(BF16)
        dk_term, dv_term = dot(q, score_grad, ((0,), (0,))), dot(g, probs_low, ((0,), (0,)))
        dk_sum[...] = dk_term if d == 0 else dk_sum[...] + dk_term
        dv_sum[...] = dv_term if d == 0 else dv_sum[...] + dv_term
    dk, dv = dk_sum[...].T.astype(BF16), dv_sum[...].T.astype(BF16)
    for r in range(PLANES):
        grad_refs[r][0] = dk[r * 128 : (r + 1) * 128]
        grad_refs[r][1] = dv[r * 128 : (r + 1) * 128]


def attention(pos, bias, queries, grads, context):
    rows = pl.BlockSpec((TOK, HEAD), lambda h, pos: (0, h))
    pair = pl.BlockSpec((2, 128, HEAD), lambda h, pos: (0, 0, h))
    tokens = PLANES * 128
    outs = call(
        attention_kernel,
        "attention",
        (PIECE // HEAD,),
        [whole((1, tokens))] + [rows] * 8 + [pair] * 8,
        [
            pl.BlockSpec((HEAD, GROUP), lambda h, pos: (h, 0)),
            pl.BlockSpec((GROUP, HEAD), lambda h, pos: (0, h)),
        ]
        + [pair] * 8,
        [struct((PIECE, GROUP)), struct((GROUP, PIECE))] + [struct((2, 128, PIECE))] * 8,
        [pltpu.VMEM((HEAD, tokens), F32)] * 2,
        30 * GROUP * PIECE * tokens,
        2 * (4 * GROUP * PIECE + 4 * tokens * PIECE),
        pos,
        bias,
        *queries,
        *grads,
        *context,
    )
    return outs[0], outs[1], outs[2:]


def output_grad_kernel(pos, *refs):
    left, right, outs, held = refs[:4], refs[4], refs[5:13], refs[13]
    for e in range(4):
        row = pl.multiple_of(shifted(pos[Z], -e) * PIECE, PIECE)
        product = dot(left[e][...], right[...]).astype(BF16)
        for p in range(PLANES):
            held[p, pl.ds(row, PIECE), :] = product[:, p * 128 : (p + 1) * 128]
    for r in range(PLANES):
        outs[r][...] = held[plane_at(r, pos)]


def query_grad_kernel(pos, *refs):
    left, right, outs, held = refs[0], refs[1:5], refs[5:13], refs[13]
    for e in range(4):
        col = pl.multiple_of(shifted(pos[Z], -e) * PIECE, PIECE)
        held[:, pl.ds(col, PIECE)] = dot(left[...], right[e][...]).astype(BF16)
    for r in range(PLANES):
        outs[r][...] = held[pl.ds(pl.multiple_of(plane_at(r, pos) * 128, 128), 128), :]


def weight_terms(name, kernel, pos, args, out, held):
    return call(
        kernel,
        name,
        (1,),
        [whole(a.shape) for a in args],
        [whole(out)] * PLANES,
        [struct(out)] * PLANES,
        [pltpu.VMEM(held, BF16)],
        2 * GROUP * BLOCK * BLOCK,
        6 * BLOCK * BLOCK,
        pos,
        *args,
    )


def output_kernel(pos, *refs):
    rows, w_ref, give, keep = refs[:4], refs[4], refs[5], refs[6]
    step = pl.program_id(0)
    product = jnp.zeros((TOK, BLOCK), F32)
    for e in range(4):
        row = pl.multiple_of(shifted(pos[Z], -e) * PIECE, PIECE)
        product = product + dot(rows[e][...], w_ref[pl.ds(row, PIECE), :], ((0,), (0,)))

    @pl.when(step < 2)
    def _():
        give[0] = product.astype(BF16)

    @pl.when(step >= 2)
    def _():
        keep[0] = product


def output_terms(pos, every_out, weight):
    return call(
        output_kernel,
        "output_terms",
        (4,),
        [pl.BlockSpec((PIECE, TOK), lambda n, pos: (0, pos[Z]))] * 4
        + [pl.BlockSpec((BLOCK, BLOCK), lambda n, pos: (0, head_block((n % 2) * 2 + 1 - n // 2, pos)))],
        [
            pl.BlockSpec((1, TOK, BLOCK), lambda n, pos: (jnp.minimum(n, 1), 0, 0)),
            pl.BlockSpec((1, TOK, BLOCK), lambda n, pos: (jnp.maximum(n - 2, 0), 0, 0)),
        ],
        [struct((2, TOK, BLOCK)), struct((2, TOK, BLOCK), F32)],
        [],
        2 * TOK * 4 * BLOCK * BLOCK,
        2 * 4 * BLOCK * BLOCK,
        pos,
        *every_out,
        weight,
    )


def context_bias(pos, lengths, slot_passage):
    slot_lengths = jnp.sum(
        jnp.where(slot_passage[:, None] == jnp.arange(4)[None, :], lengths[None, :], 0), axis=1
    )
    token = jnp.arange(PLANES * 128, dtype=jnp.int32)
    r, slot, layer, row = token // 128, (token // 32) % 4, (token // 8) % 4, token % 8
    plane = ((pos[Y] - r // 2 + 4) % 4) * 2 + (pos[XL] + r % 2) % 2
    position = (layer * PLANES + plane) * 8 + row
    limit = jnp.sum(jnp.where(slot[:, None] == jnp.arange(4)[None, :], slot_lengths[None, :], 0), axis=1)
    return jnp.where(position < limit, 0.0, -jnp.inf).astype(F32)[None, :]


def on_device(
    decoder_states,
    query_weight,
    output_weight,
    context_keys,
    context_values,
    lengths,
    slot_passage,
    output_cotangent,
):
    pos = jnp.stack([lax.axis_index(name) for name, _ in AXES]).astype(jnp.int32)

    def to_layer(x, d):
        return lax.ppermute(x, "z", [(i, (i + d) % 4) for i in range(4)]) if d else x

    def to_plane(x, r):
        pairs = [
            (y * 2 + xl, ((y + r // 2) % 4) * 2 + (xl + r % 2) % 2) for y in range(4) for xl in range(2)
        ]
        return lax.ppermute(x, ("y", "xl"), pairs) if r else x

    def back(r):
        return ((4 - r // 2) % 4) * 2 + r % 2

    def swap(x, axis):
        return lax.ppermute(x, axis, SWAP)

    def head_blocks(local):
        over_x = swap(local, "xh")
        return local, swap(local, "core"), over_x, swap(over_x, "core")

    states = head_blocks(decoder_states)
    cotangent = head_blocks(output_cotangent)

    own = jnp.stack([context_keys, context_values]).reshape(2, 8, 16, PIECE).transpose(2, 0, 1, 3)
    parts = lax.all_to_all(own, HEADS + ("z",), 0, 0, tiled=True)
    parts = parts.transpose(1, 0, 2, 3).reshape(2, 128, PIECE)
    context = [to_plane(parts, r) for r in range(PLANES)]
    bias = context_bias(pos, lengths, slot_passage)

    queries, state_parts = project("queries", pos, states, query_weight, False)
    heads_grad, cotangent_parts = project("heads_grad", pos, cotangent, output_weight, True)
    queries = [to_layer(x, d) for d, x in enumerate(queries)]
    heads_grad = [to_layer(x, d) for d, x in enumerate(heads_grad)]
    cotangent_parts = [to_layer(x, d) for d, x in enumerate(cotangent_parts)]
    state_parts = [to_layer(x, d) for d, x in enumerate(state_parts)]

    out_local, query_grad_local, context_grads = attention(pos, bias, queries, heads_grad, context)
    every_out = [to_layer(out_local, e) for e in range(4)]
    every_query_grad = [to_layer(query_grad_local, e) for e in range(4)]

    group_cotangent = assemble(
        "group_cotangent", pos, cotangent_parts, [swap(x, "core") for x in cotangent_parts], False
    )
    group_states = assemble("group_states", pos, state_parts, [swap(x, "core") for x in state_parts], True)

    def plane_sum(terms, reverse):
        moved = [to_plane(x, back(r) if reverse else r).astype(F32) for r, x in enumerate(terms)]
        total = moved[0]
        for term in moved[1:]:
            total = total + term
        return total

    terms = weight_terms(
        "output_weight_terms",
        output_grad_kernel,
        pos,
        (*every_out, group_cotangent),
        (BLOCK, 128),
        (PLANES, BLOCK, 128),
    )
    output_weight_grad = plane_sum(terms, False)

    give, keep = output_terms(pos, every_out, output_weight)
    pair = keep + swap(give, "core").astype(F32)
    attended = (pair[0] + swap(pair[1].astype(BF16), "xh").astype(F32)).astype(BF16)

    terms = weight_terms(
        "query_weight_terms",
        query_grad_kernel,
        pos,
        (group_states, *every_query_grad),
        (128, BLOCK),
        (BLOCK, BLOCK),
    )
    query_weight_grad = plane_sum(terms, False)

    sums = plane_sum(context_grads, True).astype(BF16)
    owned = lax.all_to_all(
        sums.reshape(2, 16, 8, PIECE).transpose(1, 0, 2, 3), HEADS + ("z",), 0, 0, tiled=True
    )
    owned = owned.transpose(1, 2, 0, 3).reshape(2, 8, 16 * PIECE).astype(F32)
    return attended, query_weight_grad, output_weight_grad, owned[0], owned[1]


def solution(mesh):
    devices = mesh.devices.reshape([size for _, size in AXES])
    split = Mesh(devices, [name for name, _ in AXES])
    return jax.shard_map(
        on_device,
        mesh=split,
        in_specs=(
            P(SEQ, HEADS),
            P(None, HEADS),
            P(HEADS, None),
            P(HEADS + SEQ, None),
            P(HEADS + SEQ, None),
            P(),
            P(),
            P(SEQ, HEADS),
        ),
        out_specs=(
            P(SEQ, HEADS),
            P(SEQ, HEADS),
            P(HEADS, SEQ),
            P(HEADS + SEQ, None),
            P(HEADS + SEQ, None),
        ),
        check_vma=False,
    )
```

```python
import math

import jax
import jax.numpy as jnp
from jax import lax
from jax.experimental import pallas as pl
from jax.experimental.pallas import tpu as pltpu
from jax.sharding import Mesh
from jax.sharding import PartitionSpec as P

HEAD = 128
SCALE = 1.0 / math.sqrt(HEAD)
F32 = jnp.float32
BF16 = jnp.bfloat16
AXES = (("xh", 2), ("core", 2), ("z", 4), ("y", 4), ("xl", 2))
HEADS = ("xh", "core")
SEQ = ("z", "y", "xl")
XH, CORE, Z = range(3)
SWAP = [(0, 1), (1, 0)]
VMEM = 56 * 1024 * 1024
TOK = 256
PIECE = 256
GROUP = 4 * TOK
BLOCK = 1024
PLANES = 8


def dot(a, b, contract=((1,), (0,))):
    return lax.dot_general(a, b, (contract, ((), ())), preferred_element_type=F32)


def shifted(index, by, size=4):
    return lax.rem(index + by + size, size)


def head_block(step, pos):
    return lax.rem(pos[XH] + step // 2, 2) * 2 + lax.rem(pos[CORE] + step % 2, 2)


def struct(shape, dtype=BF16):
    return jax.ShapeDtypeStruct(shape, dtype)


def whole(shape):
    return pl.BlockSpec(shape, lambda *_: (0,) * len(shape))


def call(kernel, name, grid, in_specs, out_specs, out_shape, scratch, flops, moved, pos, *args):
    return pl.pallas_call(
        kernel,
        grid_spec=pltpu.PrefetchScalarGridSpec(
            num_scalar_prefetch=1,
            grid=grid,
            in_specs=in_specs,
            out_specs=out_specs,
            scratch_shapes=scratch,
        ),
        out_shape=out_shape,
        compiler_params=pltpu.CompilerParams(vmem_limit_bytes=VMEM),
        cost_estimate=pl.CostEstimate(flops=flops, bytes_accessed=moved, transcendentals=0),
        name=name,
    )(pos, *args)


def project_kernel(transposed, final, pos, *refs):
    blocks, w_ref, refs = refs[:4], refs[4], refs[5:]
    before, refs = (refs[0], refs[1:]) if final else (None, refs)
    step = pl.program_id(0)
    contract = ((1,), (1,)) if transposed else ((1,), (0,))
    total = refs[5] if final else refs[0]

    @pl.when(step == 0)
    def _():
        product = dot(blocks[2 if final else 0][...], w_ref[...], contract)
        total[...] = product + before[...] if final else product

    @pl.when(step == 1)
    def _():
        product = total[...] + dot(blocks[3 if final else 1][...], w_ref[...], contract)
        total[...] = product
        if final:
            rows, parts, held = refs[:4], refs[4], refs[6]
            half = pl.multiple_of(pos[CORE] * (BLOCK // 2), BLOCK // 2)
            for d in range(4):
                start = pl.multiple_of(shifted(pos[Z], d) * PIECE, PIECE)
                rows[d][...] = total[:, pl.ds(start, PIECE)].astype(BF16)
                held[...] = blocks[d][...]
                parts[head_block(d, pos)] = held[:, pl.ds(half, BLOCK // 2)]


def project(name, pos, blocks, weight, transposed, before=None):
    final = before is not None
    first = 2 if final else 0

    def where(i, pos):
        block = head_block(i + first, pos)
        return (0, block) if transposed else (block, 0)

    return call(
        lambda *refs: project_kernel(transposed, final, *refs),
        name,
        (2,),
        [whole((TOK, BLOCK))] * 4
        + [pl.BlockSpec((BLOCK, BLOCK), where)]
        + ([whole((TOK, BLOCK))] if final else []),
        [whole((TOK, PIECE))] * 4 + [whole((4, TOK, BLOCK // 2))] if final else whole((TOK, BLOCK)),
        [struct((TOK, PIECE))] * 4 + [struct((4, TOK, BLOCK // 2))] if final else struct((TOK, BLOCK), F32),
        [pltpu.VMEM((TOK, BLOCK), F32), pltpu.VMEM((TOK, BLOCK), BF16)] if final else [],
        4 * TOK * BLOCK * BLOCK,
        4 * BLOCK * BLOCK,
        pos,
        *(blocks if final else blocks[:2] + blocks[:2]),
        weight,
        *([before] if final else []),
    )


def assemble_kernel(transposed, pos, mine, other, out):
    for side, ref in enumerate((mine, other)):
        half = pl.multiple_of(lax.rem(pos[CORE] + side, 2) * (BLOCK // 2), BLOCK // 2)
        if transposed:
            out[pl.ds(half, BLOCK // 2), :] = ref[...].T
        else:
            out[:, pl.ds(half, BLOCK // 2)] = ref[...]


def assemble(name, pos, mine, other, transposed):
    return call(
        lambda *refs: assemble_kernel(transposed, *refs),
        name,
        (1,),
        [whole((GROUP, BLOCK // 2))] * 2,
        whole((BLOCK, GROUP)),
        struct((BLOCK, GROUP)),
        [],
        0,
        4 * BLOCK * GROUP,
        pos,
        mine,
        other,
    )


def forward_kernel(pos, bias, *refs):
    q_refs, (k_ref, v_ref, out_ref, turned_ref, probs_ref) = refs[:4], refs[4:]
    k, v = k_ref[...], v_ref[...]
    for d in range(4):
        scores = dot(q_refs[d][...], k, ((1,), (1,))) + bias[...]
        top = jnp.max(scores, axis=1, keepdims=True)
        weights = jnp.exp((scores - top) * SCALE)
        probs = (weights * (1.0 / jnp.sum(weights, axis=1, keepdims=True))).astype(BF16)
        heads_out = dot(probs, v).astype(BF16)
        probs_ref[0, d * TOK : (d + 1) * TOK, :] = probs
        out_ref[d * TOK : (d + 1) * TOK, :] = heads_out
        token = pl.multiple_of(shifted(pos[Z], -d) * TOK, TOK)
        turned_ref[:, pl.ds(token, TOK)] = heads_out.T


def forward(pos, bias, queries, keys, values):
    rows = pl.BlockSpec((TOK, HEAD), lambda h, pos: (0, h))
    column = pl.BlockSpec((GROUP, HEAD), lambda h, pos: (0, h))
    context = keys.shape[0]
    return call(
        forward_kernel,
        "attention_forward",
        (PIECE // HEAD,),
        [whole((1, context))] + [rows] * 4 + [column] * 2,
        [
            column,
            pl.BlockSpec((HEAD, GROUP), lambda h, pos: (h, 0)),
            pl.BlockSpec((1, GROUP, context), lambda h, pos: (h, 0, 0)),
        ],
        [struct((GROUP, PIECE)), struct((PIECE, GROUP)), struct((PIECE // HEAD, GROUP, context))],
        [],
        12 * GROUP * PIECE * context,
        2 * (4 * GROUP * PIECE + 2 * GROUP * context),
        pos,
        bias,
        *queries,
        keys,
        values,
    )


def backward_kernel(pos, *refs):
    q_refs, g_refs, (k_ref, v_ref, out_ref, probs_ref) = refs[:4], refs[4:8], refs[8:12]
    dq_ref, dk_ref, dv_ref, dk_sum, dv_sum = refs[12:]
    k, v = k_ref[...], v_ref[...]
    for d in range(4):
        q, g = q_refs[d][...], g_refs[d][...]
        probs = probs_ref[0, d * TOK : (d + 1) * TOK, :]
        value_dots = dot(g, v, ((1,), (1,)))
        heads_out = out_ref[d * TOK : (d + 1) * TOK, :]
        delta = jnp.sum(g.astype(F32) * heads_out.astype(F32), axis=1, keepdims=True)
        score_grad = (probs.astype(F32) * ((value_dots - delta) * SCALE)).astype(BF16)
        token = pl.multiple_of(shifted(pos[Z], -d) * TOK, TOK)
        dq_ref[pl.ds(token, TOK), :] = dot(score_grad, k).astype(BF16)
        dk_term, dv_term = dot(q, score_grad, ((0,), (0,))), dot(g, probs, ((0,), (0,)))
        dk_sum[...] = dk_term if d == 0 else dk_sum[...] + dk_term
        dv_sum[...] = dv_term if d == 0 else dv_sum[...] + dv_term
    dk_ref[...] = dk_sum[...].T.astype(BF16)
    dv_ref[...] = dv_sum[...].T.astype(BF16)


def backward(pos, queries, grads, keys, values, heads_out, probs):
    rows = pl.BlockSpec((TOK, HEAD), lambda h, pos: (0, h))
    column = pl.BlockSpec((GROUP, HEAD), lambda h, pos: (0, h))
    context = keys.shape[0]
    return call(
        backward_kernel,
        "attention_backward",
        (PIECE // HEAD,),
        [rows] * 8 + [column] * 3 + [pl.BlockSpec((1, GROUP, context), lambda h, pos: (h, 0, 0))],
        [column] * 3,
        [struct((GROUP, PIECE))] * 3,
        [pltpu.VMEM((HEAD, context), F32)] * 2,
        16 * GROUP * PIECE * context,
        2 * (6 * GROUP * PIECE + 2 * GROUP * context),
        pos,
        *queries,
        *grads,
        keys,
        values,
        heads_out,
        probs,
    )


GATHERED = ((0, 0), (1, 0), (3, 0), (2, 0), (2, 1))


def output_grad_kernel(pos, *refs):
    left, right, out = refs[:5], refs[5], refs[6]
    for ref, (e, part) in zip(left, GATHERED):
        rows = ref.shape[0]
        row = pl.multiple_of(shifted(pos[Z], -e) * PIECE + part * rows, rows)
        product = dot(ref[...], right[...]).astype(BF16)
        for p in range(PLANES):
            out[p, pl.ds(row, rows), :] = product[:, p * 128 : (p + 1) * 128]


def query_grad_kernel(pos, *refs):
    left, right, out = refs[0], refs[1:6], refs[6]
    for e, ref in enumerate(right[:3]):
        col = pl.multiple_of(shifted(pos[Z], -GATHERED[e][0]) * PIECE, PIECE)
        out[:, pl.ds(col, PIECE)] = dot(left[...], ref[...]).astype(BF16)
    col = pl.multiple_of(shifted(pos[Z], -2) * PIECE, PIECE)
    far = jnp.concatenate([right[3][...], right[4][...]], axis=0)
    out[:, pl.ds(col, PIECE)] = dot(left[...], far).astype(BF16)


def weight_terms(name, kernel, pos, args, out):
    return call(
        kernel,
        name,
        (1,),
        [whole(a.shape) for a in args],
        whole(out),
        struct(out),
        [],
        2 * GROUP * BLOCK * BLOCK,
        6 * BLOCK * BLOCK,
        pos,
        *args,
    )


def output_kernel(pos, *refs):
    rows, w_ref, give, keep = refs[:5], refs[5], refs[6], refs[7]
    step = pl.program_id(0)
    product = jnp.zeros((TOK, BLOCK), F32)
    for ref, (e, part) in zip(rows, GATHERED):
        size = ref.shape[0]
        row = pl.multiple_of(shifted(pos[Z], -e) * PIECE + part * size, size)
        product = product + dot(ref[...], w_ref[pl.ds(row, size), :], ((0,), (0,)))

    @pl.when(step < 2)
    def _():
        give[0] = product.astype(BF16)

    @pl.when(step >= 2)
    def _():
        keep[0] = product


def output_terms(pos, every_out, weight):
    return call(
        output_kernel,
        "output_terms",
        (4,),
        [pl.BlockSpec((a.shape[0], TOK), lambda n, pos: (0, pos[Z])) for a in every_out]
        + [pl.BlockSpec((BLOCK, BLOCK), lambda n, pos: (0, head_block((n % 2) * 2 + 1 - n // 2, pos)))],
        [
            pl.BlockSpec((1, TOK, BLOCK), lambda n, pos: (jnp.minimum(n, 1), 0, 0)),
            pl.BlockSpec((1, TOK, BLOCK), lambda n, pos: (jnp.maximum(n - 2, 0), 0, 0)),
        ],
        [struct((2, TOK, BLOCK)), struct((2, TOK, BLOCK), F32)],
        [],
        2 * TOK * 4 * BLOCK * BLOCK,
        2 * 4 * BLOCK * BLOCK,
        pos,
        *every_out,
        weight,
    )


def context_bias(lengths, slot_passage):
    slot_lengths = jnp.sum(
        jnp.where(slot_passage[:, None] == jnp.arange(4)[None, :], lengths[None, :], 0), axis=1
    )
    position = jnp.arange(TOK, dtype=jnp.int32)
    valid = position[None, :] < slot_lengths[:, None]
    return jnp.where(valid, 0.0, -jnp.inf).astype(F32).reshape(1, 4 * TOK)


def on_device(
    decoder_states,
    query_weight,
    output_weight,
    context_keys,
    context_values,
    lengths,
    slot_passage,
    output_cotangent,
):
    pos = jnp.stack([lax.axis_index(name) for name, _ in AXES]).astype(jnp.int32)

    def to_layer(x, d):
        return lax.ppermute(x, "z", [(i, (i + d) % 4) for i in range(4)]) if d else x

    def swap(x, axis):
        return lax.ppermute(x, axis, SWAP)

    own = jnp.stack([context_keys, context_values]).reshape(2, 8, 16, PIECE).transpose(2, 0, 1, 3)
    own = jnp.broadcast_to(own[:, None], (16, PLANES, 2, 8, PIECE)).reshape(128, 2, 8, PIECE)
    context = lax.all_to_all(own, HEADS + SEQ, 0, 0, tiled=True)
    keys = context[:, 0].reshape(4 * TOK, PIECE)
    values = context[:, 1].reshape(4 * TOK, PIECE)
    bias = context_bias(lengths, slot_passage)

    def projected(name, local, weight, transposed):
        over_x = swap(local, "xh")
        near = (local, swap(local, "core"))
        first = project(name + "_near", pos, near, weight, transposed)
        blocks = near + (over_x, swap(over_x, "core"))
        outs = project(name, pos, blocks, weight, transposed, first)
        return [to_layer(x, d) for d, x in enumerate(outs[:4])], outs[4]

    queries, state_parts = projected("queries", decoder_states, query_weight, False)
    heads_grad, cotangent_parts = projected("heads_grad", output_cotangent, output_weight, True)

    def column_block(name, parts, transposed):
        mine = lax.all_to_all(parts, "z", 0, 0, tiled=True).reshape(GROUP, BLOCK // 2)
        return assemble(name, pos, mine, swap(mine, "core"), transposed)

    def along_z(x):
        half = x.shape[0] // 2
        left, right = to_layer(x, 1), to_layer(x, 3)
        return x, left, right, to_layer(left[:half], 1), to_layer(right[half:], 3)

    heads_out, turned_out, probs = forward(pos, bias, queries, keys, values)
    every_out = along_z(turned_out)
    query_grad, key_terms, value_terms = backward(
        pos, queries, heads_grad, keys, values, heads_out, probs
    )
    every_query_grad = along_z(query_grad)

    group_states = column_block("group_states", state_parts, True)
    group_cotangent = column_block("group_cotangent", cotangent_parts, False)

    give, keep = output_terms(pos, every_out, output_weight)
    pair = keep + swap(give, "core").astype(F32)
    attended = (pair[0] + swap(pair[1].astype(BF16), "xh").astype(F32)).astype(BF16)

    def plane_sum(terms):
        return jnp.sum(lax.all_to_all(terms, ("y", "xl"), 0, 0, tiled=True).astype(F32), axis=0)

    terms = weight_terms(
        "output_weight_terms", output_grad_kernel, pos, (*every_out, group_cotangent), (PLANES, BLOCK, 128)
    )
    output_weight_grad = plane_sum(terms)

    terms = jnp.stack([key_terms.reshape(128, 8, PIECE), value_terms.reshape(128, 8, PIECE)], 1)
    moved = lax.all_to_all(terms, HEADS + SEQ, 0, 0, tiled=True)
    owned = jnp.sum(moved.reshape(16, PLANES, 2, 8, PIECE).astype(F32), axis=1)
    owned = owned.transpose(1, 2, 0, 3).reshape(2, 8, 16 * PIECE)

    terms = weight_terms(
        "query_weight_terms", query_grad_kernel, pos, (group_states, *every_query_grad), (BLOCK, BLOCK)
    )
    query_weight_grad = plane_sum(terms.reshape(PLANES, 128, BLOCK))
    return attended, query_weight_grad, output_weight_grad, owned[0], owned[1]


def solution(mesh):
    devices = mesh.devices.reshape([size for _, size in AXES])
    split = Mesh(devices, [name for name, _ in AXES])
    return jax.shard_map(
        on_device,
        mesh=split,
        in_specs=(
            P(SEQ, HEADS),
            P(None, HEADS),
            P(HEADS, None),
            P(HEADS + SEQ, None),
            P(HEADS + SEQ, None),
            P(),
            P(),
            P(SEQ, HEADS),
        ),
        out_specs=(
            P(SEQ, HEADS),
            P(SEQ, HEADS),
            P(HEADS, SEQ),
            P(HEADS + SEQ, None),
            P(HEADS + SEQ, None),
        ),
        check_vma=False,
    )
```

```python
import math

import jax
import jax.numpy as jnp
from jax import lax
from jax.experimental import pallas as pl
from jax.experimental.pallas import tpu as pltpu
from jax.sharding import Mesh
from jax.sharding import PartitionSpec as P

HEAD = 128
SCALE = 1.0 / math.sqrt(HEAD)
LOG2E = math.log2(math.e)
F32 = jnp.float32
BF16 = jnp.bfloat16
AXES = (("xh", 2), ("core", 2), ("z", 4), ("y", 4), ("xl", 2))
HEADS = ("xh", "core")
SEQ = ("z", "y", "xl")
XH, CORE, Z = range(3)
SWAP = [(0, 1), (1, 0)]
WORK = 8 * 1024 * 1024
TOK = 256
PIECE = 256
GROUP = 4 * TOK
BLOCK = 1024
PLANES = 8


def dot(a, b, contract=((1,), (0,))):
    return lax.dot_general(a, b, (contract, ((), ())), preferred_element_type=F32)


def shifted(index, by, size=4):
    return lax.rem(index + by + size, size)


def head_block(step, pos):
    return lax.rem(pos[XH] + step // 2, 2) * 2 + lax.rem(pos[CORE] + step % 2, 2)


def struct(shape, dtype=BF16):
    return jax.ShapeDtypeStruct(shape, dtype)


def whole(shape):
    return pl.BlockSpec(shape, lambda *_: (0,) * len(shape))


def call(kernel, name, grid, in_specs, out_specs, out_shape, scratch, flops, moved, pos, *args):
    outs = zip(jax.tree.leaves(out_specs), jax.tree.leaves(out_shape))
    blocks = [(s.block_shape, a.dtype) for s, a in [*zip(in_specs, args), *outs]]
    room = sum(2 * math.prod(shape) * dtype.itemsize for shape, dtype in blocks)
    room += sum(math.prod(s.shape) * jnp.dtype(s.dtype).itemsize for s in scratch)
    return pl.pallas_call(
        kernel,
        grid_spec=pltpu.PrefetchScalarGridSpec(
            num_scalar_prefetch=1,
            grid=grid,
            in_specs=in_specs,
            out_specs=out_specs,
            scratch_shapes=scratch,
        ),
        out_shape=out_shape,
        compiler_params=pltpu.CompilerParams(vmem_limit_bytes=room + WORK),
        cost_estimate=pl.CostEstimate(flops=flops, bytes_accessed=moved, transcendentals=0),
        name=name,
    )(pos, *args)


def project_kernel(transposed, final, pos, *refs):
    blocks, w_ref, refs = refs[:4], refs[4], refs[5:]
    before, refs = (refs[0], refs[1:]) if final else (None, refs)
    step = pl.program_id(0)
    contract = ((1,), (1,)) if transposed else ((1,), (0,))
    total = refs[5] if final else refs[0]

    @pl.when(step == 0)
    def _():
        product = dot(blocks[2 if final else 0][...], w_ref[...], contract)
        total[...] = product + before[...] if final else product

    @pl.when(step == 1)
    def _():
        product = total[...] + dot(blocks[3 if final else 1][...], w_ref[...], contract)
        total[...] = product
        if final:
            rows, parts, held = refs[:4], refs[4], refs[6]
            half = pl.multiple_of(pos[CORE] * (BLOCK // 2), BLOCK // 2)
            for d in range(4):
                start = pl.multiple_of(shifted(pos[Z], d) * PIECE, PIECE)
                rows[d][...] = total[:, pl.ds(start, PIECE)].astype(BF16)
                held[...] = blocks[d][...]
                parts[head_block(d, pos)] = held[:, pl.ds(half, BLOCK // 2)]


def project(name, pos, blocks, weight, transposed, before=None):
    final = before is not None
    first = 2 if final else 0

    def where(i, pos):
        block = head_block(i + first, pos)
        return (0, block) if transposed else (block, 0)

    return call(
        lambda *refs: project_kernel(transposed, final, *refs),
        name,
        (2,),
        [whole((TOK, BLOCK))] * 4
        + [pl.BlockSpec((BLOCK, BLOCK), where)]
        + ([whole((TOK, BLOCK))] if final else []),
        [whole((TOK, PIECE))] * 4 + [whole((4, TOK, BLOCK // 2))] if final else whole((TOK, BLOCK)),
        [struct((TOK, PIECE))] * 4 + [struct((4, TOK, BLOCK // 2))] if final else struct((TOK, BLOCK), F32),
        [pltpu.VMEM((TOK, BLOCK), F32), pltpu.VMEM((TOK, BLOCK), BF16)] if final else [],
        4 * TOK * BLOCK * BLOCK,
        4 * BLOCK * BLOCK,
        pos,
        *(blocks if final else blocks[:2] + blocks[:2]),
        weight,
        *([before] if final else []),
    )


def assemble_kernel(transposed, pos, mine, other, out):
    for side, ref in enumerate((mine, other)):
        half = pl.multiple_of(lax.rem(pos[CORE] + side, 2) * (BLOCK // 2), BLOCK // 2)
        if transposed:
            out[pl.ds(half, BLOCK // 2), :] = ref[...].T
        else:
            out[:, pl.ds(half, BLOCK // 2)] = ref[...]


def assemble(name, pos, mine, other, transposed):
    return call(
        lambda *refs: assemble_kernel(transposed, *refs),
        name,
        (1,),
        [whole((GROUP, BLOCK // 2))] * 2,
        whole((BLOCK, GROUP)),
        struct((BLOCK, GROUP)),
        [],
        0,
        4 * BLOCK * GROUP,
        pos,
        mine,
        other,
    )


def forward_kernel(pos, bias, *refs):
    q_refs, (k_ref, v_ref, out_ref, turned_ref, weights_ref, share_ref) = refs[:4], refs[4:]
    k, v = k_ref[...], v_ref[...]
    for d in range(4):
        here = slice(d * TOK, (d + 1) * TOK)
        scores = dot(q_refs[d][...], k, ((1,), (1,))) + bias[...]
        top = jnp.max(scores, axis=1, keepdims=True)
        weights = jnp.exp2((scores - top) * (SCALE * LOG2E))
        share = 1.0 / jnp.sum(weights, axis=1, keepdims=True)
        weights = weights.astype(BF16)
        heads_out = (dot(weights, v) * share).astype(BF16)
        weights_ref[0, here, :] = weights
        out_ref[here, :] = heads_out
        share_ref[here, :] = jnp.broadcast_to(share, (TOK, HEAD))
        token = pl.multiple_of(shifted(pos[Z], -d) * TOK, TOK)
        turned_ref[:, pl.ds(token, TOK)] = heads_out.T


def forward(pos, bias, queries, keys, values):
    rows = pl.BlockSpec((TOK, HEAD), lambda h, pos: (0, h))
    column = pl.BlockSpec((GROUP, HEAD), lambda h, pos: (0, h))
    context = keys.shape[0]
    return call(
        forward_kernel,
        "attention_forward",
        (PIECE // HEAD,),
        [whole((1, context))] + [rows] * 4 + [column] * 2,
        [
            column,
            pl.BlockSpec((HEAD, GROUP), lambda h, pos: (h, 0)),
            pl.BlockSpec((1, GROUP, context), lambda h, pos: (h, 0, 0)),
            column,
        ],
        [
            struct((GROUP, PIECE)),
            struct((PIECE, GROUP)),
            struct((PIECE // HEAD, GROUP, context)),
            struct((GROUP, PIECE), F32),
        ],
        [],
        12 * GROUP * PIECE * context,
        2 * (4 * GROUP * PIECE + 2 * GROUP * context),
        pos,
        bias,
        *queries,
        keys,
        values,
    )


def backward_kernel(pos, *refs):
    q_refs, g_refs, (k_ref, v_ref, out_ref, weights_ref, share_ref) = refs[:4], refs[4:8], refs[8:13]
    dq_ref, dk_ref, dv_ref, dk_sum, dv_sum = refs[13:]
    k, v = k_ref[...], v_ref[...]
    for d in range(4):
        here = slice(d * TOK, (d + 1) * TOK)
        g = (g_refs[d][...].astype(F32) * (share_ref[here, :] * SCALE)).astype(BF16)
        q, weights = q_refs[d][...], weights_ref[0, here, :]
        delta = jnp.sum(g.astype(F32) * out_ref[here, :].astype(F32), axis=1, keepdims=True)
        score_grad = (weights.astype(F32) * (dot(g, v, ((1,), (1,))) - delta)).astype(BF16)
        token = pl.multiple_of(shifted(pos[Z], -d) * TOK, TOK)
        dq_ref[pl.ds(token, TOK), :] = dot(score_grad, k).astype(BF16)
        dk_term, dv_term = dot(q, score_grad, ((0,), (0,))), dot(g, weights, ((0,), (0,)))
        dk_sum[...] = dk_term if d == 0 else dk_sum[...] + dk_term
        dv_sum[...] = dv_term if d == 0 else dv_sum[...] + dv_term
    dk_ref[...] = dk_sum[...].T.astype(BF16)
    dv_ref[...] = (dv_sum[...] * (1.0 / SCALE)).T.astype(BF16)


def backward(pos, queries, grads, keys, values, heads_out, weights, share):
    rows = pl.BlockSpec((TOK, HEAD), lambda h, pos: (0, h))
    column = pl.BlockSpec((GROUP, HEAD), lambda h, pos: (0, h))
    context = keys.shape[0]
    return call(
        backward_kernel,
        "attention_backward",
        (PIECE // HEAD,),
        [rows] * 8
        + [column] * 3
        + [pl.BlockSpec((1, GROUP, context), lambda h, pos: (h, 0, 0)), column],
        [column] * 3,
        [struct((GROUP, PIECE))] * 3,
        [pltpu.VMEM((HEAD, context), F32)] * 2,
        16 * GROUP * PIECE * context,
        2 * (6 * GROUP * PIECE + 2 * GROUP * context),
        pos,
        *queries,
        *grads,
        keys,
        values,
        heads_out,
        weights,
        share,
    )


GATHERED = ((0, 0), (1, 0), (3, 0), (2, 0), (2, 1))


def output_grad_kernel(pos, *refs):
    left, right, out = refs[:5], refs[5], refs[6]
    for ref, (e, part) in zip(left, GATHERED):
        rows = ref.shape[0]
        row = pl.multiple_of(shifted(pos[Z], -e) * PIECE + part * rows, rows)
        product = dot(ref[...], right[...]).astype(BF16)
        for p in range(PLANES):
            out[p, pl.ds(row, rows), :] = product[:, p * 128 : (p + 1) * 128]


def query_grad_kernel(pos, *refs):
    left, right, out = refs[0], refs[1:6], refs[6]
    for e, ref in enumerate(right[:3]):
        col = pl.multiple_of(shifted(pos[Z], -GATHERED[e][0]) * PIECE, PIECE)
        out[:, pl.ds(col, PIECE)] = dot(left[...], ref[...]).astype(BF16)
    col = pl.multiple_of(shifted(pos[Z], -2) * PIECE, PIECE)
    far = jnp.concatenate([right[3][...], right[4][...]], axis=0)
    out[:, pl.ds(col, PIECE)] = dot(left[...], far).astype(BF16)


def weight_terms(name, kernel, pos, args, out):
    return call(
        kernel,
        name,
        (1,),
        [whole(a.shape) for a in args],
        whole(out),
        struct(out),
        [],
        2 * GROUP * BLOCK * BLOCK,
        6 * BLOCK * BLOCK,
        pos,
        *args,
    )


def output_kernel(pos, *refs):
    rows, w_ref, give, keep = refs[:5], refs[5], refs[6], refs[7]
    step = pl.program_id(0)
    product = jnp.zeros((TOK, BLOCK), F32)
    for ref, (e, part) in zip(rows, GATHERED):
        size = ref.shape[0]
        row = pl.multiple_of(shifted(pos[Z], -e) * PIECE + part * size, size)
        product = product + dot(ref[...], w_ref[pl.ds(row, size), :], ((0,), (0,)))

    @pl.when(step < 2)
    def _():
        give[0] = product.astype(BF16)

    @pl.when(step >= 2)
    def _():
        keep[0] = product


def output_terms(pos, every_out, weight):
    return call(
        output_kernel,
        "output_terms",
        (4,),
        [pl.BlockSpec((a.shape[0], TOK), lambda n, pos: (0, pos[Z])) for a in every_out]
        + [pl.BlockSpec((BLOCK, BLOCK), lambda n, pos: (0, head_block((n % 2) * 2 + 1 - n // 2, pos)))],
        [
            pl.BlockSpec((1, TOK, BLOCK), lambda n, pos: (jnp.minimum(n, 1), 0, 0)),
            pl.BlockSpec((1, TOK, BLOCK), lambda n, pos: (jnp.maximum(n - 2, 0), 0, 0)),
        ],
        [struct((2, TOK, BLOCK)), struct((2, TOK, BLOCK), F32)],
        [],
        2 * TOK * 4 * BLOCK * BLOCK,
        2 * 4 * BLOCK * BLOCK,
        pos,
        *every_out,
        weight,
    )


def context_bias(lengths, slot_passage):
    slot_lengths = jnp.sum(
        jnp.where(slot_passage[:, None] == jnp.arange(4)[None, :], lengths[None, :], 0), axis=1
    )
    position = jnp.arange(TOK, dtype=jnp.int32)
    valid = position[None, :] < slot_lengths[:, None]
    return jnp.where(valid, 0.0, -jnp.inf).astype(F32).reshape(1, 4 * TOK)


def on_device(
    decoder_states,
    query_weight,
    output_weight,
    context_keys,
    context_values,
    lengths,
    slot_passage,
    output_cotangent,
):
    pos = jnp.stack([lax.axis_index(name) for name, _ in AXES]).astype(jnp.int32)

    def to_layer(x, d):
        return lax.ppermute(x, "z", [(i, (i + d) % 4) for i in range(4)]) if d else x

    def swap(x, axis):
        return lax.ppermute(x, axis, SWAP)

    def after(x, *others):
        return lax.optimization_barrier((x, *others))[0]

    def near(name, local, weight, transposed):
        blocks = (local, swap(local, "core"))
        return blocks, project(name, pos, blocks, weight, transposed)

    def far(name, blocks, over_x, weight, transposed, first):
        blocks = blocks + (over_x, swap(over_x, "core"))
        outs = project(name, pos, blocks, weight, transposed, first)
        return [to_layer(x, d) for d, x in enumerate(outs[:4])], outs[4]

    states_x = swap(decoder_states, "xh")
    states, first_queries = near("queries_near", decoder_states, query_weight, False)
    cotangent, first_grad = near("heads_grad_near", output_cotangent, output_weight, True)
    states_x = after(states_x, first_queries, first_grad)
    cotangent_x = swap(after(output_cotangent, states_x), "xh")

    own = jnp.stack([context_keys, context_values]).reshape(2, 8, 16, PIECE).transpose(2, 0, 1, 3)
    own = jnp.broadcast_to(own[:, None], (16, PLANES, 2, 8, PIECE)).reshape(128, 2, 8, PIECE)
    context = lax.all_to_all(after(own, first_queries, first_grad), HEADS + SEQ, 0, 0, tiled=True)
    keys = context[:, 0].reshape(4 * TOK, PIECE)
    values = context[:, 1].reshape(4 * TOK, PIECE)
    bias = context_bias(lengths, slot_passage)

    def column_block(name, parts, transposed):
        mine = lax.all_to_all(parts, "z", 0, 0, tiled=True).reshape(GROUP, BLOCK // 2)
        return assemble(name, pos, mine, swap(mine, "core"), transposed)

    def ring_ends(x):
        return to_layer(x, 1), to_layer(x, 3)

    def ring(x, left, right):
        half = x.shape[0] // 2
        return x, left, right, to_layer(left[:half], 1), to_layer(right[half:], 3)

    queries, state_parts = far("queries", states, states_x, query_weight, False, first_queries)
    group_states = column_block("group_states", state_parts, True)
    heads_out, turned_out, weights, share = forward(pos, bias, queries, keys, values)
    left, right = ring_ends(turned_out)
    every_out = ring(turned_out, left, right)

    heads_grad, cotangent_parts = far(
        "heads_grad", cotangent, cotangent_x, output_weight, True, first_grad
    )
    group_cotangent = column_block("group_cotangent", cotangent_parts, False)
    query_grad, key_terms, value_terms = backward(
        pos, queries, heads_grad, keys, values, after(heads_out, left, right), weights, share
    )
    left, right = ring_ends(query_grad)
    every_query_grad = ring(query_grad, left, right)

    give, keep = output_terms(pos, every_out, output_weight)
    pair = keep + swap(give, "core").astype(F32)
    attended = (pair[0] + swap(pair[1].astype(BF16), "xh").astype(F32)).astype(BF16)

    def plane_sum(terms):
        return jnp.sum(lax.all_to_all(terms, ("y", "xl"), 0, 0, tiled=True).astype(F32), axis=0)

    terms = weight_terms(
        "output_weight_terms", output_grad_kernel, pos, (*every_out, group_cotangent), (PLANES, BLOCK, 128)
    )
    pair = lax.psum_scatter(terms, "y", scatter_dimension=0, tiled=True)
    xl = lax.axis_index("xl")
    kept, given = (lax.dynamic_index_in_dim(pair, i, 0, False) for i in (xl, 1 - xl))
    output_weight_grad = kept.astype(F32) + swap(given, "xl").astype(F32)

    terms = jnp.stack([key_terms.reshape(128, 8, PIECE), value_terms.reshape(128, 8, PIECE)], 1)
    moved = lax.all_to_all(after(terms, left, right), HEADS + SEQ, 0, 0, tiled=True)
    owned = jnp.sum(moved.reshape(16, PLANES, 2, 8, PIECE).astype(F32), axis=1)
    owned = owned.transpose(1, 2, 0, 3).reshape(2, 8, 16 * PIECE)

    terms = weight_terms(
        "query_weight_terms", query_grad_kernel, pos, (group_states, *every_query_grad), (BLOCK, BLOCK)
    )
    query_weight_grad = plane_sum(terms.reshape(PLANES, 128, BLOCK))
    return attended, query_weight_grad, output_weight_grad, owned[0], owned[1]


def solution(mesh):
    devices = mesh.devices.reshape([size for _, size in AXES])
    split = Mesh(devices, [name for name, _ in AXES])
    return jax.shard_map(
        on_device,
        mesh=split,
        in_specs=(
            P(SEQ, HEADS),
            P(None, HEADS),
            P(HEADS, None),
            P(HEADS + SEQ, None),
            P(HEADS + SEQ, None),
            P(),
            P(),
            P(SEQ, HEADS),
        ),
        out_specs=(
            P(SEQ, HEADS),
            P(SEQ, HEADS),
            P(HEADS, SEQ),
            P(HEADS + SEQ, None),
            P(HEADS + SEQ, None),
        ),
        check_vma=False,
    )
```

```python
import math

import jax
import jax.numpy as jnp
from jax import lax
from jax.experimental import pallas as pl
from jax.experimental.pallas import tpu as pltpu
from jax.sharding import Mesh
from jax.sharding import PartitionSpec as P

HEAD = 128
SCALE = 1.0 / math.sqrt(HEAD)
LOG2E = math.log2(math.e)
F32 = jnp.float32
BF16 = jnp.bfloat16
AXES = (("xh", 2), ("core", 2), ("z", 4), ("y", 4), ("xl", 2))
HEADS = ("xh", "core")
SEQ = ("z", "y", "xl")
XH, CORE, Z = range(3)
SWAP = [(0, 1), (1, 0)]
WORK = 8 * 1024 * 1024
TOK = 256
PIECE = 256
GROUP = 4 * TOK
BLOCK = 1024
PLANES = 8


def dot(a, b, contract=((1,), (0,))):
    return lax.dot_general(a, b, (contract, ((), ())), preferred_element_type=F32)


def shifted(index, by, size=4):
    return lax.rem(index + by + size, size)


def head_block(step, pos):
    return lax.rem(pos[XH] + step // 2, 2) * 2 + lax.rem(pos[CORE] + step % 2, 2)


def struct(shape, dtype=BF16):
    return jax.ShapeDtypeStruct(shape, dtype)


def whole(shape):
    return pl.BlockSpec(shape, lambda *_: (0,) * len(shape))


def call(kernel, name, grid, in_specs, out_specs, out_shape, scratch, flops, moved, pos, *args):
    outs = zip(jax.tree.leaves(out_specs), jax.tree.leaves(out_shape))
    blocks = [(s.block_shape, a.dtype) for s, a in [*zip(in_specs, args), *outs] if s is not HBM]
    room = sum(2 * math.prod(shape) * dtype.itemsize for shape, dtype in blocks)
    held = [s for s in scratch if s.memory_space == pltpu.VMEM]
    room += sum(math.prod(s.shape) * jnp.dtype(s.dtype).itemsize for s in held)
    return pl.pallas_call(
        kernel,
        grid_spec=pltpu.PrefetchScalarGridSpec(
            num_scalar_prefetch=1,
            grid=grid,
            in_specs=in_specs,
            out_specs=out_specs,
            scratch_shapes=scratch,
        ),
        out_shape=out_shape,
        compiler_params=pltpu.CompilerParams(vmem_limit_bytes=room + WORK),
        cost_estimate=pl.CostEstimate(flops=flops, bytes_accessed=moved, transcendentals=0),
        name=name,
    )(pos, *args)


def weight_copies(pos, w_ref, held, sems, blocks, by_columns):
    copies = []
    for i, block in enumerate(blocks):
        part = pl.ds(pl.multiple_of(head_block(block, pos) * BLOCK, BLOCK), BLOCK)
        source = w_ref.at[:, part] if by_columns else w_ref.at[part, :]
        copies.append(pltpu.make_async_copy(source, held.at[i], sems.at[i]))
        copies[i].start()
    return copies


def near_kernel(transposed, pos, x0, x1, w_ref, out, weights, sems):
    contract = ((1,), (1,)) if transposed else ((1,), (0,))
    copies = weight_copies(pos, w_ref, weights, sems, (0, 1), transposed)
    for i, x in enumerate((x0, x1)):
        copies[i].wait()
        product = dot(x[...], weights[i], contract)
        out[...] = product if i == 0 else out[...] + product


def far_kernel(transposed, pos, x0, x1, x2, x3, before, w_ref, *refs):
    rows, parts, (total, weights, sems) = refs[:4], refs[4], refs[5:]
    contract = ((1,), (1,)) if transposed else ((1,), (0,))
    copies = weight_copies(pos, w_ref, weights, sems, (2, 3), transposed)
    half = pl.multiple_of(pos[CORE] * (BLOCK // 2), BLOCK // 2)
    for i, x in enumerate((x0, x1, x2, x3)):
        parts[head_block(i, pos)] = x[:, pl.ds(half, BLOCK // 2)]
    for i, (x, known) in enumerate(((x2, before), (x3, total))):
        copies[i].wait()
        total[...] = known[...] + dot(x[...], weights[i], contract)
    for d in range(4):
        start = pl.multiple_of(shifted(pos[Z], d) * PIECE, PIECE)
        rows[d][...] = total[:, pl.ds(start, PIECE)].astype(BF16)


HBM = pl.BlockSpec(memory_space=pltpu.HBM)


def near_project(name, pos, blocks, weight, transposed):
    return call(
        lambda *refs: near_kernel(transposed, *refs),
        name,
        (1,),
        [whole((TOK, BLOCK))] * 2 + [HBM],
        whole((TOK, BLOCK)),
        struct((TOK, BLOCK), F32),
        [pltpu.VMEM((2, BLOCK, BLOCK), BF16), pltpu.SemaphoreType.DMA((2,))],
        4 * TOK * BLOCK * BLOCK,
        4 * BLOCK * BLOCK,
        pos,
        *blocks,
        weight,
    )


def far_project(name, pos, blocks, weight, transposed, before):
    outs = call(
        lambda *refs: far_kernel(transposed, *refs),
        name,
        (1,),
        [whole((TOK, BLOCK))] * 5 + [HBM],
        [whole((TOK, PIECE))] * 4 + [whole((4, TOK, BLOCK // 2))],
        [struct((TOK, PIECE))] * 4 + [struct((4, TOK, BLOCK // 2))],
        [
            pltpu.VMEM((TOK, BLOCK), F32),
            pltpu.VMEM((2, BLOCK, BLOCK), BF16),
            pltpu.SemaphoreType.DMA((2,)),
        ],
        4 * TOK * BLOCK * BLOCK,
        4 * BLOCK * BLOCK,
        pos,
        *blocks,
        before,
        weight,
    )
    return outs[:4], outs[4]


def assemble_kernel(pos, mine, other, out):
    for side, ref in enumerate((mine, other)):
        half = pl.multiple_of(lax.rem(pos[CORE] + side, 2) * (BLOCK // 2), BLOCK // 2)
        out[:, pl.ds(half, BLOCK // 2)] = ref[...]


def assemble(name, pos, mine, other):
    return call(
        assemble_kernel,
        name,
        (1,),
        [whole((GROUP, BLOCK // 2))] * 2,
        whole((GROUP, BLOCK)),
        struct((GROUP, BLOCK)),
        [],
        0,
        4 * BLOCK * GROUP,
        pos,
        mine,
        other,
    )


def assemble_turned_kernel(pos, m0, m1, m2, m3, other, out):
    for d, mine in enumerate((m0, m1, m2, m3)):
        token = pl.multiple_of(shifted(pos[Z], -d) * TOK, TOK)
        for side in range(2):
            half = pl.multiple_of(lax.rem(pos[CORE] + side, 2) * (BLOCK // 2), BLOCK // 2)
            part = other[d] if side else mine[...]
            out[pl.ds(half, BLOCK // 2), pl.ds(token, TOK)] = part.T


def assemble_turned(name, pos, mine, other):
    return call(
        assemble_turned_kernel,
        name,
        (1,),
        [whole((TOK, BLOCK // 2))] * 4 + [whole((4, TOK, BLOCK // 2))],
        whole((BLOCK, GROUP)),
        struct((BLOCK, GROUP)),
        [],
        0,
        4 * BLOCK * GROUP,
        pos,
        *mine,
        other,
    )


def forward_kernel(pos, bias, *refs):
    q_refs, (k_ref, v_ref, out_ref, turned_ref, weights_ref, share_ref) = refs[:4], refs[4:]
    k, v = k_ref[...], v_ref[...]
    for d in range(4):
        here = slice(d * TOK, (d + 1) * TOK)
        scores = dot(q_refs[d][...], k, ((1,), (1,))) + bias[...]
        top = jnp.max(scores, axis=1, keepdims=True)
        weights = jnp.exp2((scores - top) * (SCALE * LOG2E))
        share = 1.0 / jnp.sum(weights, axis=1, keepdims=True)
        weights = weights.astype(BF16)
        heads_out = (dot(weights, v) * share).astype(BF16)
        weights_ref[0, here, :] = weights
        out_ref[here, :] = heads_out
        share_ref[here, :] = jnp.broadcast_to(share, (TOK, HEAD))
        token = pl.multiple_of(shifted(pos[Z], -d) * TOK, TOK)
        turned_ref[:, pl.ds(token, TOK)] = heads_out.T


def forward(pos, bias, queries, keys, values):
    rows = pl.BlockSpec((TOK, HEAD), lambda h, pos: (0, h))
    column = pl.BlockSpec((GROUP, HEAD), lambda h, pos: (0, h))
    context = keys.shape[0]
    return call(
        forward_kernel,
        "attention_forward",
        (PIECE // HEAD,),
        [whole((1, context))] + [rows] * 4 + [column] * 2,
        [
            column,
            pl.BlockSpec((HEAD, GROUP), lambda h, pos: (h, 0)),
            pl.BlockSpec((1, GROUP, context), lambda h, pos: (h, 0, 0)),
            column,
        ],
        [
            struct((GROUP, PIECE)),
            struct((PIECE, GROUP)),
            struct((PIECE // HEAD, GROUP, context)),
            struct((GROUP, PIECE), F32),
        ],
        [],
        12 * GROUP * PIECE * context,
        2 * (4 * GROUP * PIECE + 2 * GROUP * context),
        pos,
        bias,
        *queries,
        keys,
        values,
    )


def backward_kernel(pos, *refs):
    q_refs, g_refs, (k_ref, v_ref, out_ref, weights_ref, share_ref) = refs[:4], refs[4:8], refs[8:13]
    dq_ref, dk_ref, dv_ref, dk_sum, dv_sum = refs[13:]
    k, v = k_ref[...], v_ref[...]
    for d in range(4):
        here = slice(d * TOK, (d + 1) * TOK)
        g = (g_refs[d][...].astype(F32) * (share_ref[here, :] * SCALE)).astype(BF16)
        q, weights = q_refs[d][...], weights_ref[0, here, :]
        delta = jnp.sum(g.astype(F32) * out_ref[here, :].astype(F32), axis=1, keepdims=True)
        score_grad = (weights.astype(F32) * (dot(g, v, ((1,), (1,))) - delta)).astype(BF16)
        token = pl.multiple_of(shifted(pos[Z], -d) * TOK, TOK)
        dq_ref[pl.ds(token, TOK), :] = dot(score_grad, k).astype(BF16)
        dk_term, dv_term = dot(q, score_grad, ((0,), (0,))), dot(g, weights, ((0,), (0,)))
        dk_sum[...] = dk_term if d == 0 else dk_sum[...] + dk_term
        dv_sum[...] = dv_term if d == 0 else dv_sum[...] + dv_term
    dk_ref[...] = dk_sum[...].T.astype(BF16)
    dv_ref[...] = (dv_sum[...] * (1.0 / SCALE)).T.astype(BF16)


def backward(pos, queries, grads, keys, values, heads_out, weights, share):
    rows = pl.BlockSpec((TOK, HEAD), lambda h, pos: (0, h))
    column = pl.BlockSpec((GROUP, HEAD), lambda h, pos: (0, h))
    context = keys.shape[0]
    return call(
        backward_kernel,
        "attention_backward",
        (PIECE // HEAD,),
        [rows] * 8
        + [column] * 3
        + [pl.BlockSpec((1, GROUP, context), lambda h, pos: (h, 0, 0)), column],
        [column] * 3,
        [struct((GROUP, PIECE))] * 3,
        [pltpu.VMEM((HEAD, context), F32)] * 2,
        16 * GROUP * PIECE * context,
        2 * (6 * GROUP * PIECE + 2 * GROUP * context),
        pos,
        *queries,
        *grads,
        keys,
        values,
        heads_out,
        weights,
        share,
    )


GATHERED = ((0, 0), (1, 0), (3, 0), (2, 0), (2, 1))


def output_grad_kernel(pos, *refs):
    left, right, out = refs[:5], refs[5], refs[6]
    for ref, (e, part) in zip(left, GATHERED):
        rows = ref.shape[0]
        row = pl.multiple_of(shifted(pos[Z], -e) * PIECE + part * rows, rows)
        product = dot(ref[...], right[...]).astype(BF16)
        for p in range(PLANES):
            out[p, pl.ds(row, rows), :] = product[:, p * 128 : (p + 1) * 128]


def query_grad_kernel(pos, *refs):
    left, right, out = refs[0], refs[1:6], refs[6]
    for e, ref in enumerate(right[:3]):
        col = pl.multiple_of(shifted(pos[Z], -GATHERED[e][0]) * PIECE, PIECE)
        out[:, pl.ds(col, PIECE)] = dot(left[...], ref[...]).astype(BF16)
    col = pl.multiple_of(shifted(pos[Z], -2) * PIECE, PIECE)
    far = jnp.concatenate([right[3][...], right[4][...]], axis=0)
    out[:, pl.ds(col, PIECE)] = dot(left[...], far).astype(BF16)


def weight_terms(name, kernel, pos, args, out):
    return call(
        kernel,
        name,
        (1,),
        [whole(a.shape) for a in args],
        whole(out),
        struct(out),
        [],
        2 * GROUP * BLOCK * BLOCK,
        6 * BLOCK * BLOCK,
        pos,
        *args,
    )


def output_kernel(pos, *refs):
    rows, w_ref, give, keep, weights, sems = refs[:5], *refs[5:]
    copies = weight_copies(pos, w_ref, weights, sems, (1, 3, 0, 2), True)
    for n in range(4):
        copies[n].wait()
        product = jnp.zeros((TOK, BLOCK), F32)
        for ref, (e, part) in zip(rows, GATHERED):
            size = ref.shape[0]
            row = pl.multiple_of(shifted(pos[Z], -e) * PIECE + part * size, size)
            product = product + dot(ref[...], weights[n, pl.ds(row, size), :], ((0,), (0,)))
        if n < 2:
            give[n] = product.astype(BF16)
        else:
            keep[n - 2] = product


def output_terms(pos, every_out, weight):
    return call(
        output_kernel,
        "output_terms",
        (1,),
        [pl.BlockSpec((a.shape[0], TOK), lambda n, pos: (0, pos[Z])) for a in every_out] + [HBM],
        [whole((2, TOK, BLOCK))] * 2,
        [struct((2, TOK, BLOCK)), struct((2, TOK, BLOCK), F32)],
        [pltpu.VMEM((4, BLOCK, BLOCK), BF16), pltpu.SemaphoreType.DMA((4,))],
        2 * TOK * 4 * BLOCK * BLOCK,
        2 * 4 * BLOCK * BLOCK,
        pos,
        *every_out,
        weight,
    )


def context_bias(lengths, slot_passage):
    slot_lengths = jnp.sum(
        jnp.where(slot_passage[:, None] == jnp.arange(4)[None, :], lengths[None, :], 0), axis=1
    )
    position = jnp.arange(TOK, dtype=jnp.int32)
    valid = position[None, :] < slot_lengths[:, None]
    return jnp.where(valid, 0.0, -jnp.inf).astype(F32).reshape(1, 4 * TOK)


def on_device(
    decoder_states,
    query_weight,
    output_weight,
    context_keys,
    context_values,
    lengths,
    slot_passage,
    output_cotangent,
):
    pos = jnp.stack([lax.axis_index(name) for name, _ in AXES]).astype(jnp.int32)

    def to_layer(x, d):
        return lax.ppermute(x, "z", [(i, (i + d) % 4) for i in range(4)]) if d else x

    def swap(x, axis):
        return lax.ppermute(x, axis, SWAP)

    def after(x, *others):
        return lax.optimization_barrier((x, *others))[0]

    def near(name, local, weight, transposed):
        blocks = (local, swap(local, "core"))
        return blocks, near_project(name, pos, blocks, weight, transposed)

    def far(name, blocks, over_x, weight, transposed, first):
        blocks = blocks + (over_x, swap(over_x, "core"))
        rows, parts = far_project(name, pos, blocks, weight, transposed, first)
        return [to_layer(x, d) for d, x in enumerate(rows)], parts

    own = jnp.stack([context_keys, context_values]).reshape(2, 8, 16, PIECE).transpose(2, 0, 1, 3)
    own = jnp.broadcast_to(own[:, None], (16, PLANES, 2, 8, PIECE)).reshape(128, 2, 8, PIECE)
    context = lax.all_to_all(own, HEADS + SEQ, 0, 0, tiled=True)
    keys = context[:, 0].reshape(4 * TOK, PIECE)
    values = context[:, 1].reshape(4 * TOK, PIECE)
    bias = context_bias(lengths, slot_passage)

    states_x = swap(decoder_states, "xh")
    states, first_queries = near("queries_near", decoder_states, query_weight, False)
    cotangent, first_grad = near("heads_grad_near", output_cotangent, output_weight, True)
    states_x = after(states_x, first_queries, first_grad)
    cotangent_x = swap(after(output_cotangent, states_x), "xh")

    def ring_ends(x):
        return to_layer(x, 1), to_layer(x, 3)

    def ring(x, left, right):
        half = x.shape[0] // 2
        return x, left, right, to_layer(left[:half], 1), to_layer(right[half:], 3)

    queries, state_parts = far("queries", states, states_x, query_weight, False, first_queries)
    mine = []
    for d in range(4):
        part = lax.dynamic_index_in_dim(state_parts, shifted(pos[Z], d), 0, False)
        mine.append(to_layer(after(part, *queries) if d else part, d))
    heads_out, turned_out, weights, share = forward(pos, bias, after(queries, *mine[1:]), keys, values)
    left, right = ring_ends(turned_out)
    every_out = ring(turned_out, left, right)

    heads_grad, cotangent_parts = far(
        "heads_grad", cotangent, cotangent_x, output_weight, True, after(first_grad, turned_out)
    )
    query_grad, key_terms, value_terms = backward(
        pos, queries, heads_grad, keys, values, after(heads_out, left, right), weights, share
    )
    left, right = ring_ends(query_grad)
    every_query_grad = ring(query_grad, left, right)

    block = lax.all_to_all(after(cotangent_parts, *heads_grad), "z", 0, 0, tiled=True)
    block = block.reshape(GROUP, BLOCK // 2)
    group_cotangent = assemble("group_cotangent", pos, block, swap(block, "core"))
    other = swap(jnp.stack(after(mine, block)), "core")
    group_states = assemble_turned("group_states", pos, mine, other)

    terms = weight_terms(
        "output_weight_terms",
        output_grad_kernel,
        pos,
        (*after(every_out, left, right), group_cotangent),
        (PLANES, BLOCK, 128),
    )
    pair = lax.psum_scatter(terms, "y", scatter_dimension=0, tiled=True)
    xl = lax.axis_index("xl")
    kept, given = (lax.dynamic_index_in_dim(pair, i, 0, False) for i in (xl, 1 - xl))
    output_weight_grad = kept.astype(F32) + swap(given, "xl").astype(F32)
    every_out = after(every_out, terms)

    give, keep = output_terms(pos, every_out, output_weight)
    pair = keep + swap(give, "core").astype(F32)
    attended = (pair[0] + swap(pair[1].astype(BF16), "xh").astype(F32)).astype(BF16)

    terms = jnp.stack([key_terms.reshape(128, 8, PIECE), value_terms.reshape(128, 8, PIECE)], 1)
    moved = lax.all_to_all(after(terms, left, right, block), HEADS + SEQ, 0, 0, tiled=True)
    owned = jnp.sum(moved.reshape(16, PLANES, 2, 8, PIECE).astype(F32), axis=1)
    owned = owned.transpose(1, 2, 0, 3).reshape(2, 8, 16 * PIECE)

    terms = weight_terms(
        "query_weight_terms", query_grad_kernel, pos, (group_states, *every_query_grad), (BLOCK, BLOCK)
    )
    terms = lax.all_to_all(terms.reshape(PLANES, 128, BLOCK), ("y", "xl"), 0, 0, tiled=True)
    query_weight_grad = jnp.sum(terms.astype(F32), axis=0)
    return attended, query_weight_grad, output_weight_grad, owned[0], owned[1]


def solution(mesh):
    devices = mesh.devices.reshape([size for _, size in AXES])
    split = Mesh(devices, [name for name, _ in AXES])
    return jax.shard_map(
        on_device,
        mesh=split,
        in_specs=(
            P(SEQ, HEADS),
            P(None, HEADS),
            P(HEADS, None),
            P(HEADS + SEQ, None),
            P(HEADS + SEQ, None),
            P(),
            P(),
            P(SEQ, HEADS),
        ),
        out_specs=(
            P(SEQ, HEADS),
            P(SEQ, HEADS),
            P(HEADS, SEQ),
            P(HEADS + SEQ, None),
            P(HEADS + SEQ, None),
        ),
        check_vma=False,
    )
```

```python
import math

import jax
import jax.numpy as jnp
from jax import lax
from jax.experimental import pallas as pl
from jax.experimental.pallas import tpu as pltpu
from jax.sharding import Mesh
from jax.sharding import PartitionSpec as P

HEAD = 128
SCALE = 1.0 / math.sqrt(HEAD)
LOG2E = math.log2(math.e)
F32 = jnp.float32
BF16 = jnp.bfloat16
AXES = (("xh", 2), ("core", 2), ("z", 4), ("y", 4), ("xl", 2))
HEADS = ("xh", "core")
SEQ = ("z", "y", "xl")
XH, CORE, Z = range(3)
SWAP = [(0, 1), (1, 0)]
VMEM = 56 * 1024 * 1024
TOK = 256
PIECE = 256
GROUP = 4 * TOK
BLOCK = 1024
PLANES = 8


def dot(a, b, contract=((1,), (0,))):
    return lax.dot_general(a, b, (contract, ((), ())), preferred_element_type=F32)


def shifted(index, by, size=4):
    return lax.rem(index + by + size, size)


def head_block(step, pos):
    return lax.rem(pos[XH] + step // 2, 2) * 2 + lax.rem(pos[CORE] + step % 2, 2)


def struct(shape, dtype=BF16):
    return jax.ShapeDtypeStruct(shape, dtype)


def whole(shape):
    return pl.BlockSpec(shape, lambda *_: (0,) * len(shape))


def call(kernel, name, grid, in_specs, out_specs, out_shape, scratch, flops, moved, pos, *args):
    return pl.pallas_call(
        kernel,
        grid_spec=pltpu.PrefetchScalarGridSpec(
            num_scalar_prefetch=1,
            grid=grid,
            in_specs=in_specs,
            out_specs=out_specs,
            scratch_shapes=scratch,
        ),
        out_shape=out_shape,
        compiler_params=pltpu.CompilerParams(vmem_limit_bytes=VMEM),
        cost_estimate=pl.CostEstimate(flops=flops, bytes_accessed=moved, transcendentals=0),
        name=name,
    )(pos, *args)


def weight_copies(pos, w_ref, held, sems, blocks, by_columns):
    copies = []
    for i, block in enumerate(blocks):
        part = pl.ds(pl.multiple_of(head_block(block, pos) * BLOCK, BLOCK), BLOCK)
        source = w_ref.at[:, part] if by_columns else w_ref.at[part, :]
        copies.append(pltpu.make_async_copy(source, held.at[i], sems.at[i]))
        copies[i].start()
    return copies


def near_kernel(transposed, pos, x0, x1, w_ref, out, weights, sems):
    contract = ((1,), (1,)) if transposed else ((1,), (0,))
    copies = weight_copies(pos, w_ref, weights, sems, (0, 1), transposed)
    for i, x in enumerate((x0, x1)):
        copies[i].wait()
        product = dot(x[...], weights[i], contract)
        out[...] = product if i == 0 else out[...] + product


def far_kernel(transposed, joined, pos, x0, x1, x2, x3, before, w_ref, *refs):
    rows, (total, weights, sems) = refs[:4], refs[-3:]
    contract = ((1,), (1,)) if transposed else ((1,), (0,))
    copies = weight_copies(pos, w_ref, weights, sems, (2, 3), transposed)
    half = pl.multiple_of(pos[CORE] * (BLOCK // 2), BLOCK // 2)
    for i, x in enumerate((x0, x1, x2, x3)):
        part = x[:, pl.ds(half, BLOCK // 2)]
        if joined:
            for d in range(4):

                @pl.when(shifted(pos[Z], d) == head_block(i, pos))
                def _(d=d, part=part):
                    rows[d][:, PIECE:] = part
        else:
            refs[4][head_block(i, pos)] = part
    for i, (x, known) in enumerate(((x2, before), (x3, total))):
        copies[i].wait()
        total[...] = known[...] + dot(x[...], weights[i], contract)
    for d in range(4):
        start = pl.multiple_of(shifted(pos[Z], d) * PIECE, PIECE)
        rows[d][:, :PIECE] = total[:, pl.ds(start, PIECE)].astype(BF16)


HBM = pl.BlockSpec(memory_space=pltpu.HBM)


def near_project(name, pos, blocks, weight, transposed):
    return call(
        lambda *refs: near_kernel(transposed, *refs),
        name,
        (1,),
        [whole((TOK, BLOCK))] * 2 + [HBM],
        whole((TOK, BLOCK)),
        struct((TOK, BLOCK), F32),
        [pltpu.VMEM((2, BLOCK, BLOCK), BF16), pltpu.SemaphoreType.DMA((2,))],
        4 * TOK * BLOCK * BLOCK,
        4 * BLOCK * BLOCK,
        pos,
        *blocks,
        weight,
    )


def far_project(name, pos, blocks, weight, transposed, joined, before):
    wide = PIECE + BLOCK // 2 if joined else PIECE
    shapes = [(TOK, wide)] * 4 + ([] if joined else [(4, TOK, BLOCK // 2)])
    outs = call(
        lambda *refs: far_kernel(transposed, joined, *refs),
        name,
        (1,),
        [whole((TOK, BLOCK))] * 5 + [HBM],
        [whole(shape) for shape in shapes],
        [struct(shape) for shape in shapes],
        [
            pltpu.VMEM((TOK, BLOCK), F32),
            pltpu.VMEM((2, BLOCK, BLOCK), BF16),
            pltpu.SemaphoreType.DMA((2,)),
        ],
        4 * TOK * BLOCK * BLOCK,
        4 * BLOCK * BLOCK,
        pos,
        *blocks,
        before,
        weight,
    )
    return outs[:4], outs[4:]


def assemble_kernel(pos, mine, other, out):
    for side, ref in enumerate((mine, other)):
        half = pl.multiple_of(lax.rem(pos[CORE] + side, 2) * (BLOCK // 2), BLOCK // 2)
        out[:, pl.ds(half, BLOCK // 2)] = ref[...]


def assemble(name, pos, mine, other):
    return call(
        assemble_kernel,
        name,
        (1,),
        [whole((GROUP, BLOCK // 2))] * 2,
        whole((GROUP, BLOCK)),
        struct((GROUP, BLOCK)),
        [],
        0,
        4 * BLOCK * GROUP,
        pos,
        mine,
        other,
    )


def assemble_turned_kernel(pos, mine, other, out):
    for d in range(4):
        token = pl.multiple_of(shifted(pos[Z], -d) * TOK, TOK)
        for side, ref in enumerate((mine, other)):
            half = pl.multiple_of(lax.rem(pos[CORE] + side, 2) * (BLOCK // 2), BLOCK // 2)
            out[pl.ds(half, BLOCK // 2), pl.ds(token, TOK)] = ref[d].T


def assemble_turned(name, pos, mine, other):
    return call(
        assemble_turned_kernel,
        name,
        (1,),
        [whole((4, TOK, BLOCK // 2))] * 2,
        whole((BLOCK, GROUP)),
        struct((BLOCK, GROUP)),
        [],
        0,
        4 * BLOCK * GROUP,
        pos,
        mine,
        other,
    )


def attention_kernel(pos, bias, *refs):
    q_refs, g_refs, (k_ref, v_ref), refs = refs[:4], refs[4:8], refs[8:10], refs[10:]
    turned_ref, dq_ref, dk_ref, dv_ref, dk_sum, dv_sum = refs
    k, v = k_ref[...], v_ref[...]
    for d in range(4):
        q = q_refs[d][...]
        scores = dot(q, k, ((1,), (1,))) + bias[...]
        top = jnp.max(scores, axis=1, keepdims=True)
        weights = jnp.exp2((scores - top) * (SCALE * LOG2E))
        share = 1.0 / jnp.sum(weights, axis=1, keepdims=True)
        low = weights.astype(BF16)
        heads_out = (dot(low, v) * share).astype(BF16)
        token = pl.multiple_of(shifted(pos[Z], -d) * TOK, TOK)
        turned_ref[:, pl.ds(token, TOK)] = heads_out.T
        g = (g_refs[d][...].astype(F32) * (share * SCALE)).astype(BF16)
        delta = jnp.sum(g.astype(F32) * heads_out.astype(F32), axis=1, keepdims=True)
        score_grad = (low.astype(F32) * (dot(g, v, ((1,), (1,))) - delta)).astype(BF16)
        dq_ref[pl.ds(token, TOK), :] = dot(score_grad, k).astype(BF16)
        dk_term, dv_term = dot(q, score_grad, ((0,), (0,))), dot(g, low, ((0,), (0,)))
        dk_sum[...] = dk_term if d == 0 else dk_sum[...] + dk_term
        dv_sum[...] = dv_term if d == 0 else dv_sum[...] + dv_term
    dk_ref[...] = dk_sum[...].T.astype(BF16)
    dv_ref[...] = (dv_sum[...] * (1.0 / SCALE)).T.astype(BF16)


def attention(pos, bias, queries, grads, keys, values):
    rows = pl.BlockSpec((TOK, HEAD), lambda h, pos: (0, h))
    column = pl.BlockSpec((GROUP, HEAD), lambda h, pos: (0, h))
    context = keys.shape[0]
    return call(
        attention_kernel,
        "attention",
        (PIECE // HEAD,),
        [whole((1, context))] + [rows] * 8 + [column] * 2,
        [pl.BlockSpec((HEAD, GROUP), lambda h, pos: (h, 0))] + [column] * 3,
        [struct((PIECE, GROUP))] + [struct((GROUP, PIECE))] * 3,
        [pltpu.VMEM((HEAD, context), F32)] * 2,
        30 * GROUP * PIECE * context,
        16 * GROUP * PIECE,
        pos,
        bias,
        *queries,
        *grads,
        keys,
        values,
    )


GATHERED = ((0, 0), (1, 0), (3, 0), (2, 0), (2, 1))


def output_grad_kernel(pos, *refs):
    left, right, out = refs[:5], refs[5], refs[6]
    for ref, (e, part) in zip(left, GATHERED):
        rows = ref.shape[0]
        row = pl.multiple_of(shifted(pos[Z], -e) * PIECE + part * rows, rows)
        product = dot(ref[...], right[...]).astype(BF16)
        for p in range(PLANES):
            out[p, pl.ds(row, rows), :] = product[:, p * 128 : (p + 1) * 128]


def query_grad_kernel(pos, *refs):
    left, right, out = refs[0], refs[1:6], refs[6]
    for e, ref in enumerate(right[:3]):
        col = pl.multiple_of(shifted(pos[Z], -GATHERED[e][0]) * PIECE, PIECE)
        out[:, pl.ds(col, PIECE)] = dot(left[...], ref[...]).astype(BF16)
    col = pl.multiple_of(shifted(pos[Z], -2) * PIECE, PIECE)
    far = jnp.concatenate([right[3][...], right[4][...]], axis=0)
    out[:, pl.ds(col, PIECE)] = dot(left[...], far).astype(BF16)


def weight_terms(name, kernel, pos, args, out):
    return call(
        kernel,
        name,
        (1,),
        [whole(a.shape) for a in args],
        whole(out),
        struct(out),
        [],
        2 * GROUP * BLOCK * BLOCK,
        6 * BLOCK * BLOCK,
        pos,
        *args,
    )


def output_kernel(pos, *refs):
    rows, w_ref, give, keep, weights, sems = refs[:5], *refs[5:]
    copies = weight_copies(pos, w_ref, weights, sems, (1, 3, 0, 2), True)
    for n in range(4):
        copies[n].wait()
        product = jnp.zeros((TOK, BLOCK), F32)
        for ref, (e, part) in zip(rows, GATHERED):
            size = ref.shape[0]
            row = pl.multiple_of(shifted(pos[Z], -e) * PIECE + part * size, size)
            product = product + dot(ref[...], weights[n, pl.ds(row, size), :], ((0,), (0,)))
        if n < 2:
            give[n] = product.astype(BF16)
        else:
            keep[n - 2] = product


def output_terms(pos, every_out, weight):
    return call(
        output_kernel,
        "output_terms",
        (1,),
        [pl.BlockSpec((a.shape[0], TOK), lambda n, pos: (0, pos[Z])) for a in every_out] + [HBM],
        [whole((2, TOK, BLOCK))] * 2,
        [struct((2, TOK, BLOCK)), struct((2, TOK, BLOCK), F32)],
        [pltpu.VMEM((4, BLOCK, BLOCK), BF16), pltpu.SemaphoreType.DMA((4,))],
        2 * TOK * 4 * BLOCK * BLOCK,
        2 * 4 * BLOCK * BLOCK,
        pos,
        *every_out,
        weight,
    )


def context_bias(lengths, slot_passage):
    slot_lengths = jnp.sum(
        jnp.where(slot_passage[:, None] == jnp.arange(4)[None, :], lengths[None, :], 0), axis=1
    )
    position = jnp.arange(TOK, dtype=jnp.int32)
    valid = position[None, :] < slot_lengths[:, None]
    return jnp.where(valid, 0.0, -jnp.inf).astype(F32).reshape(1, 4 * TOK)


def on_device(
    decoder_states,
    query_weight,
    output_weight,
    context_keys,
    context_values,
    lengths,
    slot_passage,
    output_cotangent,
):
    pos = jnp.stack([lax.axis_index(name) for name, _ in AXES]).astype(jnp.int32)

    def to_layer(x, d):
        return lax.ppermute(x, "z", [(i, (i + d) % 4) for i in range(4)]) if d else x

    def swap(x, axis):
        return lax.ppermute(x, axis, SWAP)

    def after(x, *others):
        return lax.optimization_barrier((x, *others))[0]

    def near(name, local, weight, transposed):
        blocks = (local, swap(local, "core"))
        return blocks, near_project(name, pos, blocks, weight, transposed)

    def far(name, blocks, over_x, weight, transposed, joined, first):
        blocks = blocks + (over_x, swap(over_x, "core"))
        rows, parts = far_project(name, pos, blocks, weight, transposed, joined, first)
        return [to_layer(x, d) for d, x in enumerate(rows)], parts

    own = jnp.stack([context_keys, context_values]).reshape(2, 8, 16, PIECE).transpose(2, 0, 1, 3)
    own = jnp.broadcast_to(own[:, None], (16, PLANES, 2, 8, PIECE)).reshape(128, 2, 8, PIECE)
    context = lax.all_to_all(own, HEADS + SEQ, 0, 0, tiled=True)
    keys = context[:, 0].reshape(4 * TOK, PIECE)
    values = context[:, 1].reshape(4 * TOK, PIECE)
    bias = context_bias(lengths, slot_passage)

    states_x = swap(decoder_states, "xh")
    states, first_queries = near("queries_near", decoder_states, query_weight, False)
    cotangent, first_grad = near("heads_grad_near", output_cotangent, output_weight, True)
    states_x = after(states_x, first_queries, first_grad)
    cotangent_x = swap(after(output_cotangent, states_x), "xh")

    def ring_ends(x):
        return to_layer(x, 1), to_layer(x, 3)

    def ring(x, left, right):
        half = x.shape[0] // 2
        return x, left, right, to_layer(left[:half], 1), to_layer(right[half:], 3)

    queries, _ = far("queries", states, states_x, query_weight, False, True, first_queries)
    heads_grad, parts = far(
        "heads_grad", cotangent, cotangent_x, output_weight, True, False, after(first_grad, first_queries)
    )
    cotangent_block = lax.all_to_all(after(parts[0], *heads_grad), "z", 0, 0, tiled=True)
    cotangent_block = cotangent_block.reshape(GROUP, BLOCK // 2)

    turned_out, query_grad, key_terms, value_terms = attention(
        pos, bias, queries, heads_grad, keys, values
    )
    left, right = ring_ends(turned_out)
    every_out = ring(turned_out, left, right)
    query_grad = after(query_grad, left, right)
    left, right = ring_ends(query_grad)
    every_query_grad = ring(query_grad, left, right)

    cotangent_block = after(cotangent_block, turned_out)
    group_cotangent = assemble("group_cotangent", pos, cotangent_block, swap(cotangent_block, "core"))
    state_block = jnp.stack([x[:, PIECE:] for x in after(queries, turned_out)])
    group_states = assemble_turned("group_states", pos, state_block, swap(state_block, "core"))

    terms = weight_terms(
        "output_weight_terms",
        output_grad_kernel,
        pos,
        (*every_out, group_cotangent),
        (PLANES, BLOCK, 128),
    )
    pair = lax.psum_scatter(terms, "y", scatter_dimension=0, tiled=True)
    xl = lax.axis_index("xl")
    kept, given = (lax.dynamic_index_in_dim(pair, i, 0, False) for i in (xl, 1 - xl))
    output_weight_grad = kept.astype(F32) + swap(given, "xl").astype(F32)
    every_out = after(every_out, terms)

    give, keep = output_terms(pos, every_out, output_weight)
    pair = keep + swap(give, "core").astype(F32)
    attended = (pair[0] + swap(pair[1].astype(BF16), "xh").astype(F32)).astype(BF16)

    terms = jnp.stack([key_terms.reshape(128, 8, PIECE), value_terms.reshape(128, 8, PIECE)], 1)
    moved = lax.all_to_all(after(terms, left, right), HEADS + SEQ, 0, 0, tiled=True)
    owned = jnp.sum(moved.reshape(16, PLANES, 2, 8, PIECE).astype(F32), axis=1)
    owned = owned.transpose(1, 2, 0, 3).reshape(2, 8, 16 * PIECE)

    terms = weight_terms(
        "query_weight_terms", query_grad_kernel, pos, (group_states, *every_query_grad), (BLOCK, BLOCK)
    )
    terms = lax.all_to_all(terms.reshape(PLANES, 128, BLOCK), ("y", "xl"), 0, 0, tiled=True)
    query_weight_grad = jnp.sum(terms.astype(F32), axis=0)
    return attended, query_weight_grad, output_weight_grad, owned[0], owned[1]


def solution(mesh):
    devices = mesh.devices.reshape([size for _, size in AXES])
    split = Mesh(devices, [name for name, _ in AXES])
    return jax.shard_map(
        on_device,
        mesh=split,
        in_specs=(
            P(SEQ, HEADS),
            P(None, HEADS),
            P(HEADS, None),
            P(HEADS + SEQ, None),
            P(HEADS + SEQ, None),
            P(),
            P(),
            P(SEQ, HEADS),
        ),
        out_specs=(
            P(SEQ, HEADS),
            P(SEQ, HEADS),
            P(HEADS, SEQ),
            P(HEADS + SEQ, None),
            P(HEADS + SEQ, None),
        ),
        check_vma=False,
    )
```

```python
import math

import jax
import jax.numpy as jnp
from jax import lax
from jax.experimental import pallas as pl
from jax.experimental.pallas import tpu as pltpu
from jax.sharding import Mesh
from jax.sharding import PartitionSpec as P

HEAD = 128
SCALE = 1.0 / math.sqrt(HEAD)
LOG2E = math.log2(math.e)
F32 = jnp.float32
BF16 = jnp.bfloat16
AXES = (("xh", 2), ("core", 2), ("z", 4), ("y", 4), ("xl", 2))
HEADS = ("xh", "core")
SEQ = ("z", "y", "xl")
XH, CORE, Z, Y, XL = range(5)
SWAP = [(0, 1), (1, 0)]
VMEM = 56 * 1024 * 1024
TOK = 256
PIECE = 256
GROUP = 4 * TOK
BLOCK = 1024
PLANES = 8


def dot(a, b, contract=((1,), (0,))):
    return lax.dot_general(a, b, (contract, ((), ())), preferred_element_type=F32)


def shifted(index, by, size=4):
    return lax.rem(index + by + size, size)


def head_block(step, pos):
    return lax.rem(pos[XH] + step // 2, 2) * 2 + lax.rem(pos[CORE] + step % 2, 2)


def struct(shape, dtype=BF16):
    return jax.ShapeDtypeStruct(shape, dtype)


def whole(shape):
    return pl.BlockSpec(shape, lambda *_: (0,) * len(shape))


def call(kernel, name, grid, in_specs, out_specs, out_shape, scratch, flops, moved, pos, *args):
    return pl.pallas_call(
        kernel,
        grid_spec=pltpu.PrefetchScalarGridSpec(
            num_scalar_prefetch=1,
            grid=grid,
            in_specs=in_specs,
            out_specs=out_specs,
            scratch_shapes=scratch,
        ),
        out_shape=out_shape,
        compiler_params=pltpu.CompilerParams(vmem_limit_bytes=VMEM),
        cost_estimate=pl.CostEstimate(flops=flops, bytes_accessed=moved, transcendentals=0),
        name=name,
    )(pos, *args)


def weight_copies(pos, w_ref, held, sems, blocks, by_columns):
    copies = []
    for i, block in enumerate(blocks):
        part = pl.ds(pl.multiple_of(head_block(block, pos) * BLOCK, BLOCK), BLOCK)
        source = w_ref.at[:, part] if by_columns else w_ref.at[part, :]
        copies.append(pltpu.make_async_copy(source, held.at[i], sems.at[i]))
        copies[i].start()
    return copies


def near_kernel(transposed, pos, x0, x1, w_ref, out, weights, sems):
    contract = ((1,), (1,)) if transposed else ((1,), (0,))
    copies = weight_copies(pos, w_ref, weights, sems, (0, 1), transposed)
    for i, x in enumerate((x0, x1)):
        copies[i].wait()
        product = dot(x[...], weights[i], contract)
        out[...] = product if i == 0 else out[...] + product


def far_kernel(transposed, pos, x0, x1, x2, x3, before, w_ref, *refs):
    states, refs = (None, refs) if len(refs) == 11 else (refs[0], refs[1:])
    rows, parts, (blocks, known, total, weights, weight_sems, sems) = refs[:4], refs[4], refs[5:]
    contract = ((1,), (1,)) if transposed else ((1,), (0,))
    weight_moves = weight_copies(pos, w_ref, weights, weight_sems, (2, 3), transposed)
    moves = [pltpu.make_async_copy(before, known, sems.at[4])]
    moves[0].start()
    for i, x in ((2, x2), (3, x3), (0, x0), (1, x1)):
        moves.append(pltpu.make_async_copy(x, blocks.at[i], sems.at[i]))
        moves[-1].start()
    half = pl.multiple_of(pos[CORE] * (BLOCK // 2), BLOCK // 2)
    if states is not None:
        parts[:, 0] = states[...]
    for move in moves:
        move.wait()
    for i in range(4):
        part = blocks[i, :, pl.ds(half, BLOCK // 2)]
        if states is None:
            parts[head_block(i, pos)] = part
        else:
            parts[head_block(i, pos), 1] = part
    for i, start in ((2, known), (3, total)):
        weight_moves[i - 2].wait()
        total[...] = start[...] + dot(blocks[i], weights[i - 2], contract)
    for d in range(4):
        start = pl.multiple_of(shifted(pos[Z], d) * PIECE, PIECE)
        rows[d][...] = total[:, pl.ds(start, PIECE)].astype(BF16)


HBM = pl.BlockSpec(memory_space=pltpu.HBM)


def near_project(name, pos, blocks, weight, transposed):
    return call(
        lambda *refs: near_kernel(transposed, *refs),
        name,
        (1,),
        [whole((TOK, BLOCK))] * 2 + [HBM],
        whole((TOK, BLOCK)),
        struct((TOK, BLOCK), F32),
        [pltpu.VMEM((2, BLOCK, BLOCK), BF16), pltpu.SemaphoreType.DMA((2,))],
        4 * TOK * BLOCK * BLOCK,
        4 * BLOCK * BLOCK,
        pos,
        *blocks,
        weight,
    )


def far_project(name, pos, blocks, weight, transposed, before, states=None):
    part = (4, TOK, BLOCK // 2) if states is None else (4, 2, TOK, BLOCK // 2)
    extra = () if states is None else (states,)
    outs = call(
        lambda *refs: far_kernel(transposed, *refs),
        name,
        (1,),
        [HBM] * 6 + [whole(a.shape) for a in extra],
        [whole((TOK, PIECE))] * 4 + [whole(part)],
        [struct((TOK, PIECE))] * 4 + [struct(part)],
        [
            pltpu.VMEM((4, TOK, BLOCK), BF16),
            pltpu.VMEM((TOK, BLOCK), F32),
            pltpu.VMEM((TOK, BLOCK), F32),
            pltpu.VMEM((2, BLOCK, BLOCK), BF16),
            pltpu.SemaphoreType.DMA((2,)),
            pltpu.SemaphoreType.DMA((5,)),
        ],
        4 * TOK * BLOCK * BLOCK,
        4 * BLOCK * BLOCK,
        pos,
        *blocks,
        before,
        weight,
        *extra,
    )
    return outs[:4], outs[4]


def assemble_kernel(turned, pos, mine, other, out):
    for side, ref in enumerate((mine, other)):
        half = pl.multiple_of(lax.rem(pos[CORE] + side, 2) * (BLOCK // 2), BLOCK // 2)
        for layer in range(4):
            token = slice(layer * TOK, (layer + 1) * TOK)
            if turned:
                out[pl.ds(half, BLOCK // 2), token] = ref[layer, 0].T
            else:
                out[token, pl.ds(half, BLOCK // 2)] = ref[layer, 0]


def assemble(name, pos, mine, other, which, turned):
    half = pl.BlockSpec((4, 1, TOK, BLOCK // 2), lambda i, pos: (0, which, 0, 0))
    return call(
        lambda *refs: assemble_kernel(turned, *refs),
        name,
        (1,),
        [half] * 2,
        whole((GROUP, BLOCK)),
        struct((GROUP, BLOCK)),
        [],
        0,
        4 * BLOCK * GROUP,
        pos,
        mine,
        other,
    )


def attention_kernel(pos, bias, *refs):
    q_refs, g_refs, (k_ref, v_ref), refs = refs[:4], refs[4:8], refs[8:10], refs[10:]
    turned_ref, dq_ref, dk_ref, dv_ref, dk_sum, dv_sum = refs
    k, v = k_ref[...], v_ref[...]
    for d in range(4):
        q = q_refs[d][...]
        scores = dot(q, k, ((1,), (1,))) + bias[...]
        top = jnp.max(scores, axis=1, keepdims=True)
        weights = jnp.exp2((scores - top) * (SCALE * LOG2E))
        share = 1.0 / jnp.sum(weights, axis=1, keepdims=True)
        low = weights.astype(BF16)
        heads_out = (dot(low, v) * share).astype(BF16)
        token = pl.multiple_of(shifted(pos[Z], -d) * TOK, TOK)
        turned_ref[:, pl.ds(token, TOK)] = heads_out.T
        g = (g_refs[d][...].astype(F32) * (share * SCALE)).astype(BF16)
        delta = jnp.sum(g.astype(F32) * heads_out.astype(F32), axis=1, keepdims=True)
        score_grad = (low.astype(F32) * (dot(g, v, ((1,), (1,))) - delta)).astype(BF16)
        dq_ref[pl.ds(token, TOK), :] = dot(score_grad, k).astype(BF16)
        dk_term, dv_term = dot(q, score_grad, ((0,), (0,))), dot(g, low, ((0,), (0,)))
        dk_sum[...] = dk_term if d == 0 else dk_sum[...] + dk_term
        dv_sum[...] = dv_term if d == 0 else dv_sum[...] + dv_term
    dk_ref[...] = dk_sum[...].T.astype(BF16)
    dv_ref[...] = (dv_sum[...] * (1.0 / SCALE)).T.astype(BF16)


def attention(pos, bias, queries, grads, keys, values):
    rows = pl.BlockSpec((TOK, HEAD), lambda h, pos: (0, h))
    column = pl.BlockSpec((GROUP, HEAD), lambda h, pos: (0, h))
    context = keys.shape[0]
    return call(
        attention_kernel,
        "attention",
        (PIECE // HEAD,),
        [whole((1, context))] + [rows] * 8 + [column] * 2,
        [pl.BlockSpec((HEAD, GROUP), lambda h, pos: (h, 0))] + [column] * 3,
        [struct((PIECE, GROUP))] + [struct((GROUP, PIECE))] * 3,
        [pltpu.VMEM((HEAD, context), F32)] * 2,
        30 * GROUP * PIECE * context,
        16 * GROUP * PIECE,
        pos,
        bias,
        *queries,
        *grads,
        keys,
        values,
    )


GATHERED = ((0, 0), (1, 0), (3, 0), (2, 0), (2, 1))


def output_grad_kernel(pos, *refs):
    left, right, outs, held = refs[:5], refs[5], refs[6:10], refs[10]
    for ref, (e, part) in zip(left, GATHERED):
        rows = ref.shape[0]
        row = pl.multiple_of(shifted(pos[Z], -e) * PIECE + part * rows, rows)
        product = dot(ref[...], right[...]).astype(BF16)
        for p in range(PLANES):
            held[p, pl.ds(row, rows), :] = product[:, p * 128 : (p + 1) * 128]
    for d in range(4):
        outs[d][...] = held[pl.ds(shifted(pos[Y], d) * 2, 2)]


def query_grad_kernel(pos, *refs):
    left, right, out = refs[0], refs[1:6], refs[6]
    for e, ref in enumerate(right[:3]):
        col = pl.multiple_of(shifted(pos[Z], -GATHERED[e][0]) * PIECE, PIECE)
        out[:, pl.ds(col, PIECE)] = dot(left[...], ref[...]).astype(BF16)
    col = pl.multiple_of(shifted(pos[Z], -2) * PIECE, PIECE)
    far = jnp.concatenate([right[3][...], right[4][...]], axis=0)
    out[:, pl.ds(col, PIECE)] = dot(left[...], far).astype(BF16)


def weight_terms(name, kernel, pos, args, out, count, scratch):
    return call(
        kernel,
        name,
        (1,),
        [whole(a.shape) for a in args],
        [whole(out)] * count,
        [struct(out)] * count,
        scratch,
        2 * GROUP * BLOCK * BLOCK,
        6 * BLOCK * BLOCK,
        pos,
        *args,
    )


def output_kernel(pos, *refs):
    rows, w_ref, give, keep, weights, sems = refs[:5], *refs[5:]
    copies = weight_copies(pos, w_ref, weights, sems, (1, 3, 0, 2), True)
    for n in range(4):
        copies[n].wait()
        product = jnp.zeros((TOK, BLOCK), F32)
        for ref, (e, part) in zip(rows, GATHERED):
            size = ref.shape[0]
            row = pl.multiple_of(shifted(pos[Z], -e) * PIECE + part * size, size)
            product = product + dot(ref[...], weights[n, pl.ds(row, size), :], ((0,), (0,)))
        if n < 2:
            give[n] = product.astype(BF16)
        else:
            keep[n - 2] = product


def output_terms(pos, every_out, weight):
    return call(
        output_kernel,
        "output_terms",
        (1,),
        [pl.BlockSpec((a.shape[0], TOK), lambda n, pos: (0, pos[Z])) for a in every_out] + [HBM],
        [whole((2, TOK, BLOCK))] * 2,
        [struct((2, TOK, BLOCK)), struct((2, TOK, BLOCK), F32)],
        [pltpu.VMEM((4, BLOCK, BLOCK), BF16), pltpu.SemaphoreType.DMA((4,))],
        2 * TOK * 4 * BLOCK * BLOCK,
        2 * 4 * BLOCK * BLOCK,
        pos,
        *every_out,
        weight,
    )


def context_bias(lengths, slot_passage):
    slot_lengths = jnp.sum(
        jnp.where(slot_passage[:, None] == jnp.arange(4)[None, :], lengths[None, :], 0), axis=1
    )
    position = jnp.arange(TOK, dtype=jnp.int32)
    valid = position[None, :] < slot_lengths[:, None]
    return jnp.where(valid, 0.0, -jnp.inf).astype(F32).reshape(1, 4 * TOK)


def on_device(
    decoder_states,
    query_weight,
    output_weight,
    context_keys,
    context_values,
    lengths,
    slot_passage,
    output_cotangent,
):
    pos = jnp.stack([lax.axis_index(name) for name, _ in AXES]).astype(jnp.int32)

    def to_layer(x, d):
        return lax.ppermute(x, "z", [(i, (i + d) % 4) for i in range(4)]) if d else x

    def swap(x, axis):
        return lax.ppermute(x, axis, SWAP)

    def after(x, *others):
        return lax.optimization_barrier((x, *others))[0]

    def near(name, local, weight, transposed, *others):
        blocks = (local, swap(local, "core"))
        return blocks, near_project(name, pos, after(blocks, *others), weight, transposed)

    def far(name, blocks, over_x, weight, transposed, first, *extra):
        blocks = blocks + (over_x, swap(over_x, "core"))
        rows, parts = far_project(name, pos, blocks, weight, transposed, first, *extra)
        return [to_layer(x, d) for d, x in enumerate(rows)], parts

    own = jnp.stack([context_keys, context_values]).reshape(2, 8, 16, PIECE).transpose(2, 0, 1, 3)
    own = jnp.broadcast_to(own[:, None], (16, PLANES, 2, 8, PIECE)).reshape(128, 2, 8, PIECE)
    context = lax.all_to_all(own, HEADS + SEQ, 0, 0, tiled=True)
    keys = context[:, 0].reshape(4 * TOK, PIECE)
    values = context[:, 1].reshape(4 * TOK, PIECE)
    bias = context_bias(lengths, slot_passage)

    states_x, cotangent_x = swap(decoder_states, "xh"), swap(output_cotangent, "xh")
    states, first_queries = near("queries_near", decoder_states, query_weight, False)
    cotangent, first_grad = near("heads_grad_near", output_cotangent, output_weight, True, keys)
    states_x, cotangent_x = after((states_x, cotangent_x), first_queries, first_grad)

    def ring_ends(x):
        return to_layer(x, 1), to_layer(x, 3)

    def ring(x, left, right):
        half = x.shape[0] // 2
        return x, left, right, to_layer(left[:half], 1), to_layer(right[half:], 3)

    queries, state_parts = far(
        "queries", states, states_x, query_weight, False, after(first_queries, keys)
    )
    heads_grad, parts = far(
        "heads_grad", cotangent, cotangent_x, output_weight, True, first_grad, state_parts
    )
    column_parts = lax.all_to_all(after(parts, *heads_grad), "z", 0, 0, tiled=True)

    turned_out, query_grad, key_terms, value_terms = attention(
        pos, bias, queries, heads_grad, keys, values
    )
    left, right = ring_ends(turned_out)
    every_out = ring(turned_out, left, right)
    query_grad, key_terms, value_terms = after((query_grad, key_terms, value_terms), left, right)
    left, right = ring_ends(query_grad)
    every_query_grad = ring(query_grad, left, right)

    column_parts = after(column_parts, turned_out)
    other_parts = swap(column_parts, "core")
    group_cotangent = assemble("group_cotangent", pos, column_parts, other_parts, 1, False)
    group_states = assemble("group_states", pos, column_parts, other_parts, 0, True)

    def along_y(x, d):
        return lax.ppermute(x, "y", [(i, (i + d) % 4) for i in range(4)]) if d else x

    terms = weight_terms(
        "output_weight_terms",
        output_grad_kernel,
        pos,
        (*after(every_out, left, right), group_cotangent),
        (2, BLOCK, 128),
        4,
        [pltpu.VMEM((PLANES, BLOCK, 128), BF16)],
    )
    every_out = after(every_out, terms)
    terms = after(terms, every_query_grad)
    total = sum(along_y(x, d).astype(F32) for d, x in enumerate(terms))
    kept, given = (lax.dynamic_index_in_dim(total, i, 0, False) for i in (pos[XL], 1 - pos[XL]))
    output_weight_grad = kept + swap(given.astype(BF16), "xl").astype(F32)

    give, keep = output_terms(pos, every_out, output_weight)
    pair = keep + swap(give, "core").astype(F32)
    attended = (pair[0] + swap(pair[1].astype(BF16), "xh").astype(F32)).astype(BF16)

    terms = jnp.stack([key_terms.reshape(128, 8, PIECE), value_terms.reshape(128, 8, PIECE)], 1)
    moved = lax.all_to_all(terms, HEADS + SEQ, 0, 0, tiled=True)
    owned = jnp.sum(moved.reshape(16, PLANES, 2, 8, PIECE).astype(F32), axis=1)
    owned = owned.transpose(1, 2, 0, 3).reshape(2, 8, 16 * PIECE)

    (terms,) = weight_terms(
        "query_weight_terms", query_grad_kernel, pos, (group_states, *after(every_query_grad, moved)), (BLOCK, BLOCK), 1, []
    )
    terms = after(terms, pair)
    terms = lax.all_to_all(terms.reshape(PLANES, 128, BLOCK), ("y", "xl"), 0, 0, tiled=True)
    query_weight_grad = jnp.sum(terms.astype(F32), axis=0)
    return attended, query_weight_grad, output_weight_grad, owned[0], owned[1]


def solution(mesh):
    devices = mesh.devices.reshape([size for _, size in AXES])
    split = Mesh(devices, [name for name, _ in AXES])
    return jax.shard_map(
        on_device,
        mesh=split,
        in_specs=(
            P(SEQ, HEADS),
            P(None, HEADS),
            P(HEADS, None),
            P(HEADS + SEQ, None),
            P(HEADS + SEQ, None),
            P(),
            P(),
            P(SEQ, HEADS),
        ),
        out_specs=(
            P(SEQ, HEADS),
            P(SEQ, HEADS),
            P(HEADS, SEQ),
            P(HEADS + SEQ, None),
            P(HEADS + SEQ, None),
        ),
        check_vma=False,
    )
```

```python
import math

import jax
import jax.numpy as jnp
from jax import lax
from jax.experimental import pallas as pl
from jax.experimental.pallas import tpu as pltpu
from jax.sharding import Mesh
from jax.sharding import PartitionSpec as P

HEAD = 128
SCALE = 1.0 / math.sqrt(HEAD)
LOG2E = math.log2(math.e)
F32 = jnp.float32
BF16 = jnp.bfloat16
AXES = (("xh", 2), ("core", 2), ("z", 4), ("y", 4), ("xl", 2))
HEADS = ("xh", "core")
SEQ = ("z", "y", "xl")
XH, CORE, Z, Y, XL = range(5)
SWAP = [(0, 1), (1, 0)]
VMEM = 56 * 1024 * 1024
TOK = 256
PIECE = 256
GROUP = 4 * TOK
BLOCK = 1024
PLANES = 8


def dot(a, b, contract=((1,), (0,))):
    return lax.dot_general(a, b, (contract, ((), ())), preferred_element_type=F32)


def shifted(index, by, size=4):
    return lax.rem(index + by + size, size)


def head_block(step, pos):
    return lax.rem(pos[XH] + step // 2, 2) * 2 + lax.rem(pos[CORE] + step % 2, 2)


def struct(shape, dtype=BF16):
    return jax.ShapeDtypeStruct(shape, dtype)


def whole(shape):
    return pl.BlockSpec(shape, lambda *_: (0,) * len(shape))


def call(kernel, name, grid, in_specs, out_specs, out_shape, scratch, flops, moved, pos, *args):
    return pl.pallas_call(
        kernel,
        grid_spec=pltpu.PrefetchScalarGridSpec(
            num_scalar_prefetch=1,
            grid=grid,
            in_specs=in_specs,
            out_specs=out_specs,
            scratch_shapes=scratch,
        ),
        out_shape=out_shape,
        compiler_params=pltpu.CompilerParams(vmem_limit_bytes=VMEM),
        cost_estimate=pl.CostEstimate(flops=flops, bytes_accessed=moved, transcendentals=0),
        name=name,
    )(pos, *args)


HBM = pl.BlockSpec(memory_space=pltpu.HBM)


def moved_in(pairs, sems):
    copies = [pltpu.make_async_copy(source, target, sems.at[i]) for i, (source, target) in enumerate(pairs)]
    for copy in copies:
        copy.start()
    return copies


def weight_block(w_ref, step, pos, by_columns):
    part = pl.ds(pl.multiple_of(head_block(step, pos) * BLOCK, BLOCK), BLOCK)
    return w_ref.at[:, part] if by_columns else w_ref.at[part, :]


def project_kernel(first, pos, *refs):
    before, refs = (None, refs) if first == 0 else (refs[0], refs[1:])
    sources, (wq, wo, out, blocks, weights, known, block_sems, weight_sems, known_sems) = refs[:4], refs[4:]
    pairs = [
        (weight_block(w, first + i, pos, w is wo), weights.at[2 * n + i])
        for n, w in enumerate((wq, wo))
        for i in range(2)
    ]
    moves = moved_in([(x, blocks.at[i]) for i, x in enumerate(sources)], block_sems)
    weight_moves = moved_in(pairs, weight_sems)
    if before is not None:
        moves += moved_in([(before, known)], known_sems)
    for move in moves:
        move.wait()
    for n in range(2):
        contract = ((1,), (1,)) if n else ((1,), (0,))
        weight_moves[2 * n].wait()
        total = dot(blocks[2 * n], weights[2 * n], contract)
        if before is not None:
            total = total + known[n]
        weight_moves[2 * n + 1].wait()
        total = total + dot(blocks[2 * n + 1], weights[2 * n + 1], contract)
        if before is None:
            out[n] = total
        else:
            for layer in range(4):
                out[layer, n] = total[:, layer * PIECE : (layer + 1) * PIECE].astype(BF16)


def project(name, pos, blocks, query_weight, output_weight, before=None):
    shape, dtype = ((2, TOK, BLOCK), F32) if before is None else ((4, 2, TOK, PIECE), BF16)
    args = (*(() if before is None else (before,)), *blocks, query_weight, output_weight)
    return call(
        lambda *refs: project_kernel(0 if before is None else 2, *refs),
        name,
        (1,),
        [HBM] * len(args),
        whole(shape),
        struct(shape, dtype),
        [
            pltpu.VMEM((4, TOK, BLOCK), BF16),
            pltpu.VMEM((4, BLOCK, BLOCK), BF16),
            pltpu.VMEM((2, TOK, BLOCK), F32),
            pltpu.SemaphoreType.DMA((4,)),
            pltpu.SemaphoreType.DMA((4,)),
            pltpu.SemaphoreType.DMA((1,)),
        ],
        8 * TOK * BLOCK * BLOCK,
        8 * BLOCK * BLOCK,
        pos,
        *args,
    )


def assemble_kernel(pos, p0, p1, p2, p3, turned, straight):
    for i, piece in enumerate((p0, p1, p2, p3)):
        token = pl.multiple_of(head_block(i, pos) * TOK, TOK)
        turned[:, pl.ds(token, TOK)] = piece[0].T
        straight[pl.ds(token, TOK), :] = piece[1]


def assemble(pos, pieces):
    return call(
        assemble_kernel,
        "column_blocks",
        (1,),
        [whole((2, TOK, BLOCK))] * 4,
        [whole((BLOCK, GROUP)), whole((GROUP, BLOCK))],
        [struct((BLOCK, GROUP)), struct((GROUP, BLOCK))],
        [],
        0,
        8 * BLOCK * GROUP,
        pos,
        *pieces,
    )


def attention_kernel(pos, bias, rows, k_ref, v_ref, out, dk_ref, dv_ref, dk_sum, dv_sum):
    k, v = k_ref[...], v_ref[...]
    for layer in range(4):
        q = rows[layer, 0]
        scores = dot(q, k, ((1,), (1,))) + bias[...]
        top = jnp.max(scores, axis=1, keepdims=True)
        weights = jnp.exp2((scores - top) * (SCALE * LOG2E))
        share = 1.0 / jnp.sum(weights, axis=1, keepdims=True)
        low = weights.astype(BF16)
        heads_out = (dot(low, v) * share).astype(BF16)
        token = slice(layer * TOK, (layer + 1) * TOK)
        out[0, :, token] = heads_out.T
        g = (rows[layer, 1].astype(F32) * (share * SCALE)).astype(BF16)
        delta = jnp.sum(g.astype(F32) * heads_out.astype(F32), axis=1, keepdims=True)
        score_grad = (low.astype(F32) * (dot(g, v, ((1,), (1,))) - delta)).astype(BF16)
        out[1, :, token] = dot(score_grad, k).astype(BF16).T
        dk_term, dv_term = dot(q, score_grad, ((0,), (0,))), dot(g, low, ((0,), (0,)))
        dk_sum[...] = dk_term if layer == 0 else dk_sum[...] + dk_term
        dv_sum[...] = dv_term if layer == 0 else dv_sum[...] + dv_term
    dk_ref[...] = dk_sum[...].T.astype(BF16)
    dv_ref[...] = (dv_sum[...] * (1.0 / SCALE)).T.astype(BF16)


def attention(pos, bias, rows, keys, values):
    column = pl.BlockSpec((GROUP, HEAD), lambda h, pos: (0, h))
    context = keys.shape[0]
    return call(
        attention_kernel,
        "attention",
        (PIECE // HEAD,),
        [whole((1, context)), pl.BlockSpec((4, 2, TOK, HEAD), lambda h, pos: (0, 0, 0, h))] + [column] * 2,
        [pl.BlockSpec((2, HEAD, GROUP), lambda h, pos: (0, h, 0))] + [column] * 2,
        [struct((2, PIECE, GROUP))] + [struct((GROUP, PIECE))] * 2,
        [pltpu.VMEM((HEAD, context), F32)] * 2,
        30 * GROUP * PIECE * context,
        16 * GROUP * PIECE,
        pos,
        bias,
        rows,
        keys,
        values,
    )


GATHERED = ((0, 0), (1, 0), (3, 0), (2, 0), (2, 1))


def output_grad_kernel(pos, *refs):
    left, right, outs, held = refs[:5], refs[5], refs[6:10], refs[10]
    for ref, (e, part) in zip(left, GATHERED):
        rows = ref.shape[1]
        row = pl.multiple_of(shifted(pos[Z], -e) * PIECE + part * rows, rows)
        product = dot(ref[0], right[...]).astype(BF16)
        for p in range(PLANES):
            held[p, pl.ds(row, rows), :] = product[:, p * 128 : (p + 1) * 128]
    for d in range(4):
        outs[d][...] = held[pl.ds(shifted(pos[Y], d) * 2, 2)]


def query_grad_kernel(pos, *refs):
    right, left, out = refs[:5], refs[5], refs[6]
    for ref, (e, part) in zip(right, GATHERED):
        cols = ref.shape[1]
        col = pl.multiple_of(shifted(pos[Z], -e) * PIECE + part * cols, cols)
        out[:, pl.ds(col, cols)] = dot(left[...], ref[0], ((1,), (1,))).astype(BF16)


def weight_terms(name, kernel, pos, which, gathered, block, out, count, scratch):
    return call(
        kernel,
        name,
        (1,),
        [pl.BlockSpec((1, *a.shape[1:]), lambda i, pos: (which, 0, 0)) for a in gathered] + [whole(block.shape)],
        [whole(out)] * count,
        [struct(out)] * count,
        scratch,
        2 * GROUP * BLOCK * BLOCK,
        6 * BLOCK * BLOCK,
        pos,
        *gathered,
        block,
    )


def output_kernel(pos, *refs):
    rows, w_ref, give, keep, weights, sems = refs[:5], *refs[5:]
    order = (1, 3, 0, 2)
    moves = moved_in([(weight_block(w_ref, i, pos, True), weights.at[n]) for n, i in enumerate(order)], sems)
    for n in range(4):
        moves[n].wait()
        product = jnp.zeros((TOK, BLOCK), F32)
        for ref, (e, part) in zip(rows, GATHERED):
            size = ref.shape[1]
            row = pl.multiple_of(shifted(pos[Z], -e) * PIECE + part * size, size)
            product = product + dot(ref[0], weights[n, pl.ds(row, size), :], ((0,), (0,)))
        if n < 2:
            give[n] = product.astype(BF16)
        else:
            keep[n - 2] = product


def output_terms(pos, gathered, weight):
    return call(
        output_kernel,
        "output_terms",
        (1,),
        [pl.BlockSpec((1, a.shape[1], TOK), lambda n, pos: (0, 0, pos[Z])) for a in gathered] + [HBM],
        [whole((2, TOK, BLOCK))] * 2,
        [struct((2, TOK, BLOCK)), struct((2, TOK, BLOCK), F32)],
        [pltpu.VMEM((4, BLOCK, BLOCK), BF16), pltpu.SemaphoreType.DMA((4,))],
        2 * TOK * 4 * BLOCK * BLOCK,
        2 * 4 * BLOCK * BLOCK,
        pos,
        *gathered,
        weight,
    )


def context_bias(lengths, slot_passage):
    slot_lengths = jnp.sum(
        jnp.where(slot_passage[:, None] == jnp.arange(4)[None, :], lengths[None, :], 0), axis=1
    )
    position = jnp.arange(TOK, dtype=jnp.int32)
    valid = position[None, :] < slot_lengths[:, None]
    return jnp.where(valid, 0.0, -jnp.inf).astype(F32).reshape(1, 4 * TOK)


def on_device(
    decoder_states,
    query_weight,
    output_weight,
    context_keys,
    context_values,
    lengths,
    slot_passage,
    output_cotangent,
):
    pos = jnp.stack([lax.axis_index(name) for name, _ in AXES]).astype(jnp.int32)

    def shift(x, axis, d):
        return lax.ppermute(x, axis, [(i, (i + d) % 4) for i in range(4)])

    def swap(x, axis):
        return lax.ppermute(x, axis, SWAP)

    def after(x, *others):
        return lax.optimization_barrier((x, *others))[0]

    far_states, far_cotangent = swap(decoder_states, "xh"), swap(output_cotangent, "xh")
    near = (decoder_states, swap(decoder_states, "core"), output_cotangent, swap(output_cotangent, "core"))
    products = project("project_near", pos, near, query_weight, output_weight)

    own = jnp.stack([context_keys, context_values]).reshape(2, 8, 16, PIECE).transpose(2, 0, 1, 3)
    own = jnp.broadcast_to(own[:, None], (16, PLANES, 2, 8, PIECE)).reshape(128, 2, 8, PIECE)
    context = lax.all_to_all(after(own, near), HEADS + SEQ, 0, 0, tiled=True)
    keys = context[:, 0].reshape(4 * TOK, PIECE)
    values = context[:, 1].reshape(4 * TOK, PIECE)
    bias = context_bias(lengths, slot_passage)

    far_states, far_cotangent = after((far_states, far_cotangent), products, keys)
    far = (far_states, swap(far_states, "core"), far_cotangent, swap(far_cotangent, "core"))
    rows = project("project_far", pos, far, query_weight, output_weight, products)
    rows = lax.all_to_all(rows, "z", 0, 0, tiled=True)

    pairs = [(h * 4 + z, z * 4 + h) for h in range(4) for z in range(4)]
    both = jnp.stack(after((decoder_states, output_cotangent), far_states, far_cotangent))
    piece = lax.ppermute(both, HEADS + ("z",), pairs)
    piece = after(piece, rows)
    over_x = swap(piece, "xh")

    gathered, key_terms, value_terms = attention(pos, bias, rows, keys, values)
    left, right = shift(gathered, "z", 1), shift(gathered, "z", 3)
    half = PIECE // 2
    every = (gathered, left, right, shift(left[:, :half], "z", 1), shift(right[:, half:], "z", 3))

    piece, over_x = after((piece, over_x), gathered)
    group_states, group_cotangent = assemble(
        pos, (piece, swap(piece, "core"), over_x, swap(over_x, "core"))
    )

    terms = jnp.stack([key_terms.reshape(128, 8, PIECE), value_terms.reshape(128, 8, PIECE)], 1)
    moved = lax.all_to_all(after(terms, group_states), HEADS + SEQ, 0, 0, tiled=True)
    owned = jnp.sum(moved.reshape(16, PLANES, 2, 8, PIECE).astype(F32), axis=1)
    owned = owned.transpose(1, 2, 0, 3).reshape(2, 8, 16 * PIECE)

    terms = weight_terms(
        "output_weight_terms",
        output_grad_kernel,
        pos,
        0,
        every,
        group_cotangent,
        (2, BLOCK, 128),
        4,
        [pltpu.VMEM((PLANES, BLOCK, 128), BF16)],
    )
    total = terms[0].astype(F32)
    for d in range(1, 4):
        total = total + shift(terms[d], "y", d).astype(F32)
    kept, given = (lax.dynamic_index_in_dim(total, i, 0, False) for i in (pos[XL], 1 - pos[XL]))
    output_weight_grad = kept + swap(given.astype(BF16), "xl").astype(F32)

    (query_terms,) = weight_terms(
        "query_weight_terms",
        query_grad_kernel,
        pos,
        1,
        after(every, moved, terms),
        group_states,
        (BLOCK, BLOCK),
        1,
        [],
    )
    query_sums = lax.all_to_all(query_terms.reshape(PLANES, 128, BLOCK), ("y", "xl"), 0, 0, tiled=True)
    query_weight_grad = jnp.sum(query_sums.astype(F32), axis=0)

    give, keep = output_terms(pos, after(every, query_terms), output_weight)
    pair = keep + swap(give, "core").astype(F32)
    attended = (pair[0] + swap(pair[1].astype(BF16), "xh").astype(F32)).astype(BF16)
    return attended, query_weight_grad, output_weight_grad, owned[0], owned[1]


def solution(mesh):
    devices = mesh.devices.reshape([size for _, size in AXES])
    split = Mesh(devices, [name for name, _ in AXES])
    return jax.shard_map(
        on_device,
        mesh=split,
        in_specs=(
            P(SEQ, HEADS),
            P(None, HEADS),
            P(HEADS, None),
            P(HEADS + SEQ, None),
            P(HEADS + SEQ, None),
            P(),
            P(),
            P(SEQ, HEADS),
        ),
        out_specs=(
            P(SEQ, HEADS),
            P(SEQ, HEADS),
            P(HEADS, SEQ),
            P(HEADS + SEQ, None),
            P(HEADS + SEQ, None),
        ),
        check_vma=False,
    )
```

```python
import math

import jax
import jax.numpy as jnp
from jax import lax
from jax.experimental import pallas as pl
from jax.experimental.pallas import tpu as pltpu
from jax.sharding import Mesh
from jax.sharding import PartitionSpec as P

HEAD = 128
SCALE = 1.0 / math.sqrt(HEAD)
LOG2E = math.log2(math.e)
F32 = jnp.float32
BF16 = jnp.bfloat16
AXES = (("xh", 2), ("core", 2), ("z", 4), ("y", 4), ("xl", 2))
HEADS = ("xh", "core")
SEQ = ("z", "y", "xl")
XH, CORE, Z, Y, XL = range(5)
SWAP = [(0, 1), (1, 0)]
VMEM = 56 * 1024 * 1024
TOK = 256
PIECE = 256
GROUP = 4 * TOK
BLOCK = 1024
PLANES = 8


def dot(a, b, contract=((1,), (0,))):
    return lax.dot_general(a, b, (contract, ((), ())), preferred_element_type=F32)


def shifted(index, by, size=4):
    return lax.rem(index + by + size, size)


def head_block(step, pos):
    return lax.rem(pos[XH] + step // 2, 2) * 2 + lax.rem(pos[CORE] + step % 2, 2)


def struct(shape, dtype=BF16):
    return jax.ShapeDtypeStruct(shape, dtype)


def whole(shape):
    return pl.BlockSpec(shape, lambda *_: (0,) * len(shape))


def call(kernel, name, grid, in_specs, out_specs, out_shape, scratch, flops, moved, pos, *args):
    return pl.pallas_call(
        kernel,
        grid_spec=pltpu.PrefetchScalarGridSpec(
            num_scalar_prefetch=1,
            grid=grid,
            in_specs=in_specs,
            out_specs=out_specs,
            scratch_shapes=scratch,
        ),
        out_shape=out_shape,
        compiler_params=pltpu.CompilerParams(vmem_limit_bytes=VMEM),
        cost_estimate=pl.CostEstimate(flops=flops, bytes_accessed=moved, transcendentals=0),
        name=name,
    )(pos, *args)


HBM = pl.BlockSpec(memory_space=pltpu.HBM)


def moved_in(pairs, sems):
    copies = [pltpu.make_async_copy(source, target, sems.at[i]) for i, (source, target) in enumerate(pairs)]
    for copy in copies:
        copy.start()
    return copies


def weight_block(w_ref, step, pos, by_columns):
    part = pl.ds(pl.multiple_of(head_block(step, pos) * BLOCK, BLOCK), BLOCK)
    return w_ref.at[:, part] if by_columns else w_ref.at[part, :]


def project_kernel(first, pos, *refs):
    before, refs = (None, refs) if first == 0 else (refs[0], refs[1:])
    sources, (wq, wo, out, blocks, weights, known, block_sems, weight_sems, known_sems) = refs[:4], refs[4:]
    pairs = [
        (weight_block(w, first + i, pos, w is wo), weights.at[2 * n + i])
        for n, w in enumerate((wq, wo))
        for i in range(2)
    ]
    moves = moved_in([(x, blocks.at[i]) for i, x in enumerate(sources)], block_sems)
    weight_moves = moved_in(pairs, weight_sems)
    if before is not None:
        moves += moved_in([(before, known)], known_sems)
    for move in moves:
        move.wait()
    for n in range(2):
        contract = ((1,), (1,)) if n else ((1,), (0,))
        weight_moves[2 * n].wait()
        total = dot(blocks[2 * n], weights[2 * n], contract)
        if before is not None:
            total = total + known[n]
        weight_moves[2 * n + 1].wait()
        total = total + dot(blocks[2 * n + 1], weights[2 * n + 1], contract)
        if before is None:
            out[n] = total
        else:
            for layer in range(4):
                out[layer, n] = total[:, layer * PIECE : (layer + 1) * PIECE].astype(BF16)


def project(name, pos, blocks, query_weight, output_weight, before=None):
    shape, dtype = ((2, TOK, BLOCK), F32) if before is None else ((4, 2, TOK, PIECE), BF16)
    args = (*(() if before is None else (before,)), *blocks, query_weight, output_weight)
    return call(
        lambda *refs: project_kernel(0 if before is None else 2, *refs),
        name,
        (1,),
        [HBM] * len(args),
        whole(shape),
        struct(shape, dtype),
        [
            pltpu.VMEM((4, TOK, BLOCK), BF16),
            pltpu.VMEM((4, BLOCK, BLOCK), BF16),
            pltpu.VMEM((2, TOK, BLOCK), F32),
            pltpu.SemaphoreType.DMA((4,)),
            pltpu.SemaphoreType.DMA((4,)),
            pltpu.SemaphoreType.DMA((1,)),
        ],
        8 * TOK * BLOCK * BLOCK,
        8 * BLOCK * BLOCK,
        pos,
        *args,
    )


def assemble_kernel(pos, p0, p1, p2, p3, turned, straight):
    for i, piece in enumerate((p0, p1, p2, p3)):
        col = pl.multiple_of(head_block(i, pos) * PIECE, PIECE)
        for d in range(4):
            token = pl.multiple_of(shifted(pos[Y], -d) * TOK, TOK)
            turned[pl.ds(col, PIECE), pl.ds(token, TOK)] = piece[d, 0].T
            straight[pl.ds(token, TOK), pl.ds(col, PIECE)] = piece[d, 1]


def assemble(pos, pieces):
    return call(
        assemble_kernel,
        "column_blocks",
        (1,),
        [whole((4, 2, TOK, PIECE))] * 4,
        [whole((BLOCK, GROUP)), whole((GROUP, BLOCK))],
        [struct((BLOCK, GROUP)), struct((GROUP, BLOCK))],
        [],
        0,
        8 * BLOCK * GROUP,
        pos,
        *pieces,
    )


def attention_kernel(pos, bias, rows, k_ref, v_ref, out, dk_ref, dv_ref, dk_sum, dv_sum):
    k, v = k_ref[...], v_ref[...]
    for layer in range(4):
        q = rows[layer, 0]
        scores = dot(q, k, ((1,), (1,))) + bias[...]
        top = jnp.max(scores, axis=1, keepdims=True)
        weights = jnp.exp2((scores - top) * (SCALE * LOG2E))
        share = 1.0 / jnp.sum(weights, axis=1, keepdims=True)
        low = weights.astype(BF16)
        heads_out = (dot(low, v) * share).astype(BF16)
        token = slice(layer * TOK, (layer + 1) * TOK)
        out[0, :, token] = heads_out.T
        g = (rows[layer, 1].astype(F32) * (share * SCALE)).astype(BF16)
        delta = jnp.sum(g.astype(F32) * heads_out.astype(F32), axis=1, keepdims=True)
        score_grad = (low.astype(F32) * (dot(g, v, ((1,), (1,))) - delta)).astype(BF16)
        out[1, :, token] = dot(score_grad, k).astype(BF16).T
        dk_term, dv_term = dot(q, score_grad, ((0,), (0,))), dot(g, low, ((0,), (0,)))
        dk_sum[...] = dk_term if layer == 0 else dk_sum[...] + dk_term
        dv_sum[...] = dv_term if layer == 0 else dv_sum[...] + dv_term
    dk_ref[...] = dk_sum[...].T.astype(BF16)
    dv_ref[...] = (dv_sum[...] * (1.0 / SCALE)).T.astype(BF16)


def attention(pos, bias, rows, keys, values):
    column = pl.BlockSpec((GROUP, HEAD), lambda h, pos: (0, h))
    context = keys.shape[0]
    return call(
        attention_kernel,
        "attention",
        (PIECE // HEAD,),
        [whole((1, context)), pl.BlockSpec((4, 2, TOK, HEAD), lambda h, pos: (0, 0, 0, h))] + [column] * 2,
        [pl.BlockSpec((2, HEAD, GROUP), lambda h, pos: (0, h, 0))] + [column] * 2,
        [struct((2, PIECE, GROUP))] + [struct((GROUP, PIECE))] * 2,
        [pltpu.VMEM((HEAD, context), F32)] * 2,
        30 * GROUP * PIECE * context,
        16 * GROUP * PIECE,
        pos,
        bias,
        rows,
        keys,
        values,
    )


GATHERED = ((0, 0), (1, 0), (3, 0), (2, 0), (2, 1))


def output_grad_kernel(pos, *refs):
    left, right, out = refs[:5], refs[5], refs[6]
    for ref, (e, part) in zip(left, GATHERED):
        rows = ref.shape[1]
        row = pl.multiple_of(shifted(pos[Y], -e) * PIECE + part * rows, rows)
        product = dot(ref[0], right[...]).astype(BF16)
        for p in range(PLANES):
            out[p, pl.ds(row, rows), :] = product[:, p * 128 : (p + 1) * 128]


def query_grad_kernel(pos, *refs):
    right, left, out = refs[:5], refs[5], refs[6]
    for ref, (e, part) in zip(right, GATHERED):
        cols = ref.shape[1]
        col = pl.multiple_of(shifted(pos[Y], -e) * PIECE + part * cols, cols)
        out[:, pl.ds(col, cols)] = dot(left[...], ref[0], ((1,), (1,))).astype(BF16)


def weight_terms(name, kernel, pos, which, gathered, block, out):
    return call(
        kernel,
        name,
        (1,),
        [pl.BlockSpec((1, *a.shape[1:]), lambda i, pos: (which, 0, 0)) for a in gathered] + [whole(block.shape)],
        whole(out),
        struct(out),
        [],
        2 * GROUP * BLOCK * BLOCK,
        6 * BLOCK * BLOCK,
        pos,
        *gathered,
        block,
    )


def output_kernel(pos, *refs):
    rows, w_ref, give, keep, weights, sems = refs[:5], *refs[5:]
    order = (1, 3, 0, 2)
    moves = moved_in([(weight_block(w_ref, i, pos, True), weights.at[n]) for n, i in enumerate(order)], sems)
    for n in range(4):
        moves[n].wait()
        product = jnp.zeros((TOK, BLOCK), F32)
        for ref, (e, part) in zip(rows, GATHERED):
            size = ref.shape[1]
            row = pl.multiple_of(shifted(pos[Y], -e) * PIECE + part * size, size)
            product = product + dot(ref[0], weights[n, pl.ds(row, size), :], ((0,), (0,)))
        if n < 2:
            give[n] = product.astype(BF16)
        else:
            keep[n - 2] = product


def output_terms(pos, gathered, weight):
    return call(
        output_kernel,
        "output_terms",
        (1,),
        [pl.BlockSpec((1, a.shape[1], TOK), lambda n, pos: (0, 0, pos[Y])) for a in gathered] + [HBM],
        [whole((2, TOK, BLOCK))] * 2,
        [struct((2, TOK, BLOCK)), struct((2, TOK, BLOCK), F32)],
        [pltpu.VMEM((4, BLOCK, BLOCK), BF16), pltpu.SemaphoreType.DMA((4,))],
        2 * TOK * 4 * BLOCK * BLOCK,
        2 * 4 * BLOCK * BLOCK,
        pos,
        *gathered,
        weight,
    )


def context_bias(lengths, slot_passage):
    slot_lengths = jnp.sum(
        jnp.where(slot_passage[:, None] == jnp.arange(4)[None, :], lengths[None, :], 0), axis=1
    )
    position = jnp.arange(TOK, dtype=jnp.int32)
    valid = position[None, :] < slot_lengths[:, None]
    return jnp.where(valid, 0.0, -jnp.inf).astype(F32).reshape(1, 4 * TOK)


def on_device(
    decoder_states,
    query_weight,
    output_weight,
    context_keys,
    context_values,
    lengths,
    slot_passage,
    output_cotangent,
):
    pos = jnp.stack([lax.axis_index(name) for name, _ in AXES]).astype(jnp.int32)

    def shift(x, axis, d):
        return lax.ppermute(x, axis, [(i, (i + d) % 4) for i in range(4)])

    def swap(x, axis):
        return lax.ppermute(x, axis, SWAP)

    def after(x, *others):
        return lax.optimization_barrier((x, *others))[0]

    far_states, far_cotangent = swap(decoder_states, "xh"), swap(output_cotangent, "xh")
    near = (decoder_states, swap(decoder_states, "core"), output_cotangent, swap(output_cotangent, "core"))
    products = project("project_near", pos, near, query_weight, output_weight)

    both = jnp.stack([decoder_states, output_cotangent]).reshape(2, TOK, 4, PIECE)
    quarters = [lax.dynamic_index_in_dim(both, shifted(pos[Y], d), 2, False) for d in range(4)]
    quarters = [shift(x, "y", d) if d else x for d, x in enumerate(quarters)]

    own = jnp.stack([context_keys, context_values]).reshape(2, 8, 4, 4, PIECE).transpose(2, 3, 0, 1, 4)
    own = jnp.broadcast_to(own[:, None, :, None], (4, 4, 4, 2, 2, 8, PIECE)).reshape(128, 2, 8, PIECE)
    context = lax.all_to_all(after(own, products), HEADS + SEQ, 0, 0, tiled=True)
    keys = context[:, 0].reshape(4 * TOK, PIECE)
    values = context[:, 1].reshape(4 * TOK, PIECE)
    bias = context_bias(lengths, slot_passage)

    far_states, far_cotangent = after((far_states, far_cotangent), products)
    far = (far_states, swap(far_states, "core"), far_cotangent, swap(far_cotangent, "core"))
    rows = project("project_far", pos, far, query_weight, output_weight, after(products, keys, quarters))
    rows = lax.all_to_all(rows, "y", 0, 0, tiled=True)

    piece = jnp.stack(after(quarters, rows))
    over_x = swap(piece, "xh")

    gathered, key_terms, value_terms = attention(pos, bias, rows, keys, values)
    left, right = shift(gathered, "y", 1), shift(gathered, "y", 3)
    half = PIECE // 2
    every = (gathered, left, right, shift(left[:, :half], "y", 1), shift(right[:, half:], "y", 3))

    terms = jnp.stack([key_terms.reshape(128, 8, PIECE), value_terms.reshape(128, 8, PIECE)], 1)
    moved = lax.all_to_all(terms, HEADS + SEQ, 0, 0, tiled=True)
    owned = jnp.sum(moved.reshape(4, 4, 4, 2, 2, 8, PIECE).astype(F32), axis=(1, 3))
    owned = owned.transpose(2, 3, 0, 1, 4).reshape(2, 8, 16 * PIECE)

    piece, over_x = after((piece, over_x), left, right, moved)
    group_states, group_cotangent = assemble(
        pos, (piece, swap(piece, "core"), over_x, swap(over_x, "core"))
    )

    def plane_sum(parts):
        return jnp.sum(lax.all_to_all(parts, ("z", "xl"), 0, 0, tiled=True).astype(F32), axis=0)

    output_parts = weight_terms(
        "output_weight_terms", output_grad_kernel, pos, 0, every, group_cotangent, (PLANES, BLOCK, 128)
    )
    output_weight_grad = plane_sum(output_parts)
    query_parts = weight_terms(
        "query_weight_terms", query_grad_kernel, pos, 1, after(every, output_parts), group_states, (BLOCK, BLOCK)
    )
    query_weight_grad = plane_sum(after(query_parts, output_weight_grad).reshape(PLANES, 128, BLOCK))

    give, keep = output_terms(pos, after(every, query_parts), output_weight)
    pair = keep + swap(give, "core").astype(F32)
    attended = (pair[0] + swap(pair[1].astype(BF16), "xh").astype(F32)).astype(BF16)
    return attended, query_weight_grad, output_weight_grad, owned[0], owned[1]


def solution(mesh):
    devices = mesh.devices.reshape([size for _, size in AXES])
    split = Mesh(devices, [name for name, _ in AXES])
    return jax.shard_map(
        on_device,
        mesh=split,
        in_specs=(
            P(SEQ, HEADS),
            P(None, HEADS),
            P(HEADS, None),
            P(HEADS + SEQ, None),
            P(HEADS + SEQ, None),
            P(),
            P(),
            P(SEQ, HEADS),
        ),
        out_specs=(
            P(SEQ, HEADS),
            P(SEQ, HEADS),
            P(HEADS, SEQ),
            P(HEADS + SEQ, None),
            P(HEADS + SEQ, None),
        ),
        check_vma=False,
    )
```

```python
import math

import jax
import jax.numpy as jnp
from jax import lax
from jax.experimental import pallas as pl
from jax.experimental.pallas import tpu as pltpu
from jax.sharding import Mesh
from jax.sharding import PartitionSpec as P

HEAD = 128
SCALE = 1.0 / math.sqrt(HEAD)
LOG2E = math.log2(math.e)
F32 = jnp.float32
BF16 = jnp.bfloat16
AXES = (("xh", 2), ("core", 2), ("z", 4), ("y", 4), ("xl", 2))
HEADS = ("xh", "core")
SEQ = ("z", "y", "xl")
XH, CORE, Z, Y, XL = range(5)
SWAP = [(0, 1), (1, 0)]
VMEM = 56 * 1024 * 1024
TOK = 256
PIECE = 256
GROUP = 4 * TOK
BLOCK = 1024
PLANES = 8


def dot(a, b, contract=((1,), (0,))):
    return lax.dot_general(a, b, (contract, ((), ())), preferred_element_type=F32)


def shifted(index, by, size=4):
    return lax.rem(index + by + size, size)


def head_block(step, pos):
    return lax.rem(pos[XH] + step // 2, 2) * 2 + lax.rem(pos[CORE] + step % 2, 2)


def struct(shape, dtype=BF16):
    return jax.ShapeDtypeStruct(shape, dtype)


def whole(shape):
    return pl.BlockSpec(shape, lambda *_: (0,) * len(shape))


def call(kernel, name, grid, in_specs, out_specs, out_shape, scratch, flops, moved, pos, *args):
    return pl.pallas_call(
        kernel,
        grid_spec=pltpu.PrefetchScalarGridSpec(
            num_scalar_prefetch=1,
            grid=grid,
            in_specs=in_specs,
            out_specs=out_specs,
            scratch_shapes=scratch,
        ),
        out_shape=out_shape,
        compiler_params=pltpu.CompilerParams(vmem_limit_bytes=VMEM),
        cost_estimate=pl.CostEstimate(flops=flops, bytes_accessed=moved, transcendentals=0),
        name=name,
    )(pos, *args)


HBM = pl.BlockSpec(memory_space=pltpu.HBM)


def moved_in(pairs, sems):
    copies = [pltpu.make_async_copy(source, target, sems.at[i]) for i, (source, target) in enumerate(pairs)]
    for copy in copies:
        copy.start()
    return copies


def weight_block(w_ref, step, pos, by_columns):
    part = pl.ds(pl.multiple_of(head_block(step, pos) * BLOCK, BLOCK), BLOCK)
    return w_ref.at[:, part] if by_columns else w_ref.at[part, :]


def project_kernel(first, pos, *refs):
    before, refs = (None, refs) if first == 0 else (refs[0], refs[1:])
    sources, (wq, wo, out, blocks, weights, known, block_sems, weight_sems, known_sems) = refs[:4], refs[4:]
    pairs = [
        (weight_block(w, first + i, pos, w is wo), weights.at[2 * n + i])
        for n, w in enumerate((wq, wo))
        for i in range(2)
    ]
    moves = moved_in([(x, blocks.at[i]) for i, x in enumerate(sources)], block_sems)
    weight_moves = moved_in(pairs, weight_sems)
    if before is not None:
        moves += moved_in([(before, known)], known_sems)
    for move in moves:
        move.wait()
    for n in range(2):
        contract = ((1,), (1,)) if n else ((1,), (0,))
        weight_moves[2 * n].wait()
        total = dot(blocks[2 * n], weights[2 * n], contract)
        if before is not None:
            total = total + known[n]
        weight_moves[2 * n + 1].wait()
        total = total + dot(blocks[2 * n + 1], weights[2 * n + 1], contract)
        if before is None:
            out[n] = total
        else:
            for layer in range(4):
                out[layer, n] = total[:, layer * PIECE : (layer + 1) * PIECE].astype(BF16)


def project(name, pos, blocks, query_weight, output_weight, before=None):
    shape, dtype = ((2, TOK, BLOCK), F32) if before is None else ((4, 2, TOK, PIECE), BF16)
    args = (*(() if before is None else (before,)), *blocks, query_weight, output_weight)
    return call(
        lambda *refs: project_kernel(0 if before is None else 2, *refs),
        name,
        (1,),
        [HBM] * len(args),
        whole(shape),
        struct(shape, dtype),
        [
            pltpu.VMEM((4, TOK, BLOCK), BF16),
            pltpu.VMEM((4, BLOCK, BLOCK), BF16),
            pltpu.VMEM((2, TOK, BLOCK), F32),
            pltpu.SemaphoreType.DMA((4,)),
            pltpu.SemaphoreType.DMA((4,)),
            pltpu.SemaphoreType.DMA((1,)),
        ],
        8 * TOK * BLOCK * BLOCK,
        8 * BLOCK * BLOCK,
        pos,
        *args,
    )


def assemble_kernel(pos, p0, p1, p2, p3, turned, straight):
    for i, piece in enumerate((p0, p1, p2, p3)):
        col = pl.multiple_of(head_block(i, pos) * PIECE, PIECE)
        for d in range(4):
            token = pl.multiple_of(shifted(pos[Y], -d) * TOK, TOK)
            turned[pl.ds(col, PIECE), pl.ds(token, TOK)] = piece[d, 0].T
            straight[pl.ds(token, TOK), pl.ds(col, PIECE)] = piece[d, 1]


def assemble(pos, pieces):
    return call(
        assemble_kernel,
        "column_blocks",
        (1,),
        [whole((4, 2, TOK, PIECE))] * 4,
        [whole((BLOCK, GROUP)), whole((GROUP, BLOCK))],
        [struct((BLOCK, GROUP)), struct((GROUP, BLOCK))],
        [],
        0,
        8 * BLOCK * GROUP,
        pos,
        *pieces,
    )


def attention_kernel(pos, bias, rows, k_ref, v_ref, out, dk_ref, dv_ref, dk_sum, dv_sum):
    k, v = k_ref[...], v_ref[...]
    for layer in range(4):
        q = rows[layer, 0]
        scores = dot(q, k, ((1,), (1,))) + bias[...]
        top = jnp.max(scores, axis=1, keepdims=True)
        weights = jnp.exp2((scores - top) * (SCALE * LOG2E))
        share = 1.0 / jnp.sum(weights, axis=1, keepdims=True)
        low = weights.astype(BF16)
        heads_out = (dot(low, v) * share).astype(BF16)
        token = slice(layer * TOK, (layer + 1) * TOK)
        out[0, :, token] = heads_out.T
        g = (rows[layer, 1].astype(F32) * (share * SCALE)).astype(BF16)
        delta = jnp.sum(g.astype(F32) * heads_out.astype(F32), axis=1, keepdims=True)
        score_grad = (low.astype(F32) * (dot(g, v, ((1,), (1,))) - delta)).astype(BF16)
        out[1, :, token] = dot(score_grad, k).astype(BF16).T
        dk_term, dv_term = dot(q, score_grad, ((0,), (0,))), dot(g, low, ((0,), (0,)))
        dk_sum[...] = dk_term if layer == 0 else dk_sum[...] + dk_term
        dv_sum[...] = dv_term if layer == 0 else dv_sum[...] + dv_term
    dk_ref[...] = dk_sum[...].T.astype(BF16)
    dv_ref[...] = (dv_sum[...] * (1.0 / SCALE)).T.astype(BF16)


def attention(pos, bias, rows, keys, values):
    column = pl.BlockSpec((GROUP, HEAD), lambda h, pos: (0, h))
    context = keys.shape[0]
    return call(
        attention_kernel,
        "attention",
        (PIECE // HEAD,),
        [whole((1, context)), pl.BlockSpec((4, 2, TOK, HEAD), lambda h, pos: (0, 0, 0, h))] + [column] * 2,
        [pl.BlockSpec((2, HEAD, GROUP), lambda h, pos: (0, h, 0))] + [column] * 2,
        [struct((2, PIECE, GROUP))] + [struct((GROUP, PIECE))] * 2,
        [pltpu.VMEM((HEAD, context), F32)] * 2,
        30 * GROUP * PIECE * context,
        16 * GROUP * PIECE,
        pos,
        bias,
        rows,
        keys,
        values,
    )


GATHERED = ((0, 0), (1, 0), (3, 0), (2, 0), (2, 1))


def output_grad_kernel(pos, *refs):
    left, right, out = refs[:5], refs[5], refs[6]
    for ref, (e, part) in zip(left, GATHERED):
        rows = ref.shape[1]
        row = pl.multiple_of(shifted(pos[Y], -e) * PIECE + part * rows, rows)
        product = dot(ref[0], right[...]).astype(BF16)
        for p in range(PLANES):
            out[p, pl.ds(row, rows), :] = product[:, p * 128 : (p + 1) * 128]


def query_grad_kernel(pos, *refs):
    right, left, out = refs[:5], refs[5], refs[6]
    for ref, (e, part) in zip(right, GATHERED):
        cols = ref.shape[1]
        col = pl.multiple_of(shifted(pos[Y], -e) * PIECE + part * cols, cols)
        out[:, pl.ds(col, cols)] = dot(left[...], ref[0], ((1,), (1,))).astype(BF16)


def weight_terms(name, kernel, pos, which, gathered, block, out):
    return call(
        kernel,
        name,
        (1,),
        [pl.BlockSpec((1, *a.shape[1:]), lambda i, pos: (which, 0, 0)) for a in gathered] + [whole(block.shape)],
        whole(out),
        struct(out),
        [],
        2 * GROUP * BLOCK * BLOCK,
        6 * BLOCK * BLOCK,
        pos,
        *gathered,
        block,
    )


def output_kernel(pos, *refs):
    rows, w_ref, give, keep, weights, sems = refs[:5], *refs[5:]
    order = (1, 3, 0, 2)
    moves = moved_in([(weight_block(w_ref, i, pos, True), weights.at[n]) for n, i in enumerate(order)], sems)
    for n in range(4):
        moves[n].wait()
        product = jnp.zeros((TOK, BLOCK), F32)
        for ref, (e, part) in zip(rows, GATHERED):
            size = ref.shape[1]
            row = pl.multiple_of(shifted(pos[Y], -e) * PIECE + part * size, size)
            product = product + dot(ref[0], weights[n, pl.ds(row, size), :], ((0,), (0,)))
        if n < 2:
            give[n] = product.astype(BF16)
        else:
            keep[n - 2] = product


def output_terms(pos, gathered, weight):
    return call(
        output_kernel,
        "output_terms",
        (1,),
        [pl.BlockSpec((1, a.shape[1], TOK), lambda n, pos: (0, 0, pos[Y])) for a in gathered] + [HBM],
        [whole((2, TOK, BLOCK))] * 2,
        [struct((2, TOK, BLOCK)), struct((2, TOK, BLOCK), F32)],
        [pltpu.VMEM((4, BLOCK, BLOCK), BF16), pltpu.SemaphoreType.DMA((4,))],
        2 * TOK * 4 * BLOCK * BLOCK,
        2 * 4 * BLOCK * BLOCK,
        pos,
        *gathered,
        weight,
    )


def context_bias(lengths, slot_passage):
    slot_lengths = jnp.sum(
        jnp.where(slot_passage[:, None] == jnp.arange(4)[None, :], lengths[None, :], 0), axis=1
    )
    position = jnp.arange(TOK, dtype=jnp.int32)
    valid = position[None, :] < slot_lengths[:, None]
    return jnp.where(valid, 0.0, -jnp.inf).astype(F32).reshape(1, 4 * TOK)


def on_device(
    decoder_states,
    query_weight,
    output_weight,
    context_keys,
    context_values,
    lengths,
    slot_passage,
    output_cotangent,
):
    pos = jnp.stack([lax.axis_index(name) for name, _ in AXES]).astype(jnp.int32)

    def shift(x, axis, d):
        return lax.ppermute(x, axis, [(i, (i + d) % 4) for i in range(4)])

    def swap(x, axis):
        return lax.ppermute(x, axis, SWAP)

    def after(x, *others):
        return lax.optimization_barrier((x, *others))[0]

    far_states, far_cotangent = swap(decoder_states, "xh"), swap(output_cotangent, "xh")
    near = (decoder_states, swap(decoder_states, "core"), output_cotangent, swap(output_cotangent, "core"))
    products = project("project_near", pos, near, query_weight, output_weight)

    both = jnp.stack([decoder_states, output_cotangent]).reshape(2, TOK, 4, PIECE)
    quarters = [lax.dynamic_index_in_dim(both, shifted(pos[Y], d), 2, False) for d in range(4)]
    quarters = [shift(x, "y", d) if d else x for d, x in enumerate(quarters)]

    own = jnp.stack([context_keys, context_values]).reshape(2, 8, 4, 4, PIECE).transpose(2, 3, 0, 1, 4)
    own = jnp.broadcast_to(own[:, None, :, None], (4, 4, 4, 2, 2, 8, PIECE)).reshape(128, 2, 8, PIECE)
    context = lax.all_to_all(after(own, products, far_states, far_cotangent, quarters), HEADS + SEQ, 0, 0, tiled=True)
    keys = context[:, 0].reshape(4 * TOK, PIECE)
    values = context[:, 1].reshape(4 * TOK, PIECE)
    bias = context_bias(lengths, slot_passage)

    far = (far_states, swap(far_states, "core"), far_cotangent, swap(far_cotangent, "core"))
    rows = project("project_far", pos, far, query_weight, output_weight, products)
    rows = lax.all_to_all(rows, "y", 0, 0, tiled=True)

    piece = jnp.stack(after(quarters, rows))
    over_x = swap(piece, "xh")

    gathered, key_terms, value_terms = attention(pos, bias, rows, keys, values)
    left, right = shift(gathered, "y", 1), shift(gathered, "y", 3)
    half = PIECE // 2
    every = (gathered, left, right, shift(left[:, :half], "y", 1), shift(right[:, half:], "y", 3))

    terms = jnp.stack([key_terms.reshape(128, 8, PIECE), value_terms.reshape(128, 8, PIECE)], 1)
    moved = lax.all_to_all(terms, HEADS + SEQ, 0, 0, tiled=True)
    owned = jnp.sum(moved.reshape(4, 4, 4, 2, 2, 8, PIECE).astype(F32), axis=(1, 3))
    owned = owned.transpose(2, 3, 0, 1, 4).reshape(2, 8, 16 * PIECE)

    piece, over_x = after((piece, over_x), left, right)
    group_states, group_cotangent = assemble(
        pos, (piece, swap(piece, "core"), over_x, swap(over_x, "core"))
    )

    def plane_sum(parts):
        return jnp.sum(lax.all_to_all(parts, ("z", "xl"), 0, 0, tiled=True).astype(F32), axis=0)

    output_parts = weight_terms(
        "output_weight_terms", output_grad_kernel, pos, 0, after(every, moved), group_cotangent, (PLANES, BLOCK, 128)
    )
    output_weight_grad = plane_sum(output_parts)
    query_parts = weight_terms(
        "query_weight_terms", query_grad_kernel, pos, 1, after(every, output_parts), group_states, (BLOCK, BLOCK)
    )
    give, keep = output_terms(pos, after(every, query_parts), output_weight)
    pair = keep + swap(give, "core").astype(F32)
    pair_far = pair[1].astype(BF16)
    attended = (pair[0] + swap(pair_far, "xh").astype(F32)).astype(BF16)
    query_parts = after(query_parts, output_weight_grad, pair_far)
    query_weight_grad = plane_sum(query_parts.reshape(PLANES, 128, BLOCK))
    return attended, query_weight_grad, output_weight_grad, owned[0], owned[1]


def solution(mesh):
    devices = mesh.devices.reshape([size for _, size in AXES])
    split = Mesh(devices, [name for name, _ in AXES])
    return jax.shard_map(
        on_device,
        mesh=split,
        in_specs=(
            P(SEQ, HEADS),
            P(None, HEADS),
            P(HEADS, None),
            P(HEADS + SEQ, None),
            P(HEADS + SEQ, None),
            P(),
            P(),
            P(SEQ, HEADS),
        ),
        out_specs=(
            P(SEQ, HEADS),
            P(SEQ, HEADS),
            P(HEADS, SEQ),
            P(HEADS + SEQ, None),
            P(HEADS + SEQ, None),
        ),
        check_vma=False,
    )
```

```python
import math

import jax
import jax.numpy as jnp
from jax import lax
from jax.experimental import pallas as pl
from jax.experimental.pallas import tpu as pltpu
from jax.sharding import Mesh
from jax.sharding import PartitionSpec as P

HEAD = 128
SCALE = 1.0 / math.sqrt(HEAD)
LOG2E = math.log2(math.e)
F32 = jnp.float32
BF16 = jnp.bfloat16
AXES = (("xh", 2), ("core", 2), ("z", 4), ("y", 4), ("xl", 2))
HEADS = ("xh", "core")
SEQ = ("z", "y", "xl")
XH, CORE, Z, Y, XL = range(5)
SWAP = [(0, 1), (1, 0)]
VMEM = 56 * 1024 * 1024
TOK = 256
PIECE = 256
GROUP = 4 * TOK
BLOCK = 1024
PLANES = 8


def dot(a, b, contract=((1,), (0,))):
    return lax.dot_general(a, b, (contract, ((), ())), preferred_element_type=F32)


def shifted(index, by, size=4):
    return lax.rem(index + by + size, size)


def head_block(step, pos):
    return lax.rem(pos[XH] + step // 2, 2) * 2 + lax.rem(pos[CORE] + step % 2, 2)


def struct(shape, dtype=BF16):
    return jax.ShapeDtypeStruct(shape, dtype)


def whole(shape):
    return pl.BlockSpec(shape, lambda *_: (0,) * len(shape))


def call(kernel, name, grid, in_specs, out_specs, out_shape, scratch, flops, moved, pos, *args):
    return pl.pallas_call(
        kernel,
        grid_spec=pltpu.PrefetchScalarGridSpec(
            num_scalar_prefetch=1,
            grid=grid,
            in_specs=in_specs,
            out_specs=out_specs,
            scratch_shapes=scratch,
        ),
        out_shape=out_shape,
        compiler_params=pltpu.CompilerParams(vmem_limit_bytes=VMEM),
        cost_estimate=pl.CostEstimate(flops=flops, bytes_accessed=moved, transcendentals=0),
        name=name,
    )(pos, *args)


HBM = pl.BlockSpec(memory_space=pltpu.HBM)


def moved_in(pairs, sems):
    copies = [pltpu.make_async_copy(source, target, sems.at[i]) for i, (source, target) in enumerate(pairs)]
    for copy in copies:
        copy.start()
    return copies


def weight_block(w_ref, step, pos, by_columns):
    part = pl.ds(pl.multiple_of(head_block(step, pos) * BLOCK, BLOCK), BLOCK)
    return w_ref.at[:, part] if by_columns else w_ref.at[part, :]


def project_kernel(first, pos, *refs):
    before, refs = (None, refs) if first == 0 else (refs[0], refs[1:])
    sources, (wq, wo, out, blocks, weights, known, block_sems, weight_sems, known_sems) = refs[:4], refs[4:]
    pairs = [
        (weight_block(w, first + i, pos, w is wo), weights.at[2 * n + i])
        for n, w in enumerate((wq, wo))
        for i in range(2)
    ]
    moves = moved_in([(x, blocks.at[i]) for i, x in enumerate(sources)], block_sems)
    weight_moves = moved_in(pairs, weight_sems)
    if before is not None:
        moves += moved_in([(before, known)], known_sems)
    for move in moves:
        move.wait()
    for n in range(2):
        contract = ((1,), (1,)) if n else ((1,), (0,))
        weight_moves[2 * n].wait()
        total = dot(blocks[2 * n], weights[2 * n], contract)
        if before is not None:
            total = total + known[n]
        weight_moves[2 * n + 1].wait()
        total = total + dot(blocks[2 * n + 1], weights[2 * n + 1], contract)
        if before is None:
            out[n] = total
        else:
            for layer in range(4):
                out[layer, n] = total[:, layer * PIECE : (layer + 1) * PIECE].astype(BF16)


def project(name, pos, blocks, query_weight, output_weight, before=None):
    shape, dtype = ((2, TOK, BLOCK), F32) if before is None else ((4, 2, TOK, PIECE), BF16)
    args = (*(() if before is None else (before,)), *blocks, query_weight, output_weight)
    return call(
        lambda *refs: project_kernel(0 if before is None else 2, *refs),
        name,
        (1,),
        [HBM] * len(args),
        whole(shape),
        struct(shape, dtype),
        [
            pltpu.VMEM((4, TOK, BLOCK), BF16),
            pltpu.VMEM((4, BLOCK, BLOCK), BF16),
            pltpu.VMEM((2, TOK, BLOCK), F32),
            pltpu.SemaphoreType.DMA((4,)),
            pltpu.SemaphoreType.DMA((4,)),
            pltpu.SemaphoreType.DMA((1,)),
        ],
        8 * TOK * BLOCK * BLOCK,
        8 * BLOCK * BLOCK,
        pos,
        *args,
    )


def assemble_kernel(pos, p0, p1, p2, p3, turned, straight):
    for i, piece in enumerate((p0, p1, p2, p3)):
        col = pl.multiple_of(head_block(i, pos) * PIECE, PIECE)
        for d in range(4):
            token = pl.multiple_of(shifted(pos[Y], -d) * TOK, TOK)
            turned[pl.ds(col, PIECE), pl.ds(token, TOK)] = piece[d, 0].T
            straight[pl.ds(token, TOK), pl.ds(col, PIECE)] = piece[d, 1]


def assemble(pos, pieces):
    return call(
        assemble_kernel,
        "column_blocks",
        (1,),
        [whole((4, 2, TOK, PIECE))] * 4,
        [whole((BLOCK, GROUP)), whole((GROUP, BLOCK))],
        [struct((BLOCK, GROUP)), struct((GROUP, BLOCK))],
        [],
        0,
        8 * BLOCK * GROUP,
        pos,
        *pieces,
    )


def attention_kernel(pos, bias, rows, k_ref, v_ref, out, dk_ref, dv_ref, dk_sum, dv_sum):
    k, v = k_ref[...], v_ref[...]
    for layer in range(4):
        q = rows[layer, 0]
        scores = dot(q, k, ((1,), (1,))) + bias[...]
        top = jnp.max(scores, axis=1, keepdims=True)
        weights = jnp.exp2((scores - top) * (SCALE * LOG2E))
        share = 1.0 / jnp.sum(weights, axis=1, keepdims=True)
        low = weights.astype(BF16)
        heads_out = (dot(low, v) * share).astype(BF16)
        token = slice(layer * TOK, (layer + 1) * TOK)
        out[0, :, token] = heads_out.T
        g = (rows[layer, 1].astype(F32) * (share * SCALE)).astype(BF16)
        delta = jnp.sum(g.astype(F32) * heads_out.astype(F32), axis=1, keepdims=True)
        score_grad = (low.astype(F32) * (dot(g, v, ((1,), (1,))) - delta)).astype(BF16)
        out[1, :, token] = dot(score_grad, k).astype(BF16).T
        dk_term, dv_term = dot(q, score_grad, ((0,), (0,))), dot(g, low, ((0,), (0,)))
        dk_sum[...] = dk_term if layer == 0 else dk_sum[...] + dk_term
        dv_sum[...] = dv_term if layer == 0 else dv_sum[...] + dv_term
    dk_ref[...] = dk_sum[...].T.astype(BF16)
    dv_ref[...] = (dv_sum[...] * (1.0 / SCALE)).T.astype(BF16)


def attention(pos, bias, rows, keys, values):
    column = pl.BlockSpec((GROUP, HEAD), lambda h, pos: (0, h))
    context = keys.shape[0]
    return call(
        attention_kernel,
        "attention",
        (PIECE // HEAD,),
        [whole((1, context)), pl.BlockSpec((4, 2, TOK, HEAD), lambda h, pos: (0, 0, 0, h))] + [column] * 2,
        [pl.BlockSpec((2, HEAD, GROUP), lambda h, pos: (0, h, 0))] + [column] * 2,
        [struct((2, PIECE, GROUP))] + [struct((GROUP, PIECE))] * 2,
        [pltpu.VMEM((HEAD, context), F32)] * 2,
        30 * GROUP * PIECE * context,
        16 * GROUP * PIECE,
        pos,
        bias,
        rows,
        keys,
        values,
    )


GATHERED = ((0, 0), (1, 0), (3, 0), (2, 0), (2, 1))


def output_grad_kernel(pos, *refs):
    left, right, out = refs[:5], refs[5], refs[6]
    for ref, (e, part) in zip(left, GATHERED):
        rows = ref.shape[1]
        row = pl.multiple_of(shifted(pos[Y], -e) * PIECE + part * rows, rows)
        product = dot(ref[0], right[...]).astype(BF16)
        for p in range(PLANES):
            out[p, pl.ds(row, rows), :] = product[:, p * 128 : (p + 1) * 128]


def query_grad_kernel(pos, *refs):
    right, left, out = refs[:5], refs[5], refs[6]
    for ref, (e, part) in zip(right, GATHERED):
        cols = ref.shape[1]
        col = pl.multiple_of(shifted(pos[Y], -e) * PIECE + part * cols, cols)
        out[:, pl.ds(col, cols)] = dot(left[...], ref[0], ((1,), (1,))).astype(BF16)


def one_of(pair, which):
    return pl.BlockSpec((1, *pair.shape[1:]), lambda i, pos: (which if pair.shape[0] == 2 else 0, 0, 0))


def weight_terms(name, kernel, pos, which, gathered, block, out):
    return call(
        kernel,
        name,
        (1,),
        [one_of(a, which) for a in gathered] + [whole(block.shape)],
        whole(out),
        struct(out),
        [],
        2 * GROUP * BLOCK * BLOCK,
        6 * BLOCK * BLOCK,
        pos,
        *gathered,
        block,
    )


def output_kernel(pos, *refs):
    rows, w_ref, give, keep, weights, sems = refs[:5], *refs[5:]
    order = (1, 3, 0, 2)
    moves = moved_in([(weight_block(w_ref, i, pos, True), weights.at[n]) for n, i in enumerate(order)], sems)
    for n in range(4):
        moves[n].wait()
        product = jnp.zeros((TOK, BLOCK), F32)
        for ref, (e, part) in zip(rows, GATHERED):
            size = ref.shape[1]
            row = pl.multiple_of(shifted(pos[Y], -e) * PIECE + part * size, size)
            product = product + dot(ref[0], weights[n, pl.ds(row, size), :], ((0,), (0,)))
        if n < 2:
            give[n] = product.astype(BF16)
        else:
            keep[n - 2] = product


def output_terms(pos, gathered, weight):
    return call(
        output_kernel,
        "output_terms",
        (1,),
        [pl.BlockSpec((1, a.shape[1], TOK), lambda n, pos: (0, 0, pos[Y])) for a in gathered] + [HBM],
        [whole((2, TOK, BLOCK))] * 2,
        [struct((2, TOK, BLOCK)), struct((2, TOK, BLOCK), F32)],
        [pltpu.VMEM((4, BLOCK, BLOCK), BF16), pltpu.SemaphoreType.DMA((4,))],
        2 * TOK * 4 * BLOCK * BLOCK,
        2 * 4 * BLOCK * BLOCK,
        pos,
        *gathered,
        weight,
    )


def context_bias(lengths, slot_passage):
    slot_lengths = jnp.sum(
        jnp.where(slot_passage[:, None] == jnp.arange(4)[None, :], lengths[None, :], 0), axis=1
    )
    position = jnp.arange(TOK, dtype=jnp.int32)
    valid = position[None, :] < slot_lengths[:, None]
    return jnp.where(valid, 0.0, -jnp.inf).astype(F32).reshape(1, 4 * TOK)


def on_device(
    decoder_states,
    query_weight,
    output_weight,
    context_keys,
    context_values,
    lengths,
    slot_passage,
    output_cotangent,
):
    pos = jnp.stack([lax.axis_index(name) for name, _ in AXES]).astype(jnp.int32)

    def shift(x, axis, d):
        return lax.ppermute(x, axis, [(i, (i + d) % 4) for i in range(4)])

    def swap(x, axis):
        return lax.ppermute(x, axis, SWAP)

    def after(x, *others):
        return lax.optimization_barrier((x, *others))[0]

    far_states, far_cotangent = swap(decoder_states, "xh"), swap(output_cotangent, "xh")
    near = (decoder_states, swap(decoder_states, "core"), output_cotangent, swap(output_cotangent, "core"))
    products = project("project_near", pos, near, query_weight, output_weight)

    both = jnp.stack([decoder_states, output_cotangent]).reshape(2, TOK, 4, PIECE)
    quarters = [lax.dynamic_index_in_dim(both, shifted(pos[Y], d), 2, False) for d in range(4)]
    quarters = [shift(x, "y", d) if d else x for d, x in enumerate(quarters)]

    own = jnp.stack([context_keys, context_values]).reshape(2, 8, 4, 4, PIECE).transpose(2, 3, 0, 1, 4)
    own = jnp.broadcast_to(own[:, None, :, None], (4, 4, 4, 2, 2, 8, PIECE)).reshape(128, 2, 8, PIECE)
    context = lax.all_to_all(after(own, products, far_states, far_cotangent, quarters), HEADS + SEQ, 0, 0, tiled=True)
    keys = context[:, 0].reshape(4 * TOK, PIECE)
    values = context[:, 1].reshape(4 * TOK, PIECE)
    bias = context_bias(lengths, slot_passage)

    far = (far_states, swap(far_states, "core"), far_cotangent, swap(far_cotangent, "core"))
    rows = project("project_far", pos, far, query_weight, output_weight, products)
    rows = lax.all_to_all(rows, "y", 0, 0, tiled=True)

    piece = jnp.stack(after(quarters, rows))
    over_x = swap(piece, "xh")

    gathered, key_terms, value_terms = attention(pos, bias, rows, keys, values)
    left, right = shift(gathered, "y", 1), shift(gathered, "y", 3)
    half = PIECE // 2

    def far_halves(i):
        return shift(left[i : i + 1, :half], "y", 1), shift(right[i : i + 1, half:], "y", 3)

    every_out = (gathered, left, right, *far_halves(0))
    every_grad = (gathered, left, right, *far_halves(1))

    terms = jnp.stack([key_terms.reshape(128, 8, PIECE), value_terms.reshape(128, 8, PIECE)], 1)
    moved = lax.all_to_all(terms, HEADS + SEQ, 0, 0, tiled=True)
    owned = jnp.sum(moved.reshape(4, 4, 4, 2, 2, 8, PIECE).astype(F32), axis=(1, 3))
    owned = owned.transpose(2, 3, 0, 1, 4).reshape(2, 8, 16 * PIECE)

    piece, over_x = after((piece, over_x), left, right)
    group_states, group_cotangent = assemble(
        pos, after((piece, swap(piece, "core"), over_x, swap(over_x, "core")), moved)
    )

    give, keep = output_terms(pos, every_out, output_weight)
    pair = keep + swap(give, "core").astype(F32)
    attended = (pair[0] + swap(pair[1].astype(BF16), "xh").astype(F32)).astype(BF16)

    def plane_sum(parts):
        return jnp.sum(lax.all_to_all(parts, ("z", "xl"), 0, 0, tiled=True).astype(F32), axis=0)

    output_parts = weight_terms(
        "output_weight_terms",
        output_grad_kernel,
        pos,
        0,
        after(every_out, give),
        group_cotangent,
        (PLANES, BLOCK, 128),
    )
    output_weight_grad = plane_sum(output_parts)
    query_parts = weight_terms(
        "query_weight_terms",
        query_grad_kernel,
        pos,
        1,
        after(every_grad, output_parts, attended),
        group_states,
        (BLOCK, BLOCK),
    )
    query_parts = after(query_parts, output_weight_grad)
    query_weight_grad = plane_sum(query_parts.reshape(PLANES, 128, BLOCK))
    return attended, query_weight_grad, output_weight_grad, owned[0], owned[1]


def solution(mesh):
    devices = mesh.devices.reshape([size for _, size in AXES])
    split = Mesh(devices, [name for name, _ in AXES])
    return jax.shard_map(
        on_device,
        mesh=split,
        in_specs=(
            P(SEQ, HEADS),
            P(None, HEADS),
            P(HEADS, None),
            P(HEADS + SEQ, None),
            P(HEADS + SEQ, None),
            P(),
            P(),
            P(SEQ, HEADS),
        ),
        out_specs=(
            P(SEQ, HEADS),
            P(SEQ, HEADS),
            P(HEADS, SEQ),
            P(HEADS + SEQ, None),
            P(HEADS + SEQ, None),
        ),
        check_vma=False,
    )
```

```python
import math

import jax
import jax.numpy as jnp
from jax import lax
from jax.experimental import pallas as pl
from jax.experimental.pallas import tpu as pltpu
from jax.sharding import Mesh
from jax.sharding import PartitionSpec as P

HEAD = 128
SCALE = 1.0 / math.sqrt(HEAD)
LOG2E = math.log2(math.e)
F32 = jnp.float32
BF16 = jnp.bfloat16
AXES = (("xh", 2), ("core", 2), ("z", 4), ("y", 4), ("xl", 2))
HEADS = ("xh", "core")
SEQ = ("z", "y", "xl")
XH, CORE, Z, Y, XL = range(5)
SWAP = [(0, 1), (1, 0)]
VMEM = 56 * 1024 * 1024
TOK = 256
PIECE = 256
GROUP = 4 * TOK
BLOCK = 1024
PLANES = 8


def dot(a, b, contract=((1,), (0,))):
    return lax.dot_general(a, b, (contract, ((), ())), preferred_element_type=F32)


def shifted(index, by, size=4):
    return lax.rem(index + by + size, size)


def head_block(step, pos):
    return lax.rem(pos[XH] + step // 2, 2) * 2 + lax.rem(pos[CORE] + step % 2, 2)


def struct(shape, dtype=BF16):
    return jax.ShapeDtypeStruct(shape, dtype)


def whole(shape):
    return pl.BlockSpec(shape, lambda *_: (0,) * len(shape))


def call(kernel, name, grid, in_specs, out_specs, out_shape, scratch, flops, moved, pos, *args):
    return pl.pallas_call(
        kernel,
        grid_spec=pltpu.PrefetchScalarGridSpec(
            num_scalar_prefetch=1,
            grid=grid,
            in_specs=in_specs,
            out_specs=out_specs,
            scratch_shapes=scratch,
        ),
        out_shape=out_shape,
        compiler_params=pltpu.CompilerParams(vmem_limit_bytes=VMEM),
        cost_estimate=pl.CostEstimate(flops=flops, bytes_accessed=moved, transcendentals=0),
        name=name,
    )(pos, *args)


HBM = pl.BlockSpec(memory_space=pltpu.HBM)


def moved_in(pairs, sems):
    copies = [pltpu.make_async_copy(source, target, sems.at[i]) for i, (source, target) in enumerate(pairs)]
    for copy in copies:
        copy.start()
    return copies


def weight_block(w_ref, step, pos, by_columns):
    part = pl.ds(pl.multiple_of(head_block(step, pos) * BLOCK, BLOCK), BLOCK)
    return w_ref.at[:, part] if by_columns else w_ref.at[part, :]


def project_kernel(first, pos, *refs):
    before, refs = (None, refs) if first == 0 else (refs[0], refs[1:])
    sources, (wq, wo, out, blocks, weights, known, block_sems, weight_sems, known_sems) = refs[:4], refs[4:]
    pairs = [
        (weight_block(w, first + i, pos, w is wo), weights.at[2 * n + i])
        for n, w in enumerate((wq, wo))
        for i in range(2)
    ]
    moves = moved_in([(x, blocks.at[i]) for i, x in enumerate(sources)], block_sems)
    weight_moves = moved_in(pairs, weight_sems)
    if before is not None:
        moves += moved_in([(before, known)], known_sems)
    for move in moves:
        move.wait()
    for n in range(2):
        contract = ((1,), (1,)) if n else ((1,), (0,))
        weight_moves[2 * n].wait()
        total = dot(blocks[2 * n], weights[2 * n], contract)
        if before is not None:
            total = total + known[n]
        weight_moves[2 * n + 1].wait()
        total = total + dot(blocks[2 * n + 1], weights[2 * n + 1], contract)
        if before is None:
            out[n] = total
        else:
            for layer in range(4):
                out[layer, n] = total[:, layer * PIECE : (layer + 1) * PIECE].astype(BF16)


def project(name, pos, blocks, query_weight, output_weight, before=None):
    shape, dtype = ((2, TOK, BLOCK), F32) if before is None else ((4, 2, TOK, PIECE), BF16)
    args = (*(() if before is None else (before,)), *blocks, query_weight, output_weight)
    return call(
        lambda *refs: project_kernel(0 if before is None else 2, *refs),
        name,
        (1,),
        [HBM] * len(args),
        whole(shape),
        struct(shape, dtype),
        [
            pltpu.VMEM((4, TOK, BLOCK), BF16),
            pltpu.VMEM((4, BLOCK, BLOCK), BF16),
            pltpu.VMEM((2, TOK, BLOCK), F32),
            pltpu.SemaphoreType.DMA((4,)),
            pltpu.SemaphoreType.DMA((4,)),
            pltpu.SemaphoreType.DMA((1,)),
        ],
        8 * TOK * BLOCK * BLOCK,
        8 * BLOCK * BLOCK,
        pos,
        *args,
    )


def assemble_kernel(pos, p0, p1, p2, p3, turned, straight):
    for i, piece in enumerate((p0, p1, p2, p3)):
        col = pl.multiple_of(head_block(i, pos) * PIECE, PIECE)
        for d in range(4):
            token = pl.multiple_of(shifted(pos[Y], -d) * TOK, TOK)
            turned[pl.ds(col, PIECE), pl.ds(token, TOK)] = piece[d, 0].T
            straight[pl.ds(token, TOK), pl.ds(col, PIECE)] = piece[d, 1]


def assemble(pos, pieces):
    return call(
        assemble_kernel,
        "column_blocks",
        (1,),
        [whole((4, 2, TOK, PIECE))] * 4,
        [whole((BLOCK, GROUP)), whole((GROUP, BLOCK))],
        [struct((BLOCK, GROUP)), struct((GROUP, BLOCK))],
        [],
        0,
        8 * BLOCK * GROUP,
        pos,
        *pieces,
    )


def attention_kernel(pos, bias, rows, k_ref, v_ref, out, dk_ref, dv_ref, dk_sum, dv_sum):
    k, v = k_ref[...], v_ref[...]
    for layer in range(4):
        q = rows[layer, 0]
        scores = dot(q, k, ((1,), (1,))) + bias[...]
        top = jnp.max(scores, axis=1, keepdims=True)
        weights = jnp.exp2((scores - top) * (SCALE * LOG2E))
        share = 1.0 / jnp.sum(weights, axis=1, keepdims=True)
        low = weights.astype(BF16)
        heads_out = (dot(low, v) * share).astype(BF16)
        token = slice(layer * TOK, (layer + 1) * TOK)
        out[0, :, token] = heads_out.T
        g = (rows[layer, 1].astype(F32) * (share * SCALE)).astype(BF16)
        delta = jnp.sum(g.astype(F32) * heads_out.astype(F32), axis=1, keepdims=True)
        score_grad = (low.astype(F32) * (dot(g, v, ((1,), (1,))) - delta)).astype(BF16)
        out[1, :, token] = dot(score_grad, k).astype(BF16).T
        dk_term, dv_term = dot(q, score_grad, ((0,), (0,))), dot(g, low, ((0,), (0,)))
        dk_sum[...] = dk_term if layer == 0 else dk_sum[...] + dk_term
        dv_sum[...] = dv_term if layer == 0 else dv_sum[...] + dv_term
    dk_ref[...] = dk_sum[...].T.astype(BF16)
    dv_ref[...] = (dv_sum[...] * (1.0 / SCALE)).T.astype(BF16)


def attention(pos, bias, rows, keys, values):
    column = pl.BlockSpec((GROUP, HEAD), lambda h, pos: (0, h))
    context = keys.shape[0]
    return call(
        attention_kernel,
        "attention",
        (PIECE // HEAD,),
        [whole((1, context)), pl.BlockSpec((4, 2, TOK, HEAD), lambda h, pos: (0, 0, 0, h))] + [column] * 2,
        [pl.BlockSpec((2, HEAD, GROUP), lambda h, pos: (0, h, 0))] + [column] * 2,
        [struct((2, PIECE, GROUP))] + [struct((GROUP, PIECE))] * 2,
        [pltpu.VMEM((HEAD, context), F32)] * 2,
        30 * GROUP * PIECE * context,
        16 * GROUP * PIECE,
        pos,
        bias,
        rows,
        keys,
        values,
    )


GATHERED = ((0, 0), (1, 0), (3, 0), (2, 0), (2, 1))


def output_grad_kernel(pos, *refs):
    left, right, out = refs[:5], refs[5], refs[6]
    for ref, (e, part) in zip(left, GATHERED):
        rows = ref.shape[1]
        row = pl.multiple_of(shifted(pos[Y], -e) * PIECE + part * rows, rows)
        product = dot(ref[0], right[...]).astype(BF16)
        for p in range(PLANES):
            out[p, pl.ds(row, rows), :] = product[:, p * 128 : (p + 1) * 128]


def query_grad_kernel(pos, *refs):
    right, left, out = refs[:5], refs[5], refs[6]
    for ref, (e, part) in zip(right, GATHERED):
        cols = ref.shape[1]
        col = pl.multiple_of(shifted(pos[Y], -e) * PIECE + part * cols, cols)
        out[:, pl.ds(col, cols)] = dot(left[...], ref[0], ((1,), (1,))).astype(BF16)


def one_of(pair, which):
    return pl.BlockSpec((1, *pair.shape[1:]), lambda i, pos: (which if pair.shape[0] == 2 else 0, 0, 0))


def weight_terms(name, kernel, pos, which, gathered, block, out):
    return call(
        kernel,
        name,
        (1,),
        [one_of(a, which) for a in gathered] + [whole(block.shape)],
        whole(out),
        struct(out),
        [],
        2 * GROUP * BLOCK * BLOCK,
        6 * BLOCK * BLOCK,
        pos,
        *gathered,
        block,
    )


def output_kernel(pos, *refs):
    rows, w_ref, give, keep, weights, sems = refs[:5], *refs[5:]
    order = (1, 3, 0, 2)
    moves = moved_in([(weight_block(w_ref, i, pos, True), weights.at[n]) for n, i in enumerate(order)], sems)
    for n in range(4):
        moves[n].wait()
        product = jnp.zeros((TOK, BLOCK), F32)
        for ref, (e, part) in zip(rows, GATHERED):
            size = ref.shape[1]
            row = pl.multiple_of(shifted(pos[Y], -e) * PIECE + part * size, size)
            product = product + dot(ref[0], weights[n, pl.ds(row, size), :], ((0,), (0,)))
        if n < 2:
            give[n] = product.astype(BF16)
        else:
            keep[n - 2] = product


def output_terms(pos, gathered, weight):
    return call(
        output_kernel,
        "output_terms",
        (1,),
        [pl.BlockSpec((1, a.shape[1], TOK), lambda n, pos: (0, 0, pos[Y])) for a in gathered] + [HBM],
        [whole((2, TOK, BLOCK))] * 2,
        [struct((2, TOK, BLOCK)), struct((2, TOK, BLOCK), F32)],
        [pltpu.VMEM((4, BLOCK, BLOCK), BF16), pltpu.SemaphoreType.DMA((4,))],
        2 * TOK * 4 * BLOCK * BLOCK,
        2 * 4 * BLOCK * BLOCK,
        pos,
        *gathered,
        weight,
    )


def context_bias(lengths, slot_passage):
    slot_lengths = jnp.sum(
        jnp.where(slot_passage[:, None] == jnp.arange(4)[None, :], lengths[None, :], 0), axis=1
    )
    position = jnp.arange(TOK, dtype=jnp.int32)
    valid = position[None, :] < slot_lengths[:, None]
    return jnp.where(valid, 0.0, -jnp.inf).astype(F32).reshape(1, 4 * TOK)


def on_device(
    decoder_states,
    query_weight,
    output_weight,
    context_keys,
    context_values,
    lengths,
    slot_passage,
    output_cotangent,
):
    pos = jnp.stack([lax.axis_index(name) for name, _ in AXES]).astype(jnp.int32)

    def shift(x, axis, d):
        return lax.ppermute(x, axis, [(i, (i + d) % 4) for i in range(4)])

    def swap(x, axis):
        return lax.ppermute(x, axis, SWAP)

    def after(x, *others):
        return lax.optimization_barrier((x, *others))[0]

    far_states, far_cotangent = swap(decoder_states, "xh"), swap(output_cotangent, "xh")
    near = (decoder_states, swap(decoder_states, "core"), output_cotangent, swap(output_cotangent, "core"))
    products = project("project_near", pos, near, query_weight, output_weight)

    both = jnp.stack([decoder_states, output_cotangent]).reshape(2, TOK, 4, PIECE)
    quarters = [lax.dynamic_index_in_dim(both, shifted(pos[Y], d), 2, False) for d in range(4)]
    quarters = [shift(x, "y", d) if d else x for d, x in enumerate(quarters)]

    own = jnp.stack([context_keys, context_values]).reshape(2, 8, 4, 4, PIECE).transpose(2, 3, 0, 1, 4)
    own = jnp.broadcast_to(own[:, None, :, None], (4, 4, 4, 2, 2, 8, PIECE)).reshape(128, 2, 8, PIECE)
    context = lax.all_to_all(after(own, products, far_states, far_cotangent, quarters), HEADS + SEQ, 0, 0, tiled=True)
    keys = context[:, 0].reshape(4 * TOK, PIECE)
    values = context[:, 1].reshape(4 * TOK, PIECE)
    bias = context_bias(lengths, slot_passage)

    far = (far_states, swap(far_states, "core"), far_cotangent, swap(far_cotangent, "core"))
    rows = project("project_far", pos, far, query_weight, output_weight, products)
    rows = lax.all_to_all(rows, "y", 0, 0, tiled=True)

    piece = jnp.stack(after(quarters, rows))
    over_x = swap(piece, "xh")

    gathered, key_terms, value_terms = attention(pos, bias, rows, keys, values)
    left, right = shift(gathered, "y", 1), shift(gathered, "y", 3)
    half = PIECE // 2

    def far_halves(i):
        return shift(left[i : i + 1, :half], "y", 1), shift(right[i : i + 1, half:], "y", 3)

    every_out = (gathered, left, right, *far_halves(0))
    every_grad = (gathered, left, right, *far_halves(1))

    terms = jnp.stack([key_terms.reshape(128, 8, PIECE), value_terms.reshape(128, 8, PIECE)], 1)
    moved = lax.all_to_all(terms, HEADS + SEQ, 0, 0, tiled=True)
    owned = jnp.sum(moved.reshape(4, 4, 4, 2, 2, 8, PIECE).astype(F32), axis=(1, 3))
    owned = owned.transpose(2, 3, 0, 1, 4).reshape(2, 8, 16 * PIECE)

    piece, over_x = after((piece, over_x), left, right)
    group_states, group_cotangent = assemble(
        pos, after((piece, swap(piece, "core"), over_x, swap(over_x, "core")), moved)
    )

    give, keep = output_terms(pos, every_out, output_weight)
    pair = keep + swap(give, "core").astype(F32)
    attended = (pair[0] + swap(pair[1].astype(BF16), "xh").astype(F32)).astype(BF16)

    def plane_sum(parts):
        return jnp.sum(lax.all_to_all(parts, ("z", "xl"), 0, 0, tiled=True).astype(F32), axis=0)

    output_parts = weight_terms(
        "output_weight_terms",
        output_grad_kernel,
        pos,
        0,
        after(every_out, give),
        group_cotangent,
        (PLANES, BLOCK, 128),
    )
    output_weight_grad = plane_sum(after(output_parts, attended))
    query_parts = weight_terms(
        "query_weight_terms",
        query_grad_kernel,
        pos,
        1,
        after(every_grad, output_parts),
        group_states,
        (BLOCK, BLOCK),
    )
    query_parts = after(query_parts, output_weight_grad)
    query_weight_grad = plane_sum(query_parts.reshape(PLANES, 128, BLOCK))
    return attended, query_weight_grad, output_weight_grad, owned[0], owned[1]


def solution(mesh):
    devices = mesh.devices.reshape([size for _, size in AXES])
    split = Mesh(devices, [name for name, _ in AXES])
    return jax.shard_map(
        on_device,
        mesh=split,
        in_specs=(
            P(SEQ, HEADS),
            P(None, HEADS),
            P(HEADS, None),
            P(HEADS + SEQ, None),
            P(HEADS + SEQ, None),
            P(),
            P(),
            P(SEQ, HEADS),
        ),
        out_specs=(
            P(SEQ, HEADS),
            P(SEQ, HEADS),
            P(HEADS, SEQ),
            P(HEADS + SEQ, None),
            P(HEADS + SEQ, None),
        ),
        check_vma=False,
    )
```

```python
import math

import jax
import jax.numpy as jnp
from jax import lax
from jax.experimental import pallas as pl
from jax.experimental.pallas import tpu as pltpu
from jax.sharding import Mesh
from jax.sharding import PartitionSpec as P

HEAD = 128
SCALE = 1.0 / math.sqrt(HEAD)
LOG2E = math.log2(math.e)
F32 = jnp.float32
BF16 = jnp.bfloat16
AXES = (("xh", 2), ("core", 2), ("z", 4), ("y", 4), ("xl", 2))
HEADS = ("xh", "core")
SEQ = ("z", "y", "xl")
XH, CORE, Z, Y, XL = range(5)
SWAP = [(0, 1), (1, 0)]
VMEM = 56 * 1024 * 1024
TOK = 256
PIECE = 256
GROUP = 4 * TOK
BLOCK = 1024
PLANES = 8


def dot(a, b, contract=((1,), (0,))):
    return lax.dot_general(a, b, (contract, ((), ())), preferred_element_type=F32)


def shifted(index, by, size=4):
    return lax.rem(index + by + size, size)


def head_block(step, pos):
    return lax.rem(pos[XH] + step // 2, 2) * 2 + lax.rem(pos[CORE] + step % 2, 2)


def struct(shape, dtype=BF16):
    return jax.ShapeDtypeStruct(shape, dtype)


def whole(shape):
    return pl.BlockSpec(shape, lambda *_: (0,) * len(shape))


def call(kernel, name, grid, in_specs, out_specs, out_shape, scratch, flops, moved, pos, *args):
    return pl.pallas_call(
        kernel,
        grid_spec=pltpu.PrefetchScalarGridSpec(
            num_scalar_prefetch=1,
            grid=grid,
            in_specs=in_specs,
            out_specs=out_specs,
            scratch_shapes=scratch,
        ),
        out_shape=out_shape,
        compiler_params=pltpu.CompilerParams(vmem_limit_bytes=VMEM),
        cost_estimate=pl.CostEstimate(flops=flops, bytes_accessed=moved, transcendentals=0),
        name=name,
    )(pos, *args)


HBM = pl.BlockSpec(memory_space=pltpu.HBM)


def moved_in(pairs, sems):
    copies = [pltpu.make_async_copy(source, target, sems.at[i]) for i, (source, target) in enumerate(pairs)]
    for copy in copies:
        copy.start()
    return copies


def weight_block(w_ref, step, pos, by_columns):
    part = pl.ds(pl.multiple_of(head_block(step, pos) * BLOCK, BLOCK), BLOCK)
    return w_ref.at[:, part] if by_columns else w_ref.at[part, :]


def project_kernel(first, pos, *refs):
    before, refs = (None, refs) if first == 0 else (refs[0], refs[1:])
    sources, (wq, wo, out, blocks, weights, known, block_sems, weight_sems, known_sems) = refs[:4], refs[4:]
    pairs = [
        (weight_block(w, first + i, pos, w is wo), weights.at[2 * n + i])
        for n, w in enumerate((wq, wo))
        for i in range(2)
    ]
    moves = moved_in([(x, blocks.at[i]) for i, x in enumerate(sources)], block_sems)
    weight_moves = moved_in(pairs, weight_sems)
    if before is not None:
        moves += moved_in([(before, known)], known_sems)
    for move in moves:
        move.wait()
    for n in range(2):
        contract = ((1,), (1,)) if n else ((1,), (0,))
        weight_moves[2 * n].wait()
        total = dot(blocks[2 * n], weights[2 * n], contract)
        if before is not None:
            total = total + known[n]
        weight_moves[2 * n + 1].wait()
        total = total + dot(blocks[2 * n + 1], weights[2 * n + 1], contract)
        if before is None:
            out[n] = total
        else:
            for layer in range(4):
                out[layer, n] = total[:, layer * PIECE : (layer + 1) * PIECE].astype(BF16)


def project(name, pos, blocks, query_weight, output_weight, before=None):
    shape, dtype = ((2, TOK, BLOCK), F32) if before is None else ((4, 2, TOK, PIECE), BF16)
    args = (*(() if before is None else (before,)), *blocks, query_weight, output_weight)
    return call(
        lambda *refs: project_kernel(0 if before is None else 2, *refs),
        name,
        (1,),
        [HBM] * len(args),
        whole(shape),
        struct(shape, dtype),
        [
            pltpu.VMEM((4, TOK, BLOCK), BF16),
            pltpu.VMEM((4, BLOCK, BLOCK), BF16),
            pltpu.VMEM((2, TOK, BLOCK), F32),
            pltpu.SemaphoreType.DMA((4,)),
            pltpu.SemaphoreType.DMA((4,)),
            pltpu.SemaphoreType.DMA((1,)),
        ],
        8 * TOK * BLOCK * BLOCK,
        8 * BLOCK * BLOCK,
        pos,
        *args,
    )


def assemble_kernel(pos, p0, p1, p2, p3, turned, straight):
    for i, piece in enumerate((p0, p1, p2, p3)):
        col = pl.multiple_of(head_block(i, pos) * PIECE, PIECE)
        for d in range(4):
            token = pl.multiple_of(shifted(pos[Y], -d) * TOK, TOK)
            turned[pl.ds(col, PIECE), pl.ds(token, TOK)] = piece[d, 0].T
            straight[pl.ds(token, TOK), pl.ds(col, PIECE)] = piece[d, 1]


def assemble(pos, pieces):
    return call(
        assemble_kernel,
        "column_blocks",
        (1,),
        [whole((4, 2, TOK, PIECE))] * 4,
        [whole((BLOCK, GROUP)), whole((GROUP, BLOCK))],
        [struct((BLOCK, GROUP)), struct((GROUP, BLOCK))],
        [],
        0,
        8 * BLOCK * GROUP,
        pos,
        *pieces,
    )


def attention_kernel(pos, bias, rows, k_ref, v_ref, out, dk_ref, dv_ref, dk_sum, dv_sum):
    k, v = k_ref[...], v_ref[...]
    for layer in range(4):
        q = rows[layer, 0]
        scores = dot(q, k, ((1,), (1,))) + bias[...]
        top = jnp.max(scores, axis=1, keepdims=True)
        weights = jnp.exp2((scores - top) * (SCALE * LOG2E))
        share = 1.0 / jnp.sum(weights, axis=1, keepdims=True)
        low = weights.astype(BF16)
        heads_out = (dot(low, v) * share).astype(BF16)
        token = slice(layer * TOK, (layer + 1) * TOK)
        out[0, :, token] = heads_out.T
        g = (rows[layer, 1].astype(F32) * (share * SCALE)).astype(BF16)
        delta = jnp.sum(g.astype(F32) * heads_out.astype(F32), axis=1, keepdims=True)
        score_grad = (low.astype(F32) * (dot(g, v, ((1,), (1,))) - delta)).astype(BF16)
        out[1, :, token] = dot(score_grad, k).astype(BF16).T
        dk_term, dv_term = dot(q, score_grad, ((0,), (0,))), dot(g, low, ((0,), (0,)))
        dk_sum[...] = dk_term if layer == 0 else dk_sum[...] + dk_term
        dv_sum[...] = dv_term if layer == 0 else dv_sum[...] + dv_term
    dk_ref[...] = dk_sum[...].T.astype(BF16)
    dv_ref[...] = (dv_sum[...] * (1.0 / SCALE)).T.astype(BF16)


def attention(pos, bias, rows, keys, values):
    column = pl.BlockSpec((GROUP, HEAD), lambda h, pos: (0, h))
    context = keys.shape[0]
    return call(
        attention_kernel,
        "attention",
        (PIECE // HEAD,),
        [whole((1, context)), pl.BlockSpec((4, 2, TOK, HEAD), lambda h, pos: (0, 0, 0, h))] + [column] * 2,
        [pl.BlockSpec((2, HEAD, GROUP), lambda h, pos: (0, h, 0))] + [column] * 2,
        [struct((2, PIECE, GROUP))] + [struct((GROUP, PIECE))] * 2,
        [pltpu.VMEM((HEAD, context), F32)] * 2,
        30 * GROUP * PIECE * context,
        16 * GROUP * PIECE,
        pos,
        bias,
        rows,
        keys,
        values,
    )


GATHERED = ((0, 0), (1, 0), (3, 0), (2, 0), (2, 1))


def output_grad_kernel(pos, *refs):
    left, right, out = refs[:5], refs[5], refs[6]
    for ref, (e, part) in zip(left, GATHERED):
        rows = ref.shape[1]
        row = pl.multiple_of(shifted(pos[Y], -e) * PIECE + part * rows, rows)
        product = dot(ref[0], right[...]).astype(BF16)
        for p in range(PLANES):
            out[p, pl.ds(row, rows), :] = product[:, p * 128 : (p + 1) * 128]


def query_grad_kernel(pos, *refs):
    right, left, out = refs[:5], refs[5], refs[6]
    for ref, (e, part) in zip(right, GATHERED):
        cols = ref.shape[1]
        col = pl.multiple_of(shifted(pos[Y], -e) * PIECE + part * cols, cols)
        out[:, pl.ds(col, cols)] = dot(left[...], ref[0], ((1,), (1,))).astype(BF16)


def one_of(pair, which):
    return pl.BlockSpec((1, *pair.shape[1:]), lambda i, pos: (which if pair.shape[0] == 2 else 0, 0, 0))


def weight_terms(name, kernel, pos, which, gathered, block, out):
    return call(
        kernel,
        name,
        (1,),
        [one_of(a, which) for a in gathered] + [whole(block.shape)],
        whole(out),
        struct(out),
        [],
        2 * GROUP * BLOCK * BLOCK,
        6 * BLOCK * BLOCK,
        pos,
        *gathered,
        block,
    )


def output_kernel(pos, *refs):
    rows, w_ref, give, keep, weights, sems = refs[:5], *refs[5:]
    order = (1, 3, 0, 2)
    moves = moved_in([(weight_block(w_ref, i, pos, True), weights.at[n]) for n, i in enumerate(order)], sems)
    for n in range(4):
        moves[n].wait()
        product = jnp.zeros((TOK, BLOCK), F32)
        for ref, (e, part) in zip(rows, GATHERED):
            size = ref.shape[1]
            row = pl.multiple_of(shifted(pos[Y], -e) * PIECE + part * size, size)
            product = product + dot(ref[0], weights[n, pl.ds(row, size), :], ((0,), (0,)))
        if n < 2:
            give[n] = product.astype(BF16)
        else:
            keep[n - 2] = product


def output_terms(pos, gathered, weight):
    return call(
        output_kernel,
        "output_terms",
        (1,),
        [pl.BlockSpec((1, a.shape[1], TOK), lambda n, pos: (0, 0, pos[Y])) for a in gathered] + [HBM],
        [whole((2, TOK, BLOCK))] * 2,
        [struct((2, TOK, BLOCK)), struct((2, TOK, BLOCK), F32)],
        [pltpu.VMEM((4, BLOCK, BLOCK), BF16), pltpu.SemaphoreType.DMA((4,))],
        2 * TOK * 4 * BLOCK * BLOCK,
        2 * 4 * BLOCK * BLOCK,
        pos,
        *gathered,
        weight,
    )


def context_bias(lengths, slot_passage):
    slot_lengths = jnp.sum(
        jnp.where(slot_passage[:, None] == jnp.arange(4)[None, :], lengths[None, :], 0), axis=1
    )
    position = jnp.arange(TOK, dtype=jnp.int32)
    valid = position[None, :] < slot_lengths[:, None]
    return jnp.where(valid, 0.0, -jnp.inf).astype(F32).reshape(1, 4 * TOK)


def on_device(
    decoder_states,
    query_weight,
    output_weight,
    context_keys,
    context_values,
    lengths,
    slot_passage,
    output_cotangent,
):
    pos = jnp.stack([lax.axis_index(name) for name, _ in AXES]).astype(jnp.int32)

    def shift(x, axis, d):
        return lax.ppermute(x, axis, [(i, (i + d) % 4) for i in range(4)])

    def swap(x, axis):
        return lax.ppermute(x, axis, SWAP)

    def after(x, *others):
        return lax.optimization_barrier((x, *others))[0]

    far_states, far_cotangent = swap(decoder_states, "xh"), swap(output_cotangent, "xh")
    near = (decoder_states, swap(decoder_states, "core"), output_cotangent, swap(output_cotangent, "core"))
    products = project("project_near", pos, near, query_weight, output_weight)

    both = jnp.stack([decoder_states, output_cotangent]).reshape(2, TOK, 4, PIECE)
    quarters = [lax.dynamic_index_in_dim(both, shifted(pos[Y], d), 2, False) for d in range(4)]
    quarters = [shift(x, "y", d) if d else x for d, x in enumerate(quarters)]

    own = jnp.stack([context_keys, context_values]).reshape(2, 8, 4, 4, PIECE).transpose(2, 3, 0, 1, 4)
    own = jnp.broadcast_to(own[:, None, :, None], (4, 4, 4, 2, 2, 8, PIECE)).reshape(128, 2, 8, PIECE)
    context = lax.all_to_all(after(own, products, far_states, far_cotangent, quarters), HEADS + SEQ, 0, 0, tiled=True)
    keys = context[:, 0].reshape(4 * TOK, PIECE)
    values = context[:, 1].reshape(4 * TOK, PIECE)
    bias = context_bias(lengths, slot_passage)

    far = (far_states, swap(far_states, "core"), far_cotangent, swap(far_cotangent, "core"))
    rows = project("project_far", pos, far, query_weight, output_weight, products)
    rows = lax.all_to_all(rows, "y", 0, 0, tiled=True)

    piece = jnp.stack(after(quarters, rows))
    over_x = swap(piece, "xh")

    gathered, key_terms, value_terms = attention(pos, bias, rows, keys, values)
    left, right = shift(gathered, "y", 1), shift(gathered, "y", 3)
    half = PIECE // 2

    def far_halves(i):
        return shift(left[i : i + 1, :half], "y", 1), shift(right[i : i + 1, half:], "y", 3)

    left, right = after((left, right), over_x)
    every_out = (gathered, left, right, *far_halves(0))
    every_grad = (gathered, left, right, *far_halves(1))

    terms = jnp.stack([key_terms.reshape(128, 8, PIECE), value_terms.reshape(128, 8, PIECE)], 1)
    moved = lax.all_to_all(terms, HEADS + SEQ, 0, 0, tiled=True)
    owned = jnp.sum(moved.reshape(4, 4, 4, 2, 2, 8, PIECE).astype(F32), axis=(1, 3))
    owned = owned.transpose(2, 3, 0, 1, 4).reshape(2, 8, 16 * PIECE)

    piece, over_x = after((piece, over_x), left, right)
    group_states, group_cotangent = assemble(
        pos, after((piece, swap(piece, "core"), over_x, swap(over_x, "core")), moved)
    )

    give, keep = output_terms(pos, every_out, output_weight)
    pair = keep + swap(give, "core").astype(F32)
    pair_far = pair[1].astype(BF16)
    attended = (pair[0] + swap(pair_far, "xh").astype(F32)).astype(BF16)

    def plane_sum(parts):
        return jnp.sum(lax.all_to_all(parts, ("z", "xl"), 0, 0, tiled=True).astype(F32), axis=0)

    output_parts = weight_terms(
        "output_weight_terms",
        output_grad_kernel,
        pos,
        0,
        after(every_out, give),
        group_cotangent,
        (PLANES, BLOCK, 128),
    )
    output_weight_grad = plane_sum(output_parts)
    query_parts = weight_terms(
        "query_weight_terms",
        query_grad_kernel,
        pos,
        1,
        after(every_grad, output_parts),
        group_states,
        (BLOCK, BLOCK),
    )
    query_parts = after(query_parts, output_weight_grad, pair_far)
    query_weight_grad = plane_sum(query_parts.reshape(PLANES, 128, BLOCK))
    return attended, query_weight_grad, output_weight_grad, owned[0], owned[1]


def solution(mesh):
    devices = mesh.devices.reshape([size for _, size in AXES])
    split = Mesh(devices, [name for name, _ in AXES])
    return jax.shard_map(
        on_device,
        mesh=split,
        in_specs=(
            P(SEQ, HEADS),
            P(None, HEADS),
            P(HEADS, None),
            P(HEADS + SEQ, None),
            P(HEADS + SEQ, None),
            P(),
            P(),
            P(SEQ, HEADS),
        ),
        out_specs=(
            P(SEQ, HEADS),
            P(SEQ, HEADS),
            P(HEADS, SEQ),
            P(HEADS + SEQ, None),
            P(HEADS + SEQ, None),
        ),
        check_vma=False,
    )
```

```python
import math

import jax
import jax.numpy as jnp
from jax import lax
from jax.experimental import pallas as pl
from jax.experimental.pallas import tpu as pltpu
from jax.sharding import Mesh
from jax.sharding import PartitionSpec as P

HEAD = 128
SCALE = 1.0 / math.sqrt(HEAD)
LOG2E = math.log2(math.e)
F32 = jnp.float32
BF16 = jnp.bfloat16
AXES = (("xh", 2), ("core", 2), ("z", 4), ("y", 4), ("xl", 2))
HEADS = ("xh", "core")
SEQ = ("z", "y", "xl")
XH, CORE, Z, Y, XL = range(5)
SWAP = [(0, 1), (1, 0)]
VMEM = 56 * 1024 * 1024
TOK = 256
PIECE = 256
GROUP = 4 * TOK
BLOCK = 1024
PLANES = 8


def dot(a, b, contract=((1,), (0,))):
    return lax.dot_general(a, b, (contract, ((), ())), preferred_element_type=F32)


def shifted(index, by, size=4):
    return lax.rem(index + by + size, size)


def head_block(step, pos):
    return lax.rem(pos[XH] + step // 2, 2) * 2 + lax.rem(pos[CORE] + step % 2, 2)


def struct(shape, dtype=BF16):
    return jax.ShapeDtypeStruct(shape, dtype)


def whole(shape):
    return pl.BlockSpec(shape, lambda *_: (0,) * len(shape))


def call(kernel, name, grid, in_specs, out_specs, out_shape, scratch, flops, moved, pos, *args):
    return pl.pallas_call(
        kernel,
        grid_spec=pltpu.PrefetchScalarGridSpec(
            num_scalar_prefetch=1,
            grid=grid,
            in_specs=in_specs,
            out_specs=out_specs,
            scratch_shapes=scratch,
        ),
        out_shape=out_shape,
        compiler_params=pltpu.CompilerParams(vmem_limit_bytes=VMEM),
        cost_estimate=pl.CostEstimate(flops=flops, bytes_accessed=moved, transcendentals=0),
        name=name,
    )(pos, *args)


HBM = pl.BlockSpec(memory_space=pltpu.HBM)


def moved_in(pairs, sems):
    copies = [pltpu.make_async_copy(source, target, sems.at[i]) for i, (source, target) in enumerate(pairs)]
    for copy in copies:
        copy.start()
    return copies


def weight_block(w_ref, step, pos, by_columns):
    part = pl.ds(pl.multiple_of(head_block(step, pos) * BLOCK, BLOCK), BLOCK)
    return w_ref.at[:, part] if by_columns else w_ref.at[part, :]


def project_kernel(first, pos, *refs):
    before, refs = (None, refs) if first == 0 else (refs[0], refs[1:])
    sources, (wq, wo, out, blocks, weights, known, block_sems, weight_sems, known_sems) = refs[:4], refs[4:]
    pairs = [
        (weight_block(w, first + i, pos, w is wo), weights.at[2 * n + i])
        for n, w in enumerate((wq, wo))
        for i in range(2)
    ]
    moves = moved_in([(x, blocks.at[i]) for i, x in enumerate(sources)], block_sems)
    weight_moves = moved_in(pairs, weight_sems)
    if before is not None:
        moves += moved_in([(before, known)], known_sems)
    for move in moves:
        move.wait()
    for n in range(2):
        contract = ((1,), (1,)) if n else ((1,), (0,))
        weight_moves[2 * n].wait()
        total = dot(blocks[2 * n], weights[2 * n], contract)
        if before is not None:
            total = total + known[n]
        weight_moves[2 * n + 1].wait()
        total = total + dot(blocks[2 * n + 1], weights[2 * n + 1], contract)
        if before is None:
            out[n] = total
        else:
            for layer in range(4):
                out[layer, n] = total[:, layer * PIECE : (layer + 1) * PIECE].astype(BF16)


def project(name, pos, blocks, query_weight, output_weight, before=None):
    shape, dtype = ((2, TOK, BLOCK), F32) if before is None else ((4, 2, TOK, PIECE), BF16)
    args = (*(() if before is None else (before,)), *blocks, query_weight, output_weight)
    return call(
        lambda *refs: project_kernel(0 if before is None else 2, *refs),
        name,
        (1,),
        [HBM] * len(args),
        whole(shape),
        struct(shape, dtype),
        [
            pltpu.VMEM((4, TOK, BLOCK), BF16),
            pltpu.VMEM((4, BLOCK, BLOCK), BF16),
            pltpu.VMEM((2, TOK, BLOCK), F32),
            pltpu.SemaphoreType.DMA((4,)),
            pltpu.SemaphoreType.DMA((4,)),
            pltpu.SemaphoreType.DMA((1,)),
        ],
        8 * TOK * BLOCK * BLOCK,
        8 * BLOCK * BLOCK,
        pos,
        *args,
    )


def assemble_kernel(pos, p0, p1, p2, p3, turned, straight):
    for i, piece in enumerate((p0, p1, p2, p3)):
        col = pl.multiple_of(head_block(i, pos) * PIECE, PIECE)
        for d in range(4):
            token = pl.multiple_of(shifted(pos[Y], -d) * TOK, TOK)
            turned[pl.ds(col, PIECE), pl.ds(token, TOK)] = piece[d, 0].T
            straight[pl.ds(token, TOK), pl.ds(col, PIECE)] = piece[d, 1]


def assemble(pos, pieces):
    return call(
        assemble_kernel,
        "column_blocks",
        (1,),
        [whole((4, 2, TOK, PIECE))] * 4,
        [whole((BLOCK, GROUP)), whole((GROUP, BLOCK))],
        [struct((BLOCK, GROUP)), struct((GROUP, BLOCK))],
        [],
        0,
        8 * BLOCK * GROUP,
        pos,
        *pieces,
    )


def attention_kernel(pos, bias, rows, k_ref, v_ref, out, dk_ref, dv_ref, dk_sum, dv_sum):
    k, v = k_ref[...], v_ref[...]
    for layer in range(4):
        q = rows[layer, 0]
        scores = dot(q, k, ((1,), (1,))) + bias[...]
        top = jnp.max(scores, axis=1, keepdims=True)
        weights = jnp.exp2((scores - top) * (SCALE * LOG2E))
        share = 1.0 / jnp.sum(weights, axis=1, keepdims=True)
        low = weights.astype(BF16)
        heads_out = (dot(low, v) * share).astype(BF16)
        token = slice(layer * TOK, (layer + 1) * TOK)
        out[0, :, token] = heads_out.T
        g = (rows[layer, 1].astype(F32) * (share * SCALE)).astype(BF16)
        delta = jnp.sum(g.astype(F32) * heads_out.astype(F32), axis=1, keepdims=True)
        score_grad = (low.astype(F32) * (dot(g, v, ((1,), (1,))) - delta)).astype(BF16)
        out[1, :, token] = dot(score_grad, k).astype(BF16).T
        dk_term, dv_term = dot(q, score_grad, ((0,), (0,))), dot(g, low, ((0,), (0,)))
        dk_sum[...] = dk_term if layer == 0 else dk_sum[...] + dk_term
        dv_sum[...] = dv_term if layer == 0 else dv_sum[...] + dv_term
    dk_ref[...] = dk_sum[...].T.astype(BF16)
    dv_ref[...] = (dv_sum[...] * (1.0 / SCALE)).T.astype(BF16)


def attention(pos, bias, rows, keys, values):
    column = pl.BlockSpec((GROUP, HEAD), lambda h, pos: (0, h))
    context = keys.shape[0]
    return call(
        attention_kernel,
        "attention",
        (PIECE // HEAD,),
        [whole((1, context)), pl.BlockSpec((4, 2, TOK, HEAD), lambda h, pos: (0, 0, 0, h))] + [column] * 2,
        [pl.BlockSpec((2, HEAD, GROUP), lambda h, pos: (0, h, 0))] + [column] * 2,
        [struct((2, PIECE, GROUP))] + [struct((GROUP, PIECE))] * 2,
        [pltpu.VMEM((HEAD, context), F32)] * 2,
        30 * GROUP * PIECE * context,
        16 * GROUP * PIECE,
        pos,
        bias,
        rows,
        keys,
        values,
    )


GATHERED = ((0, 0), (1, 0), (3, 0), (2, 0), (2, 1))


def output_grad_kernel(pos, *refs):
    left, right, out = refs[:5], refs[5], refs[6]
    for ref, (e, part) in zip(left, GATHERED):
        rows = ref.shape[1]
        row = pl.multiple_of(shifted(pos[Y], -e) * PIECE + part * rows, rows)
        product = dot(ref[0], right[...]).astype(BF16)
        for p in range(PLANES):
            out[p, pl.ds(row, rows), :] = product[:, p * 128 : (p + 1) * 128]


def query_grad_kernel(pos, *refs):
    right, left, out = refs[:5], refs[5], refs[6]
    for ref, (e, part) in zip(right, GATHERED):
        cols = ref.shape[1]
        col = pl.multiple_of(shifted(pos[Y], -e) * PIECE + part * cols, cols)
        out[:, pl.ds(col, cols)] = dot(left[...], ref[0], ((1,), (1,))).astype(BF16)


def one_of(pair, which):
    return pl.BlockSpec((1, *pair.shape[1:]), lambda i, pos: (which if pair.shape[0] == 2 else 0, 0, 0))


def weight_terms(name, kernel, pos, which, gathered, block, out):
    return call(
        kernel,
        name,
        (1,),
        [one_of(a, which) for a in gathered] + [whole(block.shape)],
        whole(out),
        struct(out),
        [],
        2 * GROUP * BLOCK * BLOCK,
        6 * BLOCK * BLOCK,
        pos,
        *gathered,
        block,
    )


def output_kernel(pos, *refs):
    rows, w_ref, give, keep, weights, sems = refs[:5], *refs[5:]
    order = (1, 3, 0, 2)
    moves = moved_in([(weight_block(w_ref, i, pos, True), weights.at[n]) for n, i in enumerate(order)], sems)
    for n in range(4):
        moves[n].wait()
        product = jnp.zeros((TOK, BLOCK), F32)
        for ref, (e, part) in zip(rows, GATHERED):
            size = ref.shape[1]
            row = pl.multiple_of(shifted(pos[Y], -e) * PIECE + part * size, size)
            product = product + dot(ref[0], weights[n, pl.ds(row, size), :], ((0,), (0,)))
        if n < 2:
            give[n] = product.astype(BF16)
        else:
            keep[n - 2] = product


def output_terms(pos, gathered, weight):
    return call(
        output_kernel,
        "output_terms",
        (1,),
        [pl.BlockSpec((1, a.shape[1], TOK), lambda n, pos: (0, 0, pos[Y])) for a in gathered] + [HBM],
        [whole((2, TOK, BLOCK))] * 2,
        [struct((2, TOK, BLOCK)), struct((2, TOK, BLOCK), F32)],
        [pltpu.VMEM((4, BLOCK, BLOCK), BF16), pltpu.SemaphoreType.DMA((4,))],
        2 * TOK * 4 * BLOCK * BLOCK,
        2 * 4 * BLOCK * BLOCK,
        pos,
        *gathered,
        weight,
    )


def context_bias(lengths, slot_passage):
    slot_lengths = jnp.sum(
        jnp.where(slot_passage[:, None] == jnp.arange(4)[None, :], lengths[None, :], 0), axis=1
    )
    position = jnp.arange(TOK, dtype=jnp.int32)
    valid = position[None, :] < slot_lengths[:, None]
    return jnp.where(valid, 0.0, -jnp.inf).astype(F32).reshape(1, 4 * TOK)


def on_device(
    decoder_states,
    query_weight,
    output_weight,
    context_keys,
    context_values,
    lengths,
    slot_passage,
    output_cotangent,
):
    pos = jnp.stack([lax.axis_index(name) for name, _ in AXES]).astype(jnp.int32)

    def shift(x, axis, d):
        return lax.ppermute(x, axis, [(i, (i + d) % 4) for i in range(4)])

    def swap(x, axis):
        return lax.ppermute(x, axis, SWAP)

    def after(x, *others):
        return lax.optimization_barrier((x, *others))[0]

    far_states, far_cotangent = swap(decoder_states, "xh"), swap(output_cotangent, "xh")
    near = (decoder_states, swap(decoder_states, "core"), output_cotangent, swap(output_cotangent, "core"))
    products = project("project_near", pos, near, query_weight, output_weight)

    both = jnp.stack([decoder_states, output_cotangent]).reshape(2, TOK, 4, PIECE)
    quarters = [lax.dynamic_index_in_dim(both, shifted(pos[Y], d), 2, False) for d in range(4)]
    quarters = [shift(x, "y", d) if d else x for d, x in enumerate(quarters)]

    own = jnp.stack([context_keys, context_values]).reshape(2, 8, 4, 4, PIECE).transpose(2, 3, 0, 1, 4)
    own = jnp.broadcast_to(own[:, None, :, None], (4, 4, 4, 2, 2, 8, PIECE)).reshape(128, 2, 8, PIECE)
    context = lax.all_to_all(after(own, products, far_states, far_cotangent, quarters), HEADS + SEQ, 0, 0, tiled=True)
    keys = context[:, 0].reshape(4 * TOK, PIECE)
    values = context[:, 1].reshape(4 * TOK, PIECE)
    bias = context_bias(lengths, slot_passage)

    far = (far_states, swap(far_states, "core"), far_cotangent, swap(far_cotangent, "core"))
    rows = project("project_far", pos, far, query_weight, output_weight, products)
    rows = lax.all_to_all(rows, "y", 0, 0, tiled=True)

    piece = jnp.stack(after(quarters, rows))
    over_x = swap(piece, "xh")

    gathered, key_terms, value_terms = attention(pos, bias, rows, keys, values)
    left, right = shift(gathered, "y", 1), shift(gathered, "y", 3)
    half = PIECE // 2

    def far_halves(i):
        return shift(left[i : i + 1, :half], "y", 1), shift(right[i : i + 1, half:], "y", 3)

    left, right = after((left, right), over_x)
    every_out = (gathered, left, right, *far_halves(0))
    every_grad = (gathered, left, right, *far_halves(1))

    piece, over_x = after((piece, over_x), left, right)
    group_states, group_cotangent = assemble(
        pos, (piece, swap(piece, "core"), over_x, swap(over_x, "core"))
    )

    def plane_sum(parts):
        return jnp.sum(lax.all_to_all(parts, ("z", "xl"), 0, 0, tiled=True).astype(F32), axis=0)

    output_parts = weight_terms(
        "output_weight_terms",
        output_grad_kernel,
        pos,
        0,
        every_out,
        group_cotangent,
        (PLANES, BLOCK, 128),
    )
    output_weight_grad = plane_sum(output_parts)

    give, keep = output_terms(pos, after(every_out, output_parts), output_weight)
    pair = keep + swap(give, "core").astype(F32)
    attended = (pair[0] + swap(pair[1].astype(BF16), "xh").astype(F32)).astype(BF16)

    terms = jnp.stack([key_terms.reshape(128, 8, PIECE), value_terms.reshape(128, 8, PIECE)], 1)
    moved = lax.all_to_all(after(terms, output_weight_grad), HEADS + SEQ, 0, 0, tiled=True)
    owned = jnp.sum(moved.reshape(4, 4, 4, 2, 2, 8, PIECE).astype(F32), axis=(1, 3))
    owned = owned.transpose(2, 3, 0, 1, 4).reshape(2, 8, 16 * PIECE)

    query_parts = weight_terms(
        "query_weight_terms",
        query_grad_kernel,
        pos,
        1,
        after(every_grad, output_parts),
        group_states,
        (BLOCK, BLOCK),
    )
    query_parts = after(query_parts, moved, attended)
    query_weight_grad = plane_sum(query_parts.reshape(PLANES, 128, BLOCK))
    return attended, query_weight_grad, output_weight_grad, owned[0], owned[1]


def solution(mesh):
    devices = mesh.devices.reshape([size for _, size in AXES])
    split = Mesh(devices, [name for name, _ in AXES])
    return jax.shard_map(
        on_device,
        mesh=split,
        in_specs=(
            P(SEQ, HEADS),
            P(None, HEADS),
            P(HEADS, None),
            P(HEADS + SEQ, None),
            P(HEADS + SEQ, None),
            P(),
            P(),
            P(SEQ, HEADS),
        ),
        out_specs=(
            P(SEQ, HEADS),
            P(SEQ, HEADS),
            P(HEADS, SEQ),
            P(HEADS + SEQ, None),
            P(HEADS + SEQ, None),
        ),
        check_vma=False,
    )
```

```python
import math

import jax
import jax.numpy as jnp
from jax import lax
from jax.experimental import pallas as pl
from jax.experimental.pallas import tpu as pltpu
from jax.sharding import Mesh
from jax.sharding import PartitionSpec as P

HEAD = 128
SCALE = 1.0 / math.sqrt(HEAD)
LOG2E = math.log2(math.e)
F32 = jnp.float32
BF16 = jnp.bfloat16
AXES = (("xh", 2), ("core", 2), ("z", 4), ("y", 4), ("xl", 2))
HEADS = ("xh", "core")
SEQ = ("z", "y", "xl")
XH, CORE, Z, Y, XL = range(5)
SWAP = [(0, 1), (1, 0)]
VMEM = 56 * 1024 * 1024
TOK = 256
PIECE = 256
GROUP = 4 * TOK
BLOCK = 1024
PLANES = 8


def dot(a, b, contract=((1,), (0,))):
    return lax.dot_general(a, b, (contract, ((), ())), preferred_element_type=F32)


def shifted(index, by, size=4):
    return lax.rem(index + by + size, size)


def head_block(step, pos):
    return lax.rem(pos[XH] + step // 2, 2) * 2 + lax.rem(pos[CORE] + step % 2, 2)


def struct(shape, dtype=BF16):
    return jax.ShapeDtypeStruct(shape, dtype)


def whole(shape):
    return pl.BlockSpec(shape, lambda *_: (0,) * len(shape))


def call(kernel, name, grid, in_specs, out_specs, out_shape, scratch, flops, moved, pos, *args):
    return pl.pallas_call(
        kernel,
        grid_spec=pltpu.PrefetchScalarGridSpec(
            num_scalar_prefetch=1,
            grid=grid,
            in_specs=in_specs,
            out_specs=out_specs,
            scratch_shapes=scratch,
        ),
        out_shape=out_shape,
        compiler_params=pltpu.CompilerParams(vmem_limit_bytes=VMEM),
        cost_estimate=pl.CostEstimate(flops=flops, bytes_accessed=moved, transcendentals=0),
        name=name,
    )(pos, *args)


HBM = pl.BlockSpec(memory_space=pltpu.HBM)


def moved_in(pairs, sems):
    copies = [pltpu.make_async_copy(source, target, sems.at[i]) for i, (source, target) in enumerate(pairs)]
    for copy in copies:
        copy.start()
    return copies


def weight_block(w_ref, step, pos, by_columns):
    part = pl.ds(pl.multiple_of(head_block(step, pos) * BLOCK, BLOCK), BLOCK)
    return w_ref.at[:, part] if by_columns else w_ref.at[part, :]


def project_kernel(first, pos, *refs):
    before, refs = (None, refs) if first == 0 else (refs[0], refs[1:])
    sources, (wq, wo, out, blocks, weights, known, block_sems, weight_sems, known_sems) = refs[:4], refs[4:]
    pairs = [
        (weight_block(w, first + i, pos, w is wo), weights.at[2 * n + i])
        for n, w in enumerate((wq, wo))
        for i in range(2)
    ]
    moves = moved_in([(x, blocks.at[i]) for i, x in enumerate(sources)], block_sems)
    weight_moves = moved_in(pairs, weight_sems)
    if before is not None:
        moves += moved_in([(before, known)], known_sems)
    for move in moves:
        move.wait()
    for n in range(2):
        contract = ((1,), (1,)) if n else ((1,), (0,))
        weight_moves[2 * n].wait()
        total = dot(blocks[2 * n], weights[2 * n], contract)
        if before is not None:
            total = total + known[n]
        weight_moves[2 * n + 1].wait()
        total = total + dot(blocks[2 * n + 1], weights[2 * n + 1], contract)
        if before is None:
            out[n] = total
        else:
            for layer in range(4):
                out[layer, n] = total[:, layer * PIECE : (layer + 1) * PIECE].astype(BF16)


def project(name, pos, blocks, query_weight, output_weight, before=None):
    shape, dtype = ((2, TOK, BLOCK), F32) if before is None else ((4, 2, TOK, PIECE), BF16)
    args = (*(() if before is None else (before,)), *blocks, query_weight, output_weight)
    return call(
        lambda *refs: project_kernel(0 if before is None else 2, *refs),
        name,
        (1,),
        [HBM] * len(args),
        whole(shape),
        struct(shape, dtype),
        [
            pltpu.VMEM((4, TOK, BLOCK), BF16),
            pltpu.VMEM((4, BLOCK, BLOCK), BF16),
            pltpu.VMEM((2, TOK, BLOCK), F32),
            pltpu.SemaphoreType.DMA((4,)),
            pltpu.SemaphoreType.DMA((4,)),
            pltpu.SemaphoreType.DMA((1,)),
        ],
        8 * TOK * BLOCK * BLOCK,
        8 * BLOCK * BLOCK,
        pos,
        *args,
    )


def assemble_kernel(pos, p0, p1, p2, p3, turned, straight):
    for i, piece in enumerate((p0, p1, p2, p3)):
        col = pl.multiple_of(head_block(i, pos) * PIECE, PIECE)
        for d in range(4):
            token = pl.multiple_of(shifted(pos[Y], -d) * TOK, TOK)
            turned[pl.ds(col, PIECE), pl.ds(token, TOK)] = piece[d, 0].T
            straight[pl.ds(token, TOK), pl.ds(col, PIECE)] = piece[d, 1]


def assemble(pos, pieces):
    return call(
        assemble_kernel,
        "column_blocks",
        (1,),
        [whole((4, 2, TOK, PIECE))] * 4,
        [whole((BLOCK, GROUP)), whole((GROUP, BLOCK))],
        [struct((BLOCK, GROUP)), struct((GROUP, BLOCK))],
        [],
        0,
        8 * BLOCK * GROUP,
        pos,
        *pieces,
    )


def attention_kernel(pos, bias, rows, k_ref, v_ref, out, dq_ref, dk_ref, dv_ref, dk_sum, dv_sum):
    k, v = k_ref[...], v_ref[...]
    for layer in range(4):
        q = rows[layer, 0]
        scores = dot(q, k, ((1,), (1,))) + bias[...]
        top = jnp.max(scores, axis=1, keepdims=True)
        weights = jnp.exp2((scores - top) * (SCALE * LOG2E))
        share = 1.0 / jnp.sum(weights, axis=1, keepdims=True)
        low = weights.astype(BF16)
        heads_out = (dot(low, v) * share).astype(BF16)
        token = slice(layer * TOK, (layer + 1) * TOK)
        out[0, :, token] = heads_out.T
        g = (rows[layer, 1].astype(F32) * (share * SCALE)).astype(BF16)
        delta = jnp.sum(g.astype(F32) * heads_out.astype(F32), axis=1, keepdims=True)
        score_grad = (low.astype(F32) * (dot(g, v, ((1,), (1,))) - delta)).astype(BF16)
        dq_ref[0, :, token] = dot(score_grad, k).astype(BF16).T
        dk_term, dv_term = dot(q, score_grad, ((0,), (0,))), dot(g, low, ((0,), (0,)))
        dk_sum[...] = dk_term if layer == 0 else dk_sum[...] + dk_term
        dv_sum[...] = dv_term if layer == 0 else dv_sum[...] + dv_term
    dk_ref[...] = dk_sum[...].T.astype(BF16)
    dv_ref[...] = (dv_sum[...] * (1.0 / SCALE)).T.astype(BF16)


def attention(pos, bias, rows, keys, values):
    column = pl.BlockSpec((GROUP, HEAD), lambda h, pos: (0, h))
    context = keys.shape[0]
    return call(
        attention_kernel,
        "attention",
        (PIECE // HEAD,),
        [whole((1, context)), pl.BlockSpec((4, 2, TOK, HEAD), lambda h, pos: (0, 0, 0, h))] + [column] * 2,
        [pl.BlockSpec((1, HEAD, GROUP), lambda h, pos: (0, h, 0))] * 2 + [column] * 2,
        [struct((1, PIECE, GROUP))] * 2 + [struct((GROUP, PIECE))] * 2,
        [pltpu.VMEM((HEAD, context), F32)] * 2,
        30 * GROUP * PIECE * context,
        16 * GROUP * PIECE,
        pos,
        bias,
        rows,
        keys,
        values,
    )


GATHERED = ((0, 0), (1, 0), (3, 0), (2, 0), (2, 1))


def output_grad_kernel(pos, *refs):
    left, right, out = refs[:5], refs[5], refs[6]
    for ref, (e, part) in zip(left, GATHERED):
        rows = ref.shape[1]
        row = pl.multiple_of(shifted(pos[Y], -e) * PIECE + part * rows, rows)
        product = dot(ref[0], right[...]).astype(BF16)
        for p in range(PLANES):
            out[p, pl.ds(row, rows), :] = product[:, p * 128 : (p + 1) * 128]


def query_grad_kernel(pos, *refs):
    right, left, out = refs[:5], refs[5], refs[6]
    for ref, (e, part) in zip(right, GATHERED):
        cols = ref.shape[1]
        col = pl.multiple_of(shifted(pos[Y], -e) * PIECE + part * cols, cols)
        out[:, pl.ds(col, cols)] = dot(left[...], ref[0], ((1,), (1,))).astype(BF16)


def weight_terms(name, kernel, pos, gathered, block, out):
    return call(
        kernel,
        name,
        (1,),
        [whole(a.shape) for a in gathered] + [whole(block.shape)],
        whole(out),
        struct(out),
        [],
        2 * GROUP * BLOCK * BLOCK,
        6 * BLOCK * BLOCK,
        pos,
        *gathered,
        block,
    )


def output_kernel(pos, *refs):
    rows, w_ref, give, keep, weights, sems = refs[:5], *refs[5:]
    order = (1, 3, 0, 2)
    moves = moved_in([(weight_block(w_ref, i, pos, True), weights.at[n]) for n, i in enumerate(order)], sems)
    for n in range(4):
        moves[n].wait()
        product = jnp.zeros((TOK, BLOCK), F32)
        for ref, (e, part) in zip(rows, GATHERED):
            size = ref.shape[1]
            row = pl.multiple_of(shifted(pos[Y], -e) * PIECE + part * size, size)
            product = product + dot(ref[0], weights[n, pl.ds(row, size), :], ((0,), (0,)))
        if n < 2:
            give[n] = product.astype(BF16)
        else:
            keep[n - 2] = product


def output_terms(pos, gathered, weight):
    return call(
        output_kernel,
        "output_terms",
        (1,),
        [pl.BlockSpec((1, a.shape[1], TOK), lambda n, pos: (0, 0, pos[Y])) for a in gathered] + [HBM],
        [whole((2, TOK, BLOCK))] * 2,
        [struct((2, TOK, BLOCK)), struct((2, TOK, BLOCK), F32)],
        [pltpu.VMEM((4, BLOCK, BLOCK), BF16), pltpu.SemaphoreType.DMA((4,))],
        2 * TOK * 4 * BLOCK * BLOCK,
        2 * 4 * BLOCK * BLOCK,
        pos,
        *gathered,
        weight,
    )


def context_bias(lengths, slot_passage):
    slot_lengths = jnp.sum(
        jnp.where(slot_passage[:, None] == jnp.arange(4)[None, :], lengths[None, :], 0), axis=1
    )
    position = jnp.arange(TOK, dtype=jnp.int32)
    valid = position[None, :] < slot_lengths[:, None]
    return jnp.where(valid, 0.0, -jnp.inf).astype(F32).reshape(1, 4 * TOK)


def on_device(
    decoder_states,
    query_weight,
    output_weight,
    context_keys,
    context_values,
    lengths,
    slot_passage,
    output_cotangent,
):
    pos = jnp.stack([lax.axis_index(name) for name, _ in AXES]).astype(jnp.int32)

    def shift(x, axis, d):
        return lax.ppermute(x, axis, [(i, (i + d) % 4) for i in range(4)])

    def swap(x, axis):
        return lax.ppermute(x, axis, SWAP)

    def after(x, *others):
        return lax.optimization_barrier((x, *others))[0]

    far_states, far_cotangent = swap(decoder_states, "xh"), swap(output_cotangent, "xh")
    near = (decoder_states, swap(decoder_states, "core"), output_cotangent, swap(output_cotangent, "core"))
    products = project("project_near", pos, near, query_weight, output_weight)

    both = jnp.stack([decoder_states, output_cotangent]).reshape(2, TOK, 4, PIECE)
    quarters = [lax.dynamic_index_in_dim(both, shifted(pos[Y], d), 2, False) for d in range(4)]
    quarters = [shift(x, "y", d) if d else x for d, x in enumerate(quarters)]

    own = jnp.stack([context_keys, context_values]).reshape(2, 8, 4, 4, PIECE).transpose(2, 3, 0, 1, 4)
    own = jnp.broadcast_to(own[:, None, :, None], (4, 4, 4, 2, 2, 8, PIECE)).reshape(128, 2, 8, PIECE)
    context = lax.all_to_all(after(own, products, far_states, far_cotangent, quarters), HEADS + SEQ, 0, 0, tiled=True)
    keys = context[:, 0].reshape(4 * TOK, PIECE)
    values = context[:, 1].reshape(4 * TOK, PIECE)
    bias = context_bias(lengths, slot_passage)

    far = (far_states, swap(far_states, "core"), far_cotangent, swap(far_cotangent, "core"))
    rows = project("project_far", pos, far, query_weight, output_weight, products)
    rows = lax.all_to_all(rows, "y", 0, 0, tiled=True)

    piece = jnp.stack(after(quarters, rows))
    over_x = swap(piece, "xh")

    heads_out, query_grad, key_terms, value_terms = attention(pos, bias, rows, keys, values)
    half = PIECE // 2

    def ring(x, *others):
        left, right = after((shift(x, "y", 1), shift(x, "y", 3)), *others)
        return x, left, right, shift(left[:, :half], "y", 1), shift(right[:, half:], "y", 3)

    every_out = ring(heads_out, over_x)

    piece, over_x = after((piece, over_x), *every_out[:3])
    group_states, group_cotangent = assemble(
        pos, (piece, swap(piece, "core"), over_x, swap(over_x, "core"))
    )

    def plane_sum(parts):
        return jnp.sum(lax.all_to_all(parts, ("z", "xl"), 0, 0, tiled=True).astype(F32), axis=0)

    output_parts = weight_terms(
        "output_weight_terms",
        output_grad_kernel,
        pos,
        every_out,
        group_cotangent,
        (PLANES, BLOCK, 128),
    )
    every_grad = ring(after(query_grad, every_out), output_parts)
    output_weight_grad = plane_sum(output_parts)

    give, keep = output_terms(pos, after(every_out, output_parts), output_weight)
    pair = keep + swap(give, "core").astype(F32)
    attended = (pair[0] + swap(pair[1].astype(BF16), "xh").astype(F32)).astype(BF16)

    query_parts = weight_terms(
        "query_weight_terms",
        query_grad_kernel,
        pos,
        after(every_grad, output_parts),
        group_states,
        (BLOCK, BLOCK),
    )

    terms = jnp.stack([key_terms.reshape(128, 8, PIECE), value_terms.reshape(128, 8, PIECE)], 1)
    moved = lax.all_to_all(after(terms, output_weight_grad, query_parts), HEADS + SEQ, 0, 0, tiled=True)
    owned = jnp.sum(moved.reshape(4, 4, 4, 2, 2, 8, PIECE).astype(F32), axis=(1, 3))
    owned = owned.transpose(2, 3, 0, 1, 4).reshape(2, 8, 16 * PIECE)

    query_parts = after(query_parts, moved, attended)
    query_weight_grad = plane_sum(query_parts.reshape(PLANES, 128, BLOCK))
    return attended, query_weight_grad, output_weight_grad, owned[0], owned[1]


def solution(mesh):
    devices = mesh.devices.reshape([size for _, size in AXES])
    split = Mesh(devices, [name for name, _ in AXES])
    return jax.shard_map(
        on_device,
        mesh=split,
        in_specs=(
            P(SEQ, HEADS),
            P(None, HEADS),
            P(HEADS, None),
            P(HEADS + SEQ, None),
            P(HEADS + SEQ, None),
            P(),
            P(),
            P(SEQ, HEADS),
        ),
        out_specs=(
            P(SEQ, HEADS),
            P(SEQ, HEADS),
            P(HEADS, SEQ),
            P(HEADS + SEQ, None),
            P(HEADS + SEQ, None),
        ),
        check_vma=False,
    )
```

```python
import math

import jax
import jax.numpy as jnp
from jax import lax
from jax.experimental import pallas as pl
from jax.experimental.pallas import tpu as pltpu
from jax.sharding import Mesh
from jax.sharding import PartitionSpec as P

HEAD = 128
SCALE = 1.0 / math.sqrt(HEAD)
LOG2E = math.log2(math.e)
F32 = jnp.float32
BF16 = jnp.bfloat16
AXES = (("xh", 2), ("core", 2), ("z", 4), ("y", 4), ("xl", 2))
HEADS = ("xh", "core")
SEQ = ("z", "y", "xl")
XH, CORE, Z, Y, XL = range(5)
SWAP = [(0, 1), (1, 0)]
VMEM = 56 * 1024 * 1024
TOK = 256
PIECE = 256
GROUP = 4 * TOK
BLOCK = 1024
PLANES = 8


def dot(a, b, contract=((1,), (0,))):
    return lax.dot_general(a, b, (contract, ((), ())), preferred_element_type=F32)


def shifted(index, by, size=4):
    return lax.rem(index + by + size, size)


def head_block(step, pos):
    return lax.rem(pos[XH] + step // 2, 2) * 2 + lax.rem(pos[CORE] + step % 2, 2)


def struct(shape, dtype=BF16):
    return jax.ShapeDtypeStruct(shape, dtype)


def whole(shape):
    return pl.BlockSpec(shape, lambda *_: (0,) * len(shape))


def call(kernel, name, grid, in_specs, out_specs, out_shape, scratch, flops, moved, pos, *args):
    return pl.pallas_call(
        kernel,
        grid_spec=pltpu.PrefetchScalarGridSpec(
            num_scalar_prefetch=1,
            grid=grid,
            in_specs=in_specs,
            out_specs=out_specs,
            scratch_shapes=scratch,
        ),
        out_shape=out_shape,
        compiler_params=pltpu.CompilerParams(vmem_limit_bytes=VMEM),
        cost_estimate=pl.CostEstimate(flops=flops, bytes_accessed=moved, transcendentals=0),
        name=name,
    )(pos, *args)


HBM = pl.BlockSpec(memory_space=pltpu.HBM)


def moved_in(pairs, sems):
    copies = [pltpu.make_async_copy(source, target, sems.at[i]) for i, (source, target) in enumerate(pairs)]
    for copy in copies:
        copy.start()
    return copies


def weight_block(w_ref, step, pos, by_columns):
    part = pl.ds(pl.multiple_of(head_block(step, pos) * BLOCK, BLOCK), BLOCK)
    return w_ref.at[:, part] if by_columns else w_ref.at[part, :]


def project_kernel(first, pos, *refs):
    before, refs = (None, refs) if first == 0 else (refs[0], refs[1:])
    sources, (wq, wo, out, blocks, weights, known, block_sems, weight_sems, known_sems) = refs[:4], refs[4:]
    pairs = [
        (weight_block(w, first + i, pos, w is wo), weights.at[2 * n + i])
        for n, w in enumerate((wq, wo))
        for i in range(2)
    ]
    moves = moved_in([(x, blocks.at[i]) for i, x in enumerate(sources)], block_sems)
    weight_moves = moved_in(pairs, weight_sems)
    if before is not None:
        moves += moved_in([(before, known)], known_sems)
    for move in moves:
        move.wait()
    for n in range(2):
        contract = ((1,), (1,)) if n else ((1,), (0,))
        weight_moves[2 * n].wait()
        total = dot(blocks[2 * n], weights[2 * n], contract)
        if before is not None:
            total = total + known[n]
        weight_moves[2 * n + 1].wait()
        total = total + dot(blocks[2 * n + 1], weights[2 * n + 1], contract)
        if before is None:
            out[n] = total
        else:
            for layer in range(4):
                out[layer, n] = total[:, layer * PIECE : (layer + 1) * PIECE].astype(BF16)


def project(name, pos, blocks, query_weight, output_weight, before=None):
    shape, dtype = ((2, TOK, BLOCK), F32) if before is None else ((4, 2, TOK, PIECE), BF16)
    args = (*(() if before is None else (before,)), *blocks, query_weight, output_weight)
    return call(
        lambda *refs: project_kernel(0 if before is None else 2, *refs),
        name,
        (1,),
        [HBM] * len(args),
        whole(shape),
        struct(shape, dtype),
        [
            pltpu.VMEM((4, TOK, BLOCK), BF16),
            pltpu.VMEM((4, BLOCK, BLOCK), BF16),
            pltpu.VMEM((2, TOK, BLOCK), F32),
            pltpu.SemaphoreType.DMA((4,)),
            pltpu.SemaphoreType.DMA((4,)),
            pltpu.SemaphoreType.DMA((1,)),
        ],
        8 * TOK * BLOCK * BLOCK,
        8 * BLOCK * BLOCK,
        pos,
        *args,
    )


def assemble_kernel(pos, p0, p1, p2, p3, turned, straight):
    for i, piece in enumerate((p0, p1, p2, p3)):
        col = pl.multiple_of(head_block(i, pos) * PIECE, PIECE)
        for d in range(4):
            token = pl.multiple_of(shifted(pos[Y], -d) * TOK, TOK)
            turned[pl.ds(col, PIECE), pl.ds(token, TOK)] = piece[d, 0].T
            straight[pl.ds(token, TOK), pl.ds(col, PIECE)] = piece[d, 1]


def assemble(pos, pieces):
    return call(
        assemble_kernel,
        "column_blocks",
        (1,),
        [whole((4, 2, TOK, PIECE))] * 4,
        [whole((BLOCK, GROUP)), whole((GROUP, BLOCK))],
        [struct((BLOCK, GROUP)), struct((GROUP, BLOCK))],
        [],
        0,
        8 * BLOCK * GROUP,
        pos,
        *pieces,
    )


def attention_kernel(pos, bias, rows, k_ref, v_ref, out, dq_ref, dk_ref, dv_ref, dk_sum, dv_sum):
    k, v = k_ref[...], v_ref[...]
    for layer in range(4):
        q = rows[layer, 0]
        scores = dot(q, k, ((1,), (1,))) + bias[...]
        top = jnp.max(scores, axis=1, keepdims=True)
        weights = jnp.exp2((scores - top) * (SCALE * LOG2E))
        share = 1.0 / jnp.sum(weights, axis=1, keepdims=True)
        low = weights.astype(BF16)
        heads_out = (dot(low, v) * share).astype(BF16)
        token = slice(layer * TOK, (layer + 1) * TOK)
        out[0, :, token] = heads_out.T
        g = (rows[layer, 1].astype(F32) * (share * SCALE)).astype(BF16)
        delta = jnp.sum(g.astype(F32) * heads_out.astype(F32), axis=1, keepdims=True)
        score_grad = (low.astype(F32) * (dot(g, v, ((1,), (1,))) - delta)).astype(BF16)
        dq_ref[0, :, token] = dot(score_grad, k).astype(BF16).T
        dk_term, dv_term = dot(q, score_grad, ((0,), (0,))), dot(g, low, ((0,), (0,)))
        dk_sum[...] = dk_term if layer == 0 else dk_sum[...] + dk_term
        dv_sum[...] = dv_term if layer == 0 else dv_sum[...] + dv_term
    dk_ref[...] = dk_sum[...].T.astype(BF16)
    dv_ref[...] = (dv_sum[...] * (1.0 / SCALE)).T.astype(BF16)


def attention(pos, bias, rows, keys, values):
    column = pl.BlockSpec((GROUP, HEAD), lambda h, pos: (0, h))
    context = keys.shape[0]
    return call(
        attention_kernel,
        "attention",
        (PIECE // HEAD,),
        [whole((1, context)), pl.BlockSpec((4, 2, TOK, HEAD), lambda h, pos: (0, 0, 0, h))] + [column] * 2,
        [pl.BlockSpec((1, HEAD, GROUP), lambda h, pos: (0, h, 0))] * 2 + [column] * 2,
        [struct((1, PIECE, GROUP))] * 2 + [struct((GROUP, PIECE))] * 2,
        [pltpu.VMEM((HEAD, context), F32)] * 2,
        30 * GROUP * PIECE * context,
        16 * GROUP * PIECE,
        pos,
        bias,
        rows,
        keys,
        values,
    )


GATHERED = ((0, 0), (1, 0), (3, 0), (2, 0), (2, 1))


def output_grad_kernel(pos, *refs):
    left, right, out = refs[:5], refs[5], refs[6]
    for ref, (e, part) in zip(left, GATHERED):
        rows = ref.shape[1]
        row = pl.multiple_of(shifted(pos[Y], -e) * PIECE + part * rows, rows)
        product = dot(ref[0], right[...]).astype(BF16)
        for p in range(PLANES):
            out[p, pl.ds(row, rows), :] = product[:, p * 128 : (p + 1) * 128]


def query_grad_kernel(pos, *refs):
    right, left, out = refs[:5], refs[5], refs[6]
    for ref, (e, part) in zip(right, GATHERED):
        cols = ref.shape[1]
        col = pl.multiple_of(shifted(pos[Y], -e) * PIECE + part * cols, cols)
        out[:, pl.ds(col, cols)] = dot(left[...], ref[0], ((1,), (1,))).astype(BF16)


def weight_terms(name, kernel, pos, gathered, block, out):
    return call(
        kernel,
        name,
        (1,),
        [whole(a.shape) for a in gathered] + [whole(block.shape)],
        whole(out),
        struct(out),
        [],
        2 * GROUP * BLOCK * BLOCK,
        6 * BLOCK * BLOCK,
        pos,
        *gathered,
        block,
    )


def output_kernel(pos, *refs):
    rows, w_ref, give, keep, weights, sems = refs[:5], *refs[5:]
    order = (1, 3, 0, 2)
    moves = moved_in([(weight_block(w_ref, i, pos, True), weights.at[n]) for n, i in enumerate(order)], sems)
    for n in range(4):
        moves[n].wait()
        product = jnp.zeros((TOK, BLOCK), F32)
        for ref, (e, part) in zip(rows, GATHERED):
            size = ref.shape[1]
            row = pl.multiple_of(shifted(pos[Y], -e) * PIECE + part * size, size)
            product = product + dot(ref[0], weights[n, pl.ds(row, size), :], ((0,), (0,)))
        if n < 2:
            give[n] = product.astype(BF16)
        else:
            keep[n - 2] = product


def output_terms(pos, gathered, weight):
    return call(
        output_kernel,
        "output_terms",
        (1,),
        [pl.BlockSpec((1, a.shape[1], TOK), lambda n, pos: (0, 0, pos[Y])) for a in gathered] + [HBM],
        [whole((2, TOK, BLOCK))] * 2,
        [struct((2, TOK, BLOCK)), struct((2, TOK, BLOCK), F32)],
        [pltpu.VMEM((4, BLOCK, BLOCK), BF16), pltpu.SemaphoreType.DMA((4,))],
        2 * TOK * 4 * BLOCK * BLOCK,
        2 * 4 * BLOCK * BLOCK,
        pos,
        *gathered,
        weight,
    )


def context_bias(lengths, slot_passage):
    slot_lengths = jnp.sum(
        jnp.where(slot_passage[:, None] == jnp.arange(4)[None, :], lengths[None, :], 0), axis=1
    )
    position = jnp.arange(TOK, dtype=jnp.int32)
    valid = position[None, :] < slot_lengths[:, None]
    return jnp.where(valid, 0.0, -jnp.inf).astype(F32).reshape(1, 4 * TOK)


def on_device(
    decoder_states,
    query_weight,
    output_weight,
    context_keys,
    context_values,
    lengths,
    slot_passage,
    output_cotangent,
):
    pos = jnp.stack([lax.axis_index(name) for name, _ in AXES]).astype(jnp.int32)

    def shift(x, axis, d):
        return lax.ppermute(x, axis, [(i, (i + d) % 4) for i in range(4)])

    def swap(x, axis):
        return lax.ppermute(x, axis, SWAP)

    def after(x, *others):
        return lax.optimization_barrier((x, *others))[0]

    far_states, far_cotangent = swap(decoder_states, "xh"), swap(output_cotangent, "xh")
    near = (decoder_states, swap(decoder_states, "core"), output_cotangent, swap(output_cotangent, "core"))
    products = project("project_near", pos, near, query_weight, output_weight)

    both = jnp.stack([decoder_states, output_cotangent]).reshape(2, TOK, 4, PIECE)
    quarters = [lax.dynamic_index_in_dim(both, shifted(pos[Y], d), 2, False) for d in range(4)]
    quarters = [shift(x, "y", d) if d else x for d, x in enumerate(quarters)]

    own = jnp.stack([context_keys, context_values]).reshape(2, 8, 4, 4, PIECE).transpose(2, 3, 0, 1, 4)
    own = jnp.broadcast_to(own[:, None, :, None], (4, 4, 4, 2, 2, 8, PIECE)).reshape(128, 2, 8, PIECE)
    context = lax.all_to_all(after(own, products, far_states, far_cotangent, quarters), HEADS + SEQ, 0, 0, tiled=True)
    keys = context[:, 0].reshape(4 * TOK, PIECE)
    values = context[:, 1].reshape(4 * TOK, PIECE)
    bias = context_bias(lengths, slot_passage)

    far = (far_states, swap(far_states, "core"), far_cotangent, swap(far_cotangent, "core"))
    rows = project("project_far", pos, far, query_weight, output_weight, products)
    rows = lax.all_to_all(rows, "y", 0, 0, tiled=True)

    piece = jnp.stack(after(quarters, rows))
    over_x = swap(piece, "xh")

    heads_out, query_grad, key_terms, value_terms = attention(pos, bias, rows, keys, values)
    half = PIECE // 2

    def ring(x, *others):
        left, right = after((shift(x, "y", 1), shift(x, "y", 3)), *others)
        return x, left, right, shift(left[:, :half], "y", 1), shift(right[:, half:], "y", 3)

    every_out = ring(heads_out, over_x)

    piece, over_x = after((piece, over_x), *every_out[:3])
    group_states, group_cotangent = assemble(
        pos, (piece, swap(piece, "core"), over_x, swap(over_x, "core"))
    )

    def plane_sum(parts):
        return jnp.sum(lax.all_to_all(parts, ("z", "xl"), 0, 0, tiled=True).astype(F32), axis=0)

    output_parts = weight_terms(
        "output_weight_terms",
        output_grad_kernel,
        pos,
        every_out,
        group_cotangent,
        (PLANES, BLOCK, 128),
    )
    every_grad = ring(after(query_grad, every_out), output_parts)
    output_weight_grad = plane_sum(output_parts)

    give, keep = output_terms(pos, after(every_out, output_parts), output_weight)
    pair = keep + swap(give, "core").astype(F32)
    pair_far = pair[1].astype(BF16)
    attended = (pair[0] + swap(pair_far, "xh").astype(F32)).astype(BF16)

    query_parts = weight_terms(
        "query_weight_terms",
        query_grad_kernel,
        pos,
        after(every_grad, output_parts),
        group_states,
        (BLOCK, BLOCK),
    )

    terms = jnp.stack([key_terms.reshape(128, 8, PIECE), value_terms.reshape(128, 8, PIECE)], 1)
    moved = lax.all_to_all(after(terms, output_weight_grad, pair_far), HEADS + SEQ, 0, 0, tiled=True)
    owned = jnp.sum(moved.reshape(4, 4, 4, 2, 2, 8, PIECE).astype(F32), axis=(1, 3))
    owned = owned.transpose(2, 3, 0, 1, 4).reshape(2, 8, 16 * PIECE)

    query_parts = after(query_parts, moved, attended)
    query_weight_grad = plane_sum(query_parts.reshape(PLANES, 128, BLOCK))
    return attended, query_weight_grad, output_weight_grad, owned[0], owned[1]


def solution(mesh):
    devices = mesh.devices.reshape([size for _, size in AXES])
    split = Mesh(devices, [name for name, _ in AXES])
    return jax.shard_map(
        on_device,
        mesh=split,
        in_specs=(
            P(SEQ, HEADS),
            P(None, HEADS),
            P(HEADS, None),
            P(HEADS + SEQ, None),
            P(HEADS + SEQ, None),
            P(),
            P(),
            P(SEQ, HEADS),
        ),
        out_specs=(
            P(SEQ, HEADS),
            P(SEQ, HEADS),
            P(HEADS, SEQ),
            P(HEADS + SEQ, None),
            P(HEADS + SEQ, None),
        ),
        check_vma=False,
    )
```

```python
import math

import jax
import jax.numpy as jnp
from jax import lax
from jax.experimental import pallas as pl
from jax.experimental.pallas import tpu as pltpu
from jax.sharding import Mesh
from jax.sharding import PartitionSpec as P

HEAD = 128
SCALE = 1.0 / math.sqrt(HEAD)
LOG2E = math.log2(math.e)
F32 = jnp.float32
BF16 = jnp.bfloat16
AXES = (("xh", 2), ("core", 2), ("z", 4), ("y", 4), ("xl", 2))
HEADS = ("xh", "core")
SEQ = ("z", "y", "xl")
XH, CORE, Z, Y, XL = range(5)
SWAP = [(0, 1), (1, 0)]
VMEM = 56 * 1024 * 1024
TOK = 256
PIECE = 256
GROUP = 4 * TOK
BLOCK = 1024
PLANES = 8


def dot(a, b, contract=((1,), (0,))):
    return lax.dot_general(a, b, (contract, ((), ())), preferred_element_type=F32)


def shifted(index, by, size=4):
    return lax.rem(index + by + size, size)


def head_block(step, pos):
    return lax.rem(pos[XH] + step // 2, 2) * 2 + lax.rem(pos[CORE] + step % 2, 2)


def struct(shape, dtype=BF16):
    return jax.ShapeDtypeStruct(shape, dtype)


def whole(shape):
    return pl.BlockSpec(shape, lambda *_: (0,) * len(shape))


def call(kernel, name, grid, in_specs, out_specs, out_shape, scratch, flops, moved, pos, *args):
    return pl.pallas_call(
        kernel,
        grid_spec=pltpu.PrefetchScalarGridSpec(
            num_scalar_prefetch=1,
            grid=grid,
            in_specs=in_specs,
            out_specs=out_specs,
            scratch_shapes=scratch,
        ),
        out_shape=out_shape,
        compiler_params=pltpu.CompilerParams(vmem_limit_bytes=VMEM),
        cost_estimate=pl.CostEstimate(flops=flops, bytes_accessed=moved, transcendentals=0),
        name=name,
    )(pos, *args)


HBM = pl.BlockSpec(memory_space=pltpu.HBM)


def moved_in(pairs, sems):
    copies = [pltpu.make_async_copy(source, target, sems.at[i]) for i, (source, target) in enumerate(pairs)]
    for copy in copies:
        copy.start()
    return copies


def weight_block(w_ref, step, pos, by_columns):
    part = pl.ds(pl.multiple_of(head_block(step, pos) * BLOCK, BLOCK), BLOCK)
    return w_ref.at[:, part] if by_columns else w_ref.at[part, :]


def project_kernel(first, pos, *refs):
    before, refs = (None, refs) if first == 0 else (refs[0], refs[1:])
    sources, (wq, wo, out, blocks, weights, known, block_sems, weight_sems, known_sems) = refs[:4], refs[4:]
    pairs = [
        (weight_block(w, first + i, pos, w is wo), weights.at[2 * n + i])
        for n, w in enumerate((wq, wo))
        for i in range(2)
    ]
    moves = moved_in([(x, blocks.at[i]) for i, x in enumerate(sources)], block_sems)
    weight_moves = moved_in(pairs, weight_sems)
    if before is not None:
        moves += moved_in([(before, known)], known_sems)
    for move in moves:
        move.wait()
    for n in range(2):
        contract = ((1,), (1,)) if n else ((1,), (0,))
        weight_moves[2 * n].wait()
        total = dot(blocks[2 * n], weights[2 * n], contract)
        if before is not None:
            total = total + known[n]
        weight_moves[2 * n + 1].wait()
        total = total + dot(blocks[2 * n + 1], weights[2 * n + 1], contract)
        if before is None:
            out[n] = total
        else:
            for layer in range(4):
                out[layer, n] = total[:, layer * PIECE : (layer + 1) * PIECE].astype(BF16)


def project(name, pos, blocks, query_weight, output_weight, before=None):
    shape, dtype = ((2, TOK, BLOCK), F32) if before is None else ((4, 2, TOK, PIECE), BF16)
    args = (*(() if before is None else (before,)), *blocks, query_weight, output_weight)
    return call(
        lambda *refs: project_kernel(0 if before is None else 2, *refs),
        name,
        (1,),
        [HBM] * len(args),
        whole(shape),
        struct(shape, dtype),
        [
            pltpu.VMEM((4, TOK, BLOCK), BF16),
            pltpu.VMEM((4, BLOCK, BLOCK), BF16),
            pltpu.VMEM((2, TOK, BLOCK), F32),
            pltpu.SemaphoreType.DMA((4,)),
            pltpu.SemaphoreType.DMA((4,)),
            pltpu.SemaphoreType.DMA((1,)),
        ],
        8 * TOK * BLOCK * BLOCK,
        8 * BLOCK * BLOCK,
        pos,
        *args,
    )


def assemble_kernel(pos, p0, p1, p2, p3, turned, straight):
    for i, piece in enumerate((p0, p1, p2, p3)):
        col = pl.multiple_of(head_block(i, pos) * PIECE, PIECE)
        for d in range(4):
            token = pl.multiple_of(shifted(pos[Y], -d) * TOK, TOK)
            turned[pl.ds(col, PIECE), pl.ds(token, TOK)] = piece[d, 0].T
            straight[pl.ds(token, TOK), pl.ds(col, PIECE)] = piece[d, 1]


def assemble(pos, pieces):
    return call(
        assemble_kernel,
        "column_blocks",
        (1,),
        [whole((4, 2, TOK, PIECE))] * 4,
        [whole((BLOCK, GROUP)), whole((GROUP, BLOCK))],
        [struct((BLOCK, GROUP)), struct((GROUP, BLOCK))],
        [],
        0,
        8 * BLOCK * GROUP,
        pos,
        *pieces,
    )


def attention_kernel(pos, bias, rows, k_ref, v_ref, out, dq_ref, dk_ref, dv_ref, dk_sum, dv_sum):
    k, v = k_ref[...], v_ref[...]
    for layer in range(4):
        q = rows[layer, 0]
        scores = dot(q, k, ((1,), (1,))) + bias[...]
        top = jnp.max(scores, axis=1, keepdims=True)
        weights = jnp.exp2((scores - top) * (SCALE * LOG2E))
        share = 1.0 / jnp.sum(weights, axis=1, keepdims=True)
        low = weights.astype(BF16)
        heads_out = (dot(low, v) * share).astype(BF16)
        token = slice(layer * TOK, (layer + 1) * TOK)
        out[0, :, token] = heads_out.T
        g = (rows[layer, 1].astype(F32) * (share * SCALE)).astype(BF16)
        delta = jnp.sum(g.astype(F32) * heads_out.astype(F32), axis=1, keepdims=True)
        score_grad = (low.astype(F32) * (dot(g, v, ((1,), (1,))) - delta)).astype(BF16)
        dq_ref[0, :, token] = dot(score_grad, k).astype(BF16).T
        dk_term, dv_term = dot(q, score_grad, ((0,), (0,))), dot(g, low, ((0,), (0,)))
        dk_sum[...] = dk_term if layer == 0 else dk_sum[...] + dk_term
        dv_sum[...] = dv_term if layer == 0 else dv_sum[...] + dv_term
    dk_ref[...] = dk_sum[...].T.astype(BF16)
    dv_ref[...] = (dv_sum[...] * (1.0 / SCALE)).T.astype(BF16)


def attention(pos, bias, rows, keys, values):
    column = pl.BlockSpec((GROUP, HEAD), lambda h, pos: (0, h))
    context = keys.shape[0]
    return call(
        attention_kernel,
        "attention",
        (PIECE // HEAD,),
        [whole((1, context)), pl.BlockSpec((4, 2, TOK, HEAD), lambda h, pos: (0, 0, 0, h))] + [column] * 2,
        [pl.BlockSpec((1, HEAD, GROUP), lambda h, pos: (0, h, 0))] * 2 + [column] * 2,
        [struct((1, PIECE, GROUP))] * 2 + [struct((GROUP, PIECE))] * 2,
        [pltpu.VMEM((HEAD, context), F32)] * 2,
        30 * GROUP * PIECE * context,
        16 * GROUP * PIECE,
        pos,
        bias,
        rows,
        keys,
        values,
    )


GATHERED = ((0, 0), (1, 0), (3, 0), (2, 0), (2, 1))


def output_grad_kernel(pos, *refs):
    left, right, out = refs[:5], refs[5], refs[6]
    for ref, (e, part) in zip(left, GATHERED):
        rows = ref.shape[1]
        row = pl.multiple_of(shifted(pos[Y], -e) * PIECE + part * rows, rows)
        product = dot(ref[0], right[...]).astype(BF16)
        for p in range(PLANES):
            out[p, pl.ds(row, rows), :] = product[:, p * 128 : (p + 1) * 128]


def query_grad_kernel(pos, *refs):
    right, left, out = refs[:5], refs[5], refs[6]
    for ref, (e, part) in zip(right, GATHERED):
        cols = ref.shape[1]
        col = pl.multiple_of(shifted(pos[Y], -e) * PIECE + part * cols, cols)
        out[:, pl.ds(col, cols)] = dot(left[...], ref[0], ((1,), (1,))).astype(BF16)


def weight_terms(name, kernel, pos, gathered, block, out):
    return call(
        kernel,
        name,
        (1,),
        [whole(a.shape) for a in gathered] + [whole(block.shape)],
        whole(out),
        struct(out),
        [],
        2 * GROUP * BLOCK * BLOCK,
        6 * BLOCK * BLOCK,
        pos,
        *gathered,
        block,
    )


def output_kernel(pos, *refs):
    rows, w_ref, give, keep, weights, sems = refs[:5], *refs[5:]
    order = (1, 3, 0, 2)
    moves = moved_in([(weight_block(w_ref, i, pos, True), weights.at[n]) for n, i in enumerate(order)], sems)
    for n in range(4):
        moves[n].wait()
        product = jnp.zeros((TOK, BLOCK), F32)
        for ref, (e, part) in zip(rows, GATHERED):
            size = ref.shape[1]
            row = pl.multiple_of(shifted(pos[Y], -e) * PIECE + part * size, size)
            product = product + dot(ref[0], weights[n, pl.ds(row, size), :], ((0,), (0,)))
        if n < 2:
            give[n] = product.astype(BF16)
        else:
            keep[n - 2] = product


def output_terms(pos, gathered, weight):
    return call(
        output_kernel,
        "output_terms",
        (1,),
        [pl.BlockSpec((1, a.shape[1], TOK), lambda n, pos: (0, 0, pos[Y])) for a in gathered] + [HBM],
        [whole((2, TOK, BLOCK))] * 2,
        [struct((2, TOK, BLOCK)), struct((2, TOK, BLOCK), F32)],
        [pltpu.VMEM((4, BLOCK, BLOCK), BF16), pltpu.SemaphoreType.DMA((4,))],
        2 * TOK * 4 * BLOCK * BLOCK,
        2 * 4 * BLOCK * BLOCK,
        pos,
        *gathered,
        weight,
    )


def context_bias(lengths, slot_passage):
    slot_lengths = jnp.sum(
        jnp.where(slot_passage[:, None] == jnp.arange(4)[None, :], lengths[None, :], 0), axis=1
    )
    position = jnp.arange(TOK, dtype=jnp.int32)
    valid = position[None, :] < slot_lengths[:, None]
    return jnp.where(valid, 0.0, -jnp.inf).astype(F32).reshape(1, 4 * TOK)


def on_device(
    decoder_states,
    query_weight,
    output_weight,
    context_keys,
    context_values,
    lengths,
    slot_passage,
    output_cotangent,
):
    pos = jnp.stack([lax.axis_index(name) for name, _ in AXES]).astype(jnp.int32)

    def shift(x, axis, d):
        return lax.ppermute(x, axis, [(i, (i + d) % 4) for i in range(4)])

    def swap(x, axis):
        return lax.ppermute(x, axis, SWAP)

    def after(x, *others):
        return lax.optimization_barrier((x, *others))[0]

    far_states, far_cotangent = swap(decoder_states, "xh"), swap(output_cotangent, "xh")
    near = (decoder_states, swap(decoder_states, "core"), output_cotangent, swap(output_cotangent, "core"))
    products = project("project_near", pos, near, query_weight, output_weight)

    both = jnp.stack([decoder_states, output_cotangent]).reshape(2, TOK, 4, PIECE)
    quarters = [lax.dynamic_index_in_dim(both, shifted(pos[Y], d), 2, False) for d in range(4)]
    quarters = [shift(x, "y", d) if d else x for d, x in enumerate(quarters)]

    own = jnp.stack([context_keys, context_values]).reshape(2, 8, 4, 4, PIECE).transpose(2, 3, 0, 1, 4)
    own = jnp.broadcast_to(own[:, None, :, None], (4, 4, 4, 2, 2, 8, PIECE)).reshape(128, 2, 8, PIECE)
    context = lax.all_to_all(after(own, products, far_states, far_cotangent, quarters), HEADS + SEQ, 0, 0, tiled=True)
    keys = context[:, 0].reshape(4 * TOK, PIECE)
    values = context[:, 1].reshape(4 * TOK, PIECE)
    bias = context_bias(lengths, slot_passage)

    far = (far_states, swap(far_states, "core"), far_cotangent, swap(far_cotangent, "core"))
    rows = project("project_far", pos, far, query_weight, output_weight, products)
    rows = lax.all_to_all(rows, "y", 0, 0, tiled=True)

    piece = jnp.stack(after(quarters, rows))
    over_x = swap(piece, "xh")

    heads_out, query_grad, key_terms, value_terms = attention(pos, bias, rows, keys, values)
    half = PIECE // 2

    def ring(x, *others):
        left, right = after((shift(x, "y", 1), shift(x, "y", 3)), *others)
        return x, left, right, shift(left[:, :half], "y", 1), shift(right[:, half:], "y", 3)

    every_out = ring(heads_out, over_x)

    piece, over_x = after((piece, over_x), *every_out[:3])
    group_states, group_cotangent = assemble(
        pos, (piece, swap(piece, "core"), over_x, swap(over_x, "core"))
    )

    def plane_sum(parts):
        return jnp.sum(lax.all_to_all(parts, ("z", "xl"), 0, 0, tiled=True).astype(F32), axis=0)

    output_parts = weight_terms(
        "output_weight_terms",
        output_grad_kernel,
        pos,
        every_out,
        group_cotangent,
        (PLANES, BLOCK, 128),
    )
    every_grad = ring(after(query_grad, every_out), output_parts)
    output_weight_grad = plane_sum(output_parts)

    give, keep = output_terms(pos, after(every_out, output_parts, *every_grad[:3]), output_weight)
    pair = keep + swap(give, "core").astype(F32)
    pair_far = pair[1].astype(BF16)
    attended = (pair[0] + swap(pair_far, "xh").astype(F32)).astype(BF16)

    query_parts = weight_terms(
        "query_weight_terms",
        query_grad_kernel,
        pos,
        after(every_grad, output_parts),
        group_states,
        (BLOCK, BLOCK),
    )

    terms = jnp.stack([key_terms.reshape(128, 8, PIECE), value_terms.reshape(128, 8, PIECE)], 1)
    moved = lax.all_to_all(after(terms, output_weight_grad, pair_far), HEADS + SEQ, 0, 0, tiled=True)
    owned = jnp.sum(moved.reshape(4, 4, 4, 2, 2, 8, PIECE).astype(F32), axis=(1, 3))
    owned = owned.transpose(2, 3, 0, 1, 4).reshape(2, 8, 16 * PIECE)

    query_parts = after(query_parts, moved, attended)
    query_weight_grad = plane_sum(query_parts.reshape(PLANES, 128, BLOCK))
    return attended, query_weight_grad, output_weight_grad, owned[0], owned[1]


def solution(mesh):
    devices = mesh.devices.reshape([size for _, size in AXES])
    split = Mesh(devices, [name for name, _ in AXES])
    return jax.shard_map(
        on_device,
        mesh=split,
        in_specs=(
            P(SEQ, HEADS),
            P(None, HEADS),
            P(HEADS, None),
            P(HEADS + SEQ, None),
            P(HEADS + SEQ, None),
            P(),
            P(),
            P(SEQ, HEADS),
        ),
        out_specs=(
            P(SEQ, HEADS),
            P(SEQ, HEADS),
            P(HEADS, SEQ),
            P(HEADS + SEQ, None),
            P(HEADS + SEQ, None),
        ),
        check_vma=False,
    )
```
